128 devices in a mesh: dp: 32 (over y_lo, z, x), mp: 4 (over y_hi, core).
Axes of the slice: x: 4, y: 4 (y_hi: 2, y_lo: 2; y = y_hi * 2 + y_lo), z: 4, core: 2. Of those that a mesh axis runs over, the one named last changes fastest.
Arguments:
- frames: bfloat16 [1536, 81, 512], P(('dp', 'mp')), may hold values from -6 to 6
- camera_ids: int32 [1536], P(('dp', 'mp')), may hold values from 0 to 1
- instruction_ids: int32 [256], P('dp'), may hold values from 0 to 743
- action_bins: int32 [1536, 11], P('dp'), may hold values from 0 to 255
- final_mask: int32 [1536], P('dp'), may hold values 0 or 1
- step_count: int32 [1], replicated, may hold values from 2 to 20
- conv_w: float32 [1033, 3072], P(None, ('dp', 'mp')), may hold values from -0.75 to 0.75
- conv_m1: float32 [1033, 3072], P(None, ('dp', 'mp')), may hold values from -4.7683716e-06 to 4.7683716e-06
- conv_m2: float32 [1033, 3072], P(None, ('dp', 'mp')), may hold values from 2.3060689e-14 to 1.8448551e-13
- cond_w: float32 [1770, 512], P(None, ('dp', 'mp')), may hold values from -0.75 to 0.75
- cond_m1: float32 [1770, 512], P(None, ('dp', 'mp')), may hold values from -4.7683716e-06 to 4.7683716e-06
- cond_m2: float32 [1770, 512], P(None, ('dp', 'mp')), may hold values from 2.3060689e-14 to 1.8448551e-13
- small_w: float32 [11, 512], P(None, ('dp', 'mp')), may hold values from -4 to 4
- small_m1: float32 [11, 512], P(None, ('dp', 'mp')), may hold values from -4.7683716e-06 to 4.7683716e-06
- small_m2: float32 [11, 512], P(None, ('dp', 'mp')), may hold values from 2.3060689e-14 to 1.8448551e-13
- attn_w: float32 [4, 512, 512], P(None, 'dp', 'mp'), may hold values from -0.25 to 0.25
- attn_m1: float32 [4, 512, 512], P(None, 'dp', 'mp'), may hold values from -4.7683716e-06 to 4.7683716e-06
- attn_m2: float32 [4, 512, 512], P(None, 'dp', 'mp'), may hold values from 2.3060689e-14 to 1.8448551e-13
- mlp_w: float32 [2, 512, 2048], P(None, 'dp', 'mp'), may hold values from -0.25 to 0.25
- mlp_m1: float32 [2, 512, 2048], P(None, 'dp', 'mp'), may hold values from -4.7683716e-06 to 4.7683716e-06
- mlp_m2: float32 [2, 512, 2048], P(None, 'dp', 'mp'), may hold values from 2.3060689e-14 to 1.8448551e-13
- head_w: float32 [512, 11, 256], P('dp', None, 'mp'), may hold values from -1 to 1
- head_m1: float32 [512, 11, 256], P('dp', None, 'mp'), may hold values from -4.7683716e-06 to 4.7683716e-06
- head_m2: float32 [512, 11, 256], P('dp', None, 'mp'), may hold values from 2.3060689e-14 to 1.8448551e-13
Outputs:
- loss: float32 [], replicated
- grad_norm: float32 [], replicated
- conv_new: float32 [1033, 3072], P(None, ('dp', 'mp'))
- conv_first: float32 [1033, 3072], P(None, ('dp', 'mp'))
- conv_second: float32 [1033, 3072], P(None, ('dp', 'mp'))
- cond_new: float32 [1770, 512], P(None, ('dp', 'mp'))
- cond_first: float32 [1770, 512], P(None, ('dp', 'mp'))
- cond_second: float32 [1770, 512], P(None, ('dp', 'mp'))
- small_new: float32 [11, 512], P(None, ('dp', 'mp'))
- small_first: float32 [11, 512], P(None, ('dp', 'mp'))
- small_second: float32 [11, 512], P(None, ('dp', 'mp'))
- attn_new: float32 [4, 512, 512], P(None, 'dp', 'mp')
- attn_first: float32 [4, 512, 512], P(None, 'dp', 'mp')
- attn_second: float32 [4, 512, 512], P(None, 'dp', 'mp')
- mlp_new: float32 [2, 512, 2048], P(None, 'dp', 'mp')
- mlp_first: float32 [2, 512, 2048], P(None, 'dp', 'mp')
- mlp_second: float32 [2, 512, 2048], P(None, 'dp', 'mp')
- head_new: float32 [512, 11, 256], P('dp', None, 'mp')
- head_first: float32 [512, 11, 256], P('dp', None, 'mp')
- head_second: float32 [512, 11, 256], P('dp', None, 'mp')
The draws below stay inside these ranges and needn't reach their ends.
All inputs are finite; a program needn't handle non-finite values. No bound on the sum of `final_mask` on one device may be relied on, other than what follows from the above.
Results may differ from the reference program's by a relative error of at most 0.0091.
The reference program's roundings to bfloat16 on the way count: a program that leaves them out, or rounds other values in their place, can miss the bound.
Values may be sent and summed in bfloat16 or wider, within the bound.
A program may use at most 576 MiB of HBM per device.

```python
import math
import jax
import jax.numpy as jnp
from jax import lax

D = 512
EXP = 3072
H = 8
HD = 64
FF = 2048
INSTR = 744
DIMS = 11
BINS = 256
NTOK = 8
FRAMES = 6
MAP = 9
PIX = 81
EXAMPLES = 256
IMAGES = 1536
PARAMS = 8672768
N_DP = 32


def touch_ends(entries, own_key, smallest, high):
    shape = entries.shape
    index_at = [jax.random.randint(jax.random.fold_in(own_key, axis), (), 0, shape[axis]) for axis in range(len(shape))]
    entries = entries.at[tuple(index_at)].set(smallest)
    longest = shape.index(max(shape))
    index_at[longest] = (index_at[longest] + 1) % shape[longest]
    return entries.at[tuple(index_at)].set(high)


def steps_of(own_key, dims, pieces, low, largest):
    level, own = 1.0, jax.random.fold_in(own_key, 6)
    for dim, blocks in pieces:
        steps = jnp.exp(jax.random.uniform(jax.random.fold_in(own, dim), (blocks,), jnp.float32, low / len(pieces), largest / len(pieces)))
        level = level * jnp.repeat(steps, dims[dim] // blocks).reshape([-1 if axis == dim else 1 for axis in range(len(dims))])
    return level


def noise(stream_key, dims, scale, most, shards=(), kind=jnp.bfloat16):
    entries = jax.random.normal(stream_key, dims, jnp.float32) * scale
    if len(shards) > 0:
        entries = steps_of(stream_key, dims, shards, -0.22, 0.18) * entries
    return jnp.clip(entries, min=-most, max=most).astype(kind)


def setup_inputs(seed: int = 0) -> dict:
    arg_keys = jax.random.split(jax.random.key(seed), 25)
    return {
        "frames": noise(arg_keys[0], (IMAGES, PIX, D), 1.0, 6.0, ((0, 128),)),
        "camera_ids": touch_ends(jax.random.randint(arg_keys[1], (IMAGES,), 0, 2), jax.random.fold_in(arg_keys[1], 1), 0, 1).astype(jnp.int32),
        "instruction_ids": touch_ends(jax.random.randint(arg_keys[2], (EXAMPLES,), 0, INSTR), jax.random.fold_in(arg_keys[2], 1), 0, INSTR - 1).astype(jnp.int32),
        "action_bins": touch_ends(jax.random.randint(arg_keys[3], (IMAGES, DIMS), 0, BINS), jax.random.fold_in(arg_keys[3], 1), 0, BINS - 1).astype(jnp.int32),
        "final_mask": touch_ends((jax.random.randint(arg_keys[4], (IMAGES,), 0, 2) < 1).astype(jnp.int32), jax.random.fold_in(arg_keys[4], 1), 0, 1),
        "step_count": jax.random.randint(arg_keys[5], (1,), 2, 21).astype(jnp.int32),
        "conv_w": noise(arg_keys[6], (2 * D + 9, EXP), 64 ** -0.5, 0.75, ((1, 128),), jnp.float32),
        "conv_m1": noise(arg_keys[7], (2 * D + 9, EXP), (0.0022 * PARAMS ** -0.5), 4.76837158203125e-06, ((1, 128),), jnp.float32),
        "conv_m2": jnp.clip(jnp.exp(math.log(1.844855106354626e-13) - 2.0794415 * jax.random.uniform(arg_keys[8], (2 * D + 9, EXP), jnp.float32) ** steps_of(arg_keys[8], (2 * D + 9, EXP), ((1, 128),), -0.2, 0.2)), 2.3060688829432824e-14, 1.844855106354626e-13),
        "cond_w": noise(arg_keys[9], (2 * D + INSTR + 2, D), 64 ** -0.5, 0.75, ((1, 128),), jnp.float32),
        "cond_m1": noise(arg_keys[10], (2 * D + INSTR + 2, D), (0.0022 * PARAMS ** -0.5), 4.76837158203125e-06, ((1, 128),), jnp.float32),
        "cond_m2": jnp.clip(jnp.exp(math.log(1.844855106354626e-13) - 2.0794415 * jax.random.uniform(arg_keys[11], (2 * D + INSTR + 2, D), jnp.float32) ** steps_of(arg_keys[11], (2 * D + INSTR + 2, D), ((1, 128),), -0.2, 0.2)), 2.3060688829432824e-14, 1.844855106354626e-13),
        "small_w": noise(arg_keys[12], (NTOK + 3, D), 0.25, 4.0, ((1, 128),), jnp.float32),
        "small_m1": noise(arg_keys[13], (NTOK + 3, D), (0.0022 * PARAMS ** -0.5), 4.76837158203125e-06, ((1, 128),), jnp.float32),
        "small_m2": jnp.clip(jnp.exp(math.log(1.844855106354626e-13) - 2.0794415 * jax.random.uniform(arg_keys[14], (NTOK + 3, D), jnp.float32) ** steps_of(arg_keys[14], (NTOK + 3, D), ((1, 128),), -0.2, 0.2)), 2.3060688829432824e-14, 1.844855106354626e-13),
        "attn_w": noise(arg_keys[15], (4, D, D), D ** -0.5, 0.25, ((1, 32), (2, 4)), jnp.float32),
        "attn_m1": noise(arg_keys[16], (4, D, D), (0.0022 * PARAMS ** -0.5), 4.76837158203125e-06, ((1, 32), (2, 4)), jnp.float32),
        "attn_m2": jnp.clip(jnp.exp(math.log(1.844855106354626e-13) - 2.0794415 * jax.random.uniform(arg_keys[17], (4, D, D), jnp.float32) ** steps_of(arg_keys[17], (4, D, D), ((1, 32), (2, 4)), -0.2, 0.2)), 2.3060688829432824e-14, 1.844855106354626e-13),
        "mlp_w": noise(arg_keys[18], (2, D, FF), D ** -0.5, 0.25, ((1, 32), (2, 4)), jnp.float32),
        "mlp_m1": noise(arg_keys[19], (2, D, FF), (0.0022 * PARAMS ** -0.5), 4.76837158203125e-06, ((1, 32), (2, 4)), jnp.float32),
        "mlp_m2": jnp.clip(jnp.exp(math.log(1.844855106354626e-13) - 2.0794415 * jax.random.uniform(arg_keys[20], (2, D, FF), jnp.float32) ** steps_of(arg_keys[20], (2, D, FF), ((1, 32), (2, 4)), -0.2, 0.2)), 2.3060688829432824e-14, 1.844855106354626e-13),
        "head_w": noise(arg_keys[21], (D, DIMS, BINS), (D // 16) ** -0.5, 1.0, ((0, 32), (2, 4)), jnp.float32),
        "head_m1": noise(arg_keys[22], (D, DIMS, BINS), (0.0022 * PARAMS ** -0.5), 4.76837158203125e-06, ((0, 32), (2, 4)), jnp.float32),
        "head_m2": jnp.clip(jnp.exp(math.log(1.844855106354626e-13) - 2.0794415 * jax.random.uniform(arg_keys[23], (D, DIMS, BINS), jnp.float32) ** steps_of(arg_keys[23], (D, DIMS, BINS), ((0, 32), (2, 4)), -0.2, 0.2)), 2.3060688829432824e-14, 1.844855106354626e-13),
    }


@jax.custom_vjp
def low(v):
    return lax.optimization_barrier(v.astype(jnp.bfloat16)).astype(jnp.float32)

@jax.custom_vjp
def low_back(v):
    return v

def low_keep(v):
    return (low(v), None)

def low_pass(kept, grad):
    return (grad,)

def back_keep(v):
    return (v, None)

def back_low(kept, grad):
    return (low(grad),)
low.defvjp(low_keep, low_pass)
low_back.defvjp(back_keep, back_low)
HIGH = lax.Precision.HIGHEST
LN_EPS = 1e-06
CLIP_NORM = 0.02
BETA_ONE = 0.9
BETA_TWO = 0.999
ADAM_EPS = 1e-08
DECAY = 0.01
RATES = (0.1, 0.1, 0.2, 0.05, 0.05, 0.2)

def matmul(a, b):
    return jnp.dot(a, b, precision=HIGH, preferred_element_type=jnp.float32)

def layer_norm(x, gain):
    centre = x - lax.optimization_barrier(jnp.mean(x, -1, keepdims=True))
    return centre * lax.rsqrt(lax.optimization_barrier(jnp.mean(centre * centre, -1, keepdims=True)) + LN_EPS) * (1.0 + gain)

def depthwise(act, kernel):
    padded = jnp.pad(act, ((0, 0), (1, 1), (1, 1), (0, 0)))
    total = jnp.zeros_like(act)
    for offset in range(9):
        row, col = (offset // 3, offset % 3)
        total = total + padded[:, row:row + MAP, col:col + MAP, :] * kernel[offset]
    return total

def block_loss(weights, block):
    conv, cond, small, attn, mlp, head = weights
    frames, camera, instr, labels, mask = block
    images = frames.shape[0]
    flat = frames.astype(jnp.float32).reshape(images * PIX, D)
    pre = low_back(matmul(flat, conv[:D]) * (8.0 / math.sqrt(D)))
    act = jax.nn.silu(pre).reshape(images, MAP, MAP, EXP)
    mid = low(jax.nn.silu(depthwise(act, conv[2 * D:] * (8.0 / 3.0))).reshape(images * PIX, EXP))
    proj = low_back(matmul(mid, conv[D:2 * D].T) * (8.0 / math.sqrt(EXP)))
    table = cond[2 * D:]
    instr_img = jnp.repeat(instr, FRAMES)
    cvec = low(table[instr_img] + table[INSTR + camera])
    film = low_back(matmul(cvec, cond[:2 * D].T) * (16.0 / math.sqrt(D)))
    gamma = film[:, None, :D]
    beta = film[:, None, D:]
    feature = flat.reshape(images, PIX, D) + proj.reshape(images, PIX, D) * (1.0 + gamma) + beta
    gains = small[:3]
    learner = small[3:]
    logit = jnp.einsum('kpd,td->kpt', feature, learner, precision=HIGH) * (4.0 / math.sqrt(D))
    weight = jax.nn.softmax(logit, axis=1)
    tok = low(jnp.einsum('kpt,kpd->ktd', weight, feature, precision=HIGH).reshape(images * NTOK, D))
    rows = tok.shape[0]
    seq = FRAMES * NTOK
    count_ex = rows // seq
    h1 = low(layer_norm(tok, gains[0]))

    def heads(w):
        return low(low_back(matmul(h1, w))).reshape(count_ex, seq, H, HD)
    q = heads(attn[0])
    k = heads(attn[1])
    v = heads(attn[2])
    scores = low_back(jnp.einsum('bqhd,bkhd->bhqk', q, k, precision=HIGH) * HD ** (-0.5))
    causal = jnp.tril(jnp.ones((seq, seq), bool))
    prob = low(jax.nn.softmax(jnp.where(causal, scores, -1e+30), axis=-1))
    ctx = low(low_back(jnp.einsum('bhqk,bkhd->bqhd', prob, v, precision=HIGH))).reshape(rows, D)
    x1 = tok + low_back(2.0 * matmul(ctx, attn[3].T))
    h2 = low(layer_norm(x1, gains[1]))
    up = low_back(matmul(h2, mlp[0]))
    hidden = low(jax.nn.gelu(up, approximate=True))
    x2 = x1 + low_back(matmul(hidden, mlp[1].T))
    normed = layer_norm(x2, gains[2])
    pooled = low(lax.optimization_barrier(jnp.mean(normed.reshape(images, NTOK, D), axis=1)))
    logits = low_back(matmul(pooled, head.reshape(D, DIMS * BINS))).reshape(images, DIMS, BINS)
    lse = jax.nn.logsumexp(logits, axis=-1)
    target = jnp.take_along_axis(logits, labels[..., None], axis=-1)[..., 0]
    return jnp.sum(mask.astype(jnp.float32)[:, None] * (lse - target))

def adam(master, first, second, grad, t, rate):
    first_new = BETA_ONE * first + (1.0 - BETA_ONE) * grad
    second_new = BETA_TWO * second + (1.0 - BETA_TWO) * grad * grad
    m_hat = first_new / (1.0 - BETA_ONE ** t)
    v_hat = second_new / (1.0 - BETA_TWO ** t)
    master_new = master - rate * (m_hat / (jnp.sqrt(v_hat) + ADAM_EPS) + DECAY * master)
    return [master_new, first_new, second_new]

def reference(frames, camera_ids, instruction_ids, action_bins, final_mask, step_count, conv_w, conv_m1, conv_m2, cond_w, cond_m1, cond_m2, small_w, small_m1, small_m2, attn_w, attn_m1, attn_m2, mlp_w, mlp_m1, mlp_m2, head_w, head_m1, head_m2):
    masters = (conv_w, cond_w, small_w, attn_w, mlp_w, head_w)
    firsts = (conv_m1, cond_m1, small_m1, attn_m1, mlp_m1, head_m1)
    seconds = (conv_m2, cond_m2, small_m2, attn_m2, mlp_m2, head_m2)
    weights = tuple((w.astype(jnp.bfloat16).astype(jnp.float32) for w in masters))
    groups = N_DP
    data = (frames.reshape(groups, -1, PIX, D), camera_ids.reshape(groups, -1), instruction_ids.reshape(groups, -1), action_bins.reshape(groups, -1, DIMS), final_mask.reshape(groups, -1))
    checked = jax.checkpoint(block_loss)

    def total(wts):

        def step(carry, block):
            return (carry + checked(wts, block), None)
        return lax.scan(step, jnp.zeros((), jnp.float32), data)[0]
    loss_sum, pull = jax.vjp(total, weights)
    grads = pull(jnp.ones((), jnp.float32))[0]
    count = jnp.sum(final_mask.astype(jnp.float32))
    square = jnp.zeros((), jnp.float32)
    for g in grads:
        square = square + jnp.sum(g * g)
    norm = jnp.sqrt(square) / count
    scale = jnp.minimum(1.0, CLIP_NORM / norm) / count
    t = step_count[0].astype(jnp.float32)
    outs = [loss_sum / count, norm]
    for idx in range(6):
        outs.extend(adam(masters[idx], firsts[idx], seconds[idx], grads[idx] * scale, t, RATES[idx]))
    return (outs[0], outs[1], outs[2], outs[3], outs[4], outs[5], outs[6], outs[7], outs[8], outs[9], outs[10], outs[11], outs[12], outs[13], outs[14], outs[15], outs[16], outs[17], outs[18], outs[19])
```

```python
import functools
import math

import jax
import jax.numpy as jnp
from jax import lax
from jax.experimental import pallas as pl
from jax.experimental.pallas import tpu as pltpu
from jax.sharding import Mesh
from jax.sharding import PartitionSpec as P

f32 = jnp.float32
bf16 = jnp.bfloat16

NAMES = ("dp_0", "dp_1", "dp_2", "mp_0", "mp_1")
SIZES = {"l": 2, "z": 4, "x": 4, "h": 2, "c": 2}
RING = 4
MESH_ID = pl.DeviceIdType.MESH
ANY = pl.BlockSpec(memory_space=pl.ANY)
INVMEM = pl.BlockSpec(memory_space=pltpu.VMEM)


def here():
    low, z, x, high, core = (lax.axis_index(n) for n in NAMES)
    return {"x": x, "y": high * 2 + low, "z": z, "c": core}


def device_of(axis, at):
    if axis == "y":
        return {"dp_0": lax.rem(at, 2), "mp_0": at // 2}
    return {{"x": "dp_2", "z": "dp_1", "c": "mp_1"}[axis]: at}


def spot(dims, at):
    index = []
    for d in dims:
        if d == "l":
            index.append(lax.rem(at["y"], 2) if "y" in at else slice(None))
        elif d == "h":
            index.append(at["y"] // 2 if "y" in at else slice(None))
        else:
            index.append(at.get(d, slice(None)))
    return tuple(index)


def without(dims, axis):
    return tuple(d for d in dims if d not in ("lh" if axis == "y" else axis))


def lead(dims):
    return tuple(SIZES[d] for d in dims)


def greet(me):
    barrier = pltpu.get_barrier_semaphore()
    for axis in "xyz":
        for k in range(1, RING):
            pl.semaphore_signal(barrier, inc=1, device_id=device_of(axis, lax.rem(me[axis] + k, RING)), device_id_type=MESH_ID)
    pl.semaphore_signal(barrier, inc=1, device_id=device_of("c", 1 - me["c"]), device_id_type=MESH_ID)
    pl.semaphore_wait(barrier, 10)


def remote(src, dst, send, recv, axis, at):
    return pltpu.make_async_remote_copy(
        src_ref=src, dst_ref=dst, send_sem=send, recv_sem=recv, device_id=device_of(axis, at), device_id_type=MESH_ID
    )


def gather_kernel(plan, *refs):
    n = len(plan)
    frames, shards, frames2, outs = refs[0], refs[1 : 1 + n], refs[1 + n], refs[2 + n : 2 + 2 * n]
    send, recv, fsend, frecv, local = refs[2 + 2 * n :]
    me = here()
    greet(me)
    own_frames = pltpu.make_async_copy(frames, frames2.at[me["c"]], local.at[n])
    own_frames.start()
    swap = remote(frames, frames2.at[me["c"]], fsend.at[n, 0], frecv.at[n, 0], "c", 1 - me["c"])
    swap.start()

    def region(b, phase, pos=None):
        dims, order = plan[b]
        at = {a: me[a] for a in order[phase:]}
        if pos is not None:
            at[order[phase]] = pos
        if "c" in dims:
            at["c"] = me["c"]
        return spot(dims, at)

    def start(b, phase):
        dims, order = plan[b]
        where = outs[b].at[region(b, phase)]
        src = shards[b] if phase == 0 else where
        copies = []
        for k in (2, 1, 3):
            c = remote(src, where, send.at[b, phase, k - 1], recv.at[b, phase, k - 1], order[phase], lax.rem(me[order[phase]] + k, RING))
            c.start()
            copies.append((k, c))
        return copies

    kept = []
    for b in range(n):
        c = pltpu.make_async_copy(shards[b], outs[b].at[region(b, 0)], local.at[b])
        c.start()
        kept.append(c)
    going = [start(b, 0) for b in range(n)]
    forwards = []

    def forward(b, number, where):
        c = remote(outs[b].at[where], outs[b].at[where], fsend.at[b, number], frecv.at[b, number], "c", 1 - me["c"])
        c.start()
        forwards.append(c)

    for phase in range(3):
        for b in range(n):
            dims, order = plan[b]
            if phase == 0:
                kept[b].wait()
            nxt = None
            for k, c in going[b]:
                c.wait()
                if phase > 0 and "c" in dims:
                    forward(b, 3 * (phase - 1) + k, region(b, phase, lax.rem(me[order[phase]] + RING - k, RING)))
            if phase == 0 and "c" in dims:
                forward(b, 0, region(b, 1))
            if phase < 2:
                going[b] = start(b, phase + 1)
    for c in forwards:
        c.wait()
    swap.wait()
    own_frames.wait()


def gather_all(frames, shards, plan, collective_id):
    n = len(plan)
    outs = [jax.ShapeDtypeStruct((2, *frames.shape), frames.dtype)]
    for s, (dims, _) in zip(shards, plan):
        outs.append(jax.ShapeDtypeStruct((*lead(dims), *s.shape), s.dtype))
    return pl.pallas_call(
        functools.partial(gather_kernel, plan),
        out_shape=outs,
        in_specs=[ANY] * (1 + n),
        out_specs=[ANY] * (1 + n),
        scratch_shapes=[
            pltpu.SemaphoreType.DMA((n, 3, 3)),
            pltpu.SemaphoreType.DMA((n, 3, 3)),
            pltpu.SemaphoreType.DMA((n + 1, 7)),
            pltpu.SemaphoreType.DMA((n + 1, 7)),
            pltpu.SemaphoreType.DMA((n + 1,)),
        ],
        compiler_params=pltpu.CompilerParams(collective_id=collective_id, has_side_effects=True),
    )(frames, *shards)


def split_index(i, sizes):
    index = []
    for s in reversed(sizes):
        index.append(lax.rem(i, s))
        i = i // s
    return tuple(reversed(index))


def add_slabs(acc, others, dims):
    sizes = lead(dims)

    def one(i, _):
        at = split_index(i, sizes)
        total = acc[at].astype(f32)
        for o in others:
            total = total + o[at].astype(f32)
        acc[at] = total.astype(acc.dtype)
        return 0

    lax.fori_loop(0, math.prod(sizes), one, 0)


def folded(v):
    total = None
    for r in range(0, v.shape[0], 8):
        for c in range(0, v.shape[1], 128):
            part = v[r : r + 8, c : c + 128]
            total = part if total is None else total + part
    return total


def scatter_kernel(plan, *refs):
    n = len(plan)
    stats, parts, stats_out, outs = refs[0], refs[1 : 1 + n], refs[1 + n], refs[2 + n : 2 + 2 * n]
    at = 2 + 2 * n
    halves, arrived = refs[at : at + n], refs[at + n : at + 2 * n]
    accs, boxes = [], []
    at += 2 * n
    for b in range(n):
        accs.append(refs[at : at + 3])
        boxes.append(refs[at + 3 : at + 6])
        at += 6
    tile, tile_box, send, recv, csend, crecv, local, tsend, trecv = refs[at:]
    me = here()
    greet(me)
    first, kept = [], []
    for b, (dims, order) in enumerate(plan):
        if "c" in dims:
            c = remote(parts[b].at[spot(dims, {"c": 1 - me["c"]})], arrived[b], csend.at[b], crecv.at[b], "c", 1 - me["c"])
            c.start()
            first.append(c)
            mine = pltpu.make_async_copy(parts[b].at[spot(dims, {"c": me["c"]})], halves[b], local.at[b])
        else:
            first.append(None)
            mine = pltpu.make_async_copy(parts[b].at[spot(dims, {order[0]: me[order[0]]})], accs[b][0], local.at[b])
        mine.start()
        kept.append(mine)

    def start(b, phase, src, dims):
        axis = plan[b][1][phase]
        copies = []
        for k in (2, 1, 3):
            pos = lax.rem(me[axis] + k, RING)
            c = remote(src.at[spot(dims, {axis: pos})], boxes[b][phase].at[k - 1], send.at[b, phase, k - 1], recv.at[b, phase, k - 1], axis, pos)
            c.start()
            copies.append(c)
        return copies

    going = [None] * n
    left = [None] * n
    ordered = [b for b in range(n) if first[b] is None] + [b for b in range(n) if first[b] is not None]
    for b in ordered:
        dims, order = plan[b]
        if first[b] is None:
            left[b] = dims
            going[b] = start(b, 0, parts[b], dims)
    for b in ordered:
        dims, order = plan[b]
        if first[b] is not None:
            left[b] = without(dims, "c")
            kept[b].wait()
            first[b].wait()
            add_slabs(halves[b], [arrived[b]], left[b])
            going[b] = start(b, 0, halves[b], left[b])
    square = jnp.zeros((8, 128), f32)
    for phase in range(3):
        for b in ordered:
            axis = plan[b][1][phase]
            rest = without(left[b], axis)
            acc, box = accs[b][phase], boxes[b][phase]
            if phase == 0 and first[b] is None:
                kept[b].wait()
            for c in going[b]:
                c.wait()
            if phase == 0:
                if first[b] is not None:
                    mine = pltpu.make_async_copy(halves[b].at[spot(left[b], {axis: me[axis]})], acc, local.at[b])
                    mine.start()
                    mine.wait()
                add_slabs(acc, [box.at[k] for k in range(3)], rest)
            elif phase == 1:
                before = accs[b][0]
                source = before.at[spot(left[b], {axis: me[axis]})]
                for i in range(math.prod(lead(rest))):
                    w = split_index(i, lead(rest))
                    total = source[w].astype(f32)
                    for k in range(3):
                        total = total + box[(k, *w)].astype(f32)
                    acc[w] = total.astype(acc.dtype)
            else:
                total = accs[b][1][spot(left[b], {axis: me[axis]})].astype(f32)
                for k in range(3):
                    total = total + box[k].astype(f32)
                outs[b][...] = total
                square = square + folded(total * total)
            left[b] = rest
            if phase < 2:
                going[b] = start(b, phase + 1, acc, rest)
    tile[0, 0:16, :] = stats[...]
    tile[0, 16:24, :] = square
    for phase, axis in enumerate("cxyz"):
        ring = 2 if axis == "c" else RING
        copies = []
        for k in range(1, ring):
            c = remote(tile.at[phase], tile_box.at[phase, k - 1], tsend.at[phase, k - 1], trecv.at[phase, k - 1], axis, lax.rem(me[axis] + k, ring))
            c.start()
            copies.append(c)
        total = tile[phase]
        for k, c in enumerate(copies):
            c.wait()
        for k, c in enumerate(copies):
            total = total + tile_box[phase, k]
        tile[phase + 1] = total
    stats_out[...] = tile[4]


def scatter_all(stats, parts, plan, collective_id):
    n = len(plan)
    outs = [jax.ShapeDtypeStruct((24, 128), f32)]
    halves, arrived, later = [], [], []
    for p, (dims, order) in zip(parts, plan):
        slab = p.shape[-2:]
        outs.append(jax.ShapeDtypeStruct(slab, f32))
        rest = dims
        if "c" in dims:
            rest = without(dims, "c")
            halves.append(pltpu.VMEM((*lead(rest), *slab), p.dtype))
            arrived.append(pltpu.VMEM((*lead(rest), *slab), p.dtype))
        else:
            halves.append(pltpu.VMEM((8, 128), p.dtype))
            arrived.append(pltpu.VMEM((8, 128), p.dtype))
        accs, boxes = [], []
        for axis in order:
            rest = without(rest, axis)
            accs.append(pltpu.VMEM((*lead(rest), *slab), p.dtype))
            boxes.append(pltpu.VMEM((3, *lead(rest), *slab), p.dtype))
        later += accs + boxes
    return pl.pallas_call(
        functools.partial(scatter_kernel, plan),
        out_shape=outs,
        in_specs=[INVMEM] + [ANY] * n,
        out_specs=[INVMEM] * (1 + n),
        scratch_shapes=[
            *halves,
            *arrived,
            *later,
            pltpu.VMEM((5, 24, 128), f32),
            pltpu.VMEM((4, 3, 24, 128), f32),
            pltpu.SemaphoreType.DMA((n, 3, 3)),
            pltpu.SemaphoreType.DMA((n, 3, 3)),
            pltpu.SemaphoreType.DMA((n,)),
            pltpu.SemaphoreType.DMA((n,)),
            pltpu.SemaphoreType.DMA((n,)),
            pltpu.SemaphoreType.DMA((4, 3)),
            pltpu.SemaphoreType.DMA((4, 3)),
        ],
        compiler_params=pltpu.CompilerParams(collective_id=collective_id, has_side_effects=True, vmem_limit_bytes=56 * 2**20),
    )(stats, *parts)


PLAN = (
    (("l", "z", "x", "h"), ("x", "z", "y")),
    (("l", "z", "x", "h"), ("x", "z", "y")),
    (("l", "z", "x", "h", "c"), ("z", "y", "x")),
    (("h", "c", "l", "z", "x"), ("y", "x", "z")),
    (("h", "c", "l", "z", "x"), ("z", "y", "x")),
)

D, EXP, MAP, PIX = 512, 3072, 9, 81
PAIR = 24
WIDTH = 384
OWNERS = WIDTH // 24
CHUNK = 3
SPAN = CHUNK * MAP * PAIR
EXPAND = 8.0 / math.sqrt(D)
PROJECT = 8.0 / math.sqrt(EXP)
VMEM_BYTES = 60 * 2**20


def sigmoid(v):
    return 0.5 + 0.5 * jnp.tanh(0.5 * v)


def nt(left, right):
    return lax.dot_general(left, right, (((1,), (1,)), ((), ())), preferred_element_type=f32)


def nn(left, right):
    return lax.dot_general(left, right, (((1,), (0,)), ((), ())), preferred_element_type=f32)


def tn(left, right):
    return lax.dot_general(left, right, (((0,), (0,)), ((), ())), preferred_element_type=f32)


def clear_borders(padded):
    zero = jnp.zeros((MAP, PAIR, WIDTH), f32)
    padded[0] = zero
    padded[MAP + 1] = zero


def each_block(body):
    def one(row, _):
        for lane in range(WIDTH // 128):
            for group in range(PAIR // 8):
                body(row, slice(8 * group, 8 * group + 8), slice(128 * lane, 128 * lane + 128))
        return 0

    lax.fori_loop(0, MAP, one, 0)


def forward_kernel(frames, expand, project, taps, pre, deep, out, act):
    step = pl.program_id(0)

    @pl.when(step == 0)
    def _():
        clear_borders(act)
        out[...] = jnp.zeros_like(out)

    weight = expand[...].reshape(WIDTH, D)
    back = project[...].reshape(WIDTH, D)

    def enter(i, _):
        rows = pl.ds(pl.multiple_of(i * SPAN, SPAN), SPAN)
        e = nt(frames[rows, :], weight) * EXPAND
        e = e.reshape(CHUNK * MAP, PAIR, WIDTH)
        pre[pl.ds(i * CHUNK * MAP, CHUNK * MAP)] = e
        act[pl.ds(1 + i * CHUNK, CHUNK)] = (e * sigmoid(e)).reshape(CHUNK, MAP, PAIR, WIDTH)
        return 0

    lax.fori_loop(0, MAP // CHUNK, enter, 0)

    def mix(row, subs, lanes):
        near = act[pl.ds(row, 3), :, subs, lanes]
        tap = [jnp.broadcast_to(taps[t : t + 1, lanes], (8, 128)) for t in range(9)]
        for col in range(MAP):
            total = None
            for t in range(9):
                at = col + t % 3 - 1
                if 0 <= at < MAP:
                    term = near[t // 3, at] * tap[t]
                    total = term if total is None else total + term
            deep[row * MAP + col, subs, lanes] = total

    each_block(mix)

    def leave(i, _):
        rows = pl.ds(pl.multiple_of(i * SPAN, SPAN), SPAN)
        v = deep[pl.ds(i * CHUNK * MAP, CHUNK * MAP)].reshape(SPAN, WIDTH)
        out[rows, :] += nn((v * sigmoid(v)).astype(bf16), back) * PROJECT
        return 0

    lax.fori_loop(0, MAP // CHUNK, leave, 0)


def conv_forward(frames, expand, project, taps):
    steps = expand.shape[0] // OWNERS
    channels = steps * WIDTH
    whole = pl.BlockSpec((PIX * PAIR, D), lambda i: (0, 0))
    weights = pl.BlockSpec((OWNERS, 24, D), lambda i: (i, 0, 0))
    maps = pl.BlockSpec((PIX, PAIR, WIDTH), lambda i: (0, 0, i))
    small = pl.BlockSpec((9, WIDTH), lambda i: (0, i))
    kept = jax.ShapeDtypeStruct((PIX, PAIR, channels), f32)
    return pl.pallas_call(
        forward_kernel,
        grid=(steps,),
        out_shape=[kept, kept, jax.ShapeDtypeStruct((PIX * PAIR, D), f32)],
        in_specs=[whole, weights, weights, small],
        out_specs=[maps, maps, whole],
        scratch_shapes=[pltpu.VMEM((MAP + 2, MAP, PAIR, WIDTH), f32)],
        compiler_params=pltpu.CompilerParams(vmem_limit_bytes=VMEM_BYTES),
    )(frames, expand, project, taps)


def backward_kernel(frames, grads, project, taps, pre, deep, dexpand, dproject, dtaps, spread, mid, dpre, acc):
    step = pl.program_id(0)

    @pl.when(step == 0)
    def _():
        clear_borders(spread)

    back = project[...].reshape(WIDTH, D)

    def enter(i, _):
        rows = pl.ds(pl.multiple_of(i * SPAN, SPAN), SPAN)
        dmid = nt(grads[rows, :], back) * PROJECT
        v = deep[pl.ds(i * CHUNK * MAP, CHUNK * MAP)].reshape(SPAN, WIDTH)
        s = sigmoid(v)
        m = v * s
        mid[rows, :] = m.astype(bf16)
        dv = dmid * (s + m * (1.0 - s))
        spread[pl.ds(1 + i * CHUNK, CHUNK)] = dv.reshape(CHUNK, MAP, PAIR, WIDTH)
        return 0

    lax.fori_loop(0, MAP // CHUNK, enter, 0)
    acc[...] = jnp.zeros_like(acc)

    def mix(row, subs, lanes):
        near = spread[pl.ds(row, 3), :, subs, lanes]
        tap = [jnp.broadcast_to(taps[t : t + 1, lanes], (8, 128)) for t in range(9)]
        sums = [None] * 9
        for col in range(MAP):
            e = pre[row * MAP + col, subs, lanes]
            s = sigmoid(e)
            a = e * s
            total = None
            for t in range(9):
                at = col + 1 - t % 3
                if 0 <= at < MAP:
                    g = near[2 - t // 3, at]
                    term = g * tap[t]
                    total = term if total is None else total + term
                    term = g * a
                    sums[t] = term if sums[t] is None else sums[t] + term
            dpre[row * MAP + col, subs, lanes] = total * (s + a * (1.0 - s))
        for t in range(9):
            acc[t, :, lanes] += sums[t]

    each_block(mix)
    dtaps[...] = jnp.sum(acc[...], axis=1) * (8.0 / 3.0)
    low = dpre[...].reshape(PIX * PAIR, WIDTH).astype(bf16)
    dexpand[...] = (tn(low, frames[...]) * EXPAND).astype(bf16).reshape(OWNERS, 24, D)
    dproject[...] = (tn(mid[...], grads[...]) * PROJECT).astype(bf16).reshape(OWNERS, 24, D)


def conv_backward(frames, grads, project, taps, pre, deep):
    steps = project.shape[0] // OWNERS
    channels = steps * WIDTH
    whole = pl.BlockSpec((PIX * PAIR, D), lambda i: (0, 0))
    weights = pl.BlockSpec((OWNERS, 24, D), lambda i: (i, 0, 0))
    maps = pl.BlockSpec((PIX, PAIR, WIDTH), lambda i: (0, 0, i))
    small = pl.BlockSpec((9, WIDTH), lambda i: (0, i))
    owned = jax.ShapeDtypeStruct((OWNERS * steps, 24, D), bf16)
    return pl.pallas_call(
        backward_kernel,
        grid=(steps,),
        out_shape=[owned, owned, jax.ShapeDtypeStruct((9, channels), f32)],
        in_specs=[whole, whole, weights, small, maps, maps],
        out_specs=[weights, weights, small],
        scratch_shapes=[
            pltpu.VMEM((MAP + 2, MAP, PAIR, WIDTH), f32),
            pltpu.VMEM((PIX * PAIR, WIDTH), bf16),
            pltpu.VMEM((PIX, PAIR, WIDTH), f32),
            pltpu.VMEM((9, 8, WIDTH), f32),
        ],
        compiler_params=pltpu.CompilerParams(vmem_limit_bytes=VMEM_BYTES),
    )(frames, grads, project, taps, pre, deep)


INSTR, DIMS, BINS, NTOK, FRAMES, HEADS, HD = 744, 11, 256, 8, 6, 8, 64
TABLE = INSTR + 2
TAIL = TABLE + 11
IMAGES = 12
MP = ("mp_0", "mp_1")
DP_MP = NAMES
DP = ("dp_0", "dp_1", "dp_2")
HIGH = lax.Precision.HIGHEST
LN_EPS = 1e-06
CLIP_NORM = 0.02
BETA_ONE = 0.9
BETA_TWO = 0.999
ADAM_EPS = 1e-08
DECAY = 0.01
OUT_MULT = 2.0
RATES = (0.1, 0.1, 0.2, 0.05, 0.05, 0.2)


def layer_fwd(x, gain):
    centre = x - jnp.mean(x, -1, keepdims=True)
    inverse = lax.rsqrt(jnp.mean(centre * centre, -1, keepdims=True) + LN_EPS)
    normed = centre * inverse
    return (normed * (1.0 + gain), (normed, inverse))


def layer_back(kept, gain, grad_out):
    normed, inverse = kept
    dnormed = grad_out * (1.0 + gain)
    grad_in = inverse * (
        dnormed
        - jnp.mean(dnormed, -1, keepdims=True)
        - normed * jnp.mean(dnormed * normed, -1, keepdims=True)
    )
    return (grad_in, jnp.sum(grad_out * normed, 0))


def learn_tokens(feature, learner):
    logit = jnp.einsum("kpd,td->kpt", feature, learner, precision=HIGH) * (4.0 / math.sqrt(D))
    weight = jax.nn.softmax(logit, axis=1)
    return jnp.einsum("kpt,kpd->ktd", weight, feature, precision=HIGH)


def gelu_tanh(value):
    return jax.nn.gelu(value, approximate=True)


def adam(master, first, second, grad, t, rate):
    first_new = BETA_ONE * first + (1.0 - BETA_ONE) * grad
    second_new = BETA_TWO * second + (1.0 - BETA_TWO) * grad * grad
    m_hat = first_new / (1.0 - BETA_ONE**t)
    v_hat = second_new / (1.0 - BETA_TWO**t)
    master_new = master - rate * (m_hat / (jnp.sqrt(v_hat) + ADAM_EPS) + DECAY * master)
    return [master_new, first_new, second_new]


def pack_misc(film, table, small, taps):
    n = film.shape[0]
    tail = jnp.concatenate([table, small, taps], axis=2)
    tail = jnp.pad(tail, ((0, 0), (0, 0), (0, 2 * D - tail.shape[2])))
    return jnp.concatenate([film[:, :, :D], film[:, :, D:], tail[:, :, :D], tail[:, :, D:]], axis=1)


def unpack_misc(misc):
    film = jnp.concatenate([misc[:, 0:4], misc[:, 4:8]], axis=2)
    tail = jnp.concatenate([misc[:, 8:12], misc[:, 12:16]], axis=2)
    return film, tail[:, :, :TABLE], tail[:, :, TABLE:TAIL], tail[:, :, TAIL : TAIL + 54]


def pack_attn_head(attn, head):
    both = jnp.concatenate([*attn, head], axis=-1)
    return jnp.pad(both, [(0, 0)] * (both.ndim - 1) + [(0, 1280 - both.shape[-1])])


def swap_cores(value):
    return lax.ppermute(value, "mp_1", [(0, 1), (1, 0)])


def transformer(tok, weights_one, weights_two, gains, bins, mask_f):
    rows = tok.shape[0]
    seq = FRAMES * NTOK
    count_ex = rows // seq
    scale = HD ** (-0.5)
    wq, wk, wv, wo = (weights_one[:, :, 128 * j : 128 * j + 128] for j in range(4))
    head = weights_one[:, :, 512 : 512 + DIMS * 64]
    up_w, down_w = weights_two[:, :, :512], weights_two[:, :, 512:]

    def dot(spec, a, b):
        return jnp.einsum(spec, a, b, preferred_element_type=f32)

    h1, kept1 = layer_fwd(tok, gains[0])
    h1_low = h1.astype(bf16)
    split = (count_ex, seq, HEADS, HD)
    q, k, v = (dot("rd,mdc->rmc", h1_low, w).astype(bf16).reshape(split) for w in (wq, wk, wv))
    scores = dot("bqhd,bkhd->bhqk", q, k) * scale
    causal = jnp.tril(jnp.ones((seq, seq), bool))
    prob = jax.nn.softmax(jnp.where(causal, scores, -1e30), axis=-1)
    prob_low = prob.astype(bf16)
    ctx = dot("bhqk,bkhd->bqhd", prob_low, v).astype(bf16).reshape(rows, 4, 128)
    x1 = tok + OUT_MULT * dot("rmc,mdc->rd", ctx, wo)
    h2, kept2 = layer_fwd(x1, gains[1])
    h2_low = h2.astype(bf16)
    up = dot("rd,mdc->rmc", h2_low, up_w)
    hidden, gelu_pull = jax.vjp(gelu_tanh, up)
    hidden_low = hidden.astype(bf16)
    x2 = x1 + dot("rmc,mdc->rd", hidden_low, down_w)
    normed, kept3 = layer_fwd(x2, gains[2])
    pooled = jnp.mean(normed.reshape(-1, NTOK, D), axis=1).astype(bf16)
    count = pooled.shape[0]
    logits = dot("rd,mdc->rmc", pooled, head).reshape(count, 4, DIMS, 64)
    index = jnp.arange(4)[:, None, None] * 64 + jnp.arange(64)
    hit = bins[:, None, :, None] == index
    top = jnp.max(logits, (1, 3), keepdims=True)
    expo = jnp.exp(logits - top)
    total = jnp.sum(expo, (1, 3), keepdims=True)
    lse = top + jnp.log(total)
    target = jnp.sum(jnp.where(hit, logits, 0.0), (1, 3))
    loss_part = jnp.sum(mask_f * jnp.sum(lse[:, 0, :, 0] - target, -1))
    dlogit = mask_f[:, None, None, None] * (jnp.exp(logits - lse) - hit.astype(f32))
    dlogit = dlogit.astype(bf16).reshape(count, 4, DIMS * 64)
    dhead = dot("rd,rmc->mdc", pooled, dlogit)
    dpooled = dot("rmc,mdc->rd", dlogit, head)
    dnormed = jnp.broadcast_to(dpooled[:, None, :] / NTOK, (count, NTOK, D)).reshape(rows, D)
    dx2, dgain2 = layer_back(kept3, gains[2], dnormed)
    dbranch = dx2.astype(bf16)
    ddown = dot("rd,rmc->mdc", dbranch, hidden_low)
    dup = gelu_pull(dot("rd,mdc->rmc", dbranch, down_w))[0].astype(bf16)
    dupw = dot("rd,rmc->mdc", h2_low, dup)
    dh2 = dot("rmc,mdc->rd", dup, up_w)
    dx1_norm, dgain1 = layer_back(kept2, gains[1], dh2)
    dx1 = dx2 + dx1_norm
    dattn = dx1.astype(bf16)
    dctx = (dot("rd,mdc->rmc", dattn, wo) * OUT_MULT).astype(bf16)
    dwo = dot("rd,rmc->mdc", dattn, ctx) * OUT_MULT
    dctx4 = dctx.reshape(split)
    dprob = dot("bqhd,bkhd->bhqk", dctx4, v)
    dv = dot("bhqk,bqhd->bkhd", prob_low, dctx4)
    ds = (prob * (dprob - jnp.sum(prob * dprob, -1, keepdims=True))).astype(bf16)
    dq = dot("bhqk,bkhd->bqhd", ds, k) * scale
    dk = dot("bhqk,bqhd->bkhd", ds, q) * scale
    grads = [g.astype(bf16).reshape(rows, 4, 128) for g in (dq, dk, dv)]
    dws = [dot("rd,rmc->mdc", h1_low, g) for g in grads]
    dh1 = sum(dot("rmc,mdc->rd", g, w) for g, w in zip(grads, (wq, wk, wv)))
    dtok_norm, dgain0 = layer_back(kept1, gains[0], dh1)
    done_one = pack_attn_head([g.astype(bf16) for g in (*dws, dwo)], dhead.astype(bf16))
    done_two = jnp.concatenate([dupw.astype(bf16), ddown.astype(bf16)], axis=-1)
    return loss_part, dx1 + dtok_norm, (dgain0, dgain1, dgain2), done_one, done_two


def per_device(
    frames, camera_ids, instruction_ids, action_bins, final_mask, step_count,
    conv_w, conv_m1, conv_m2, cond_w, cond_m1, cond_m2, small_w, small_m1, small_m2,
    attn_w, attn_m1, attn_m2, mlp_w, mlp_m1, mlp_m2, head_w, head_m1, head_m2,
):
    mp_idx = lax.axis_index(MP)
    core = lax.axis_index("mp_1")
    conv_t = conv_w.T.astype(bf16)
    cond_t = cond_w.T.astype(bf16)
    misc = pack_misc(
        cond_t[None, :, : 2 * D], cond_t[None, :, 2 * D :], small_w.T.astype(bf16)[None], conv_t[:, 2 * D :].reshape(1, 4, 54)
    )[0]
    attn_l = attn_w.astype(bf16)
    shards = (
        conv_t[:, :D],
        conv_t[:, D : 2 * D],
        misc,
        pack_attn_head([attn_l[j] for j in range(4)], head_w.astype(bf16).reshape(16, DIMS * 64)),
        jnp.moveaxis(mlp_w.astype(bf16), 0, 1).reshape(16, 1024),
    )
    frames2, expand, project, misc_all, one_all, two_all = gather_all(frames, shards, PLAN, 1)
    expand = expand.reshape(64, 24, D)
    project = project.reshape(64, 24, D)
    film_t, table_t, small_t, taps_all = unpack_misc(misc_all.reshape(128, 16, D))
    film_w = film_t.reshape(D, 2 * D)
    table_w = table_t.reshape(D, TABLE)
    small_f = small_t.reshape(D, 11).T.astype(f32)
    taps_own = lax.dynamic_index_in_dim(taps_all.reshape(64, 2, 24, 9), core, 1, keepdims=False)
    taps = taps_own.reshape(1536, 9).T.astype(f32) * (8.0 / 3.0)
    weights_one = one_all.reshape(4, D, 1280)
    weights_two = two_all.reshape(4, D, 1024)

    cells = frames2.transpose(2, 0, 1, 3).reshape(PIX * PAIR, D)
    pre, deep, part = conv_forward(cells, expand, project, taps)
    part = part.reshape(PIX, 2, IMAGES, D)
    kept = lax.dynamic_index_in_dim(part, core, 1, keepdims=False)
    sent = swap_cores(lax.dynamic_index_in_dim(part, 1 - core, 1, keepdims=False))
    proj3 = (kept + sent).transpose(1, 0, 2)

    slot = mp_idx * IMAGES + jnp.arange(IMAGES)
    example = slot // FRAMES
    instr_img = jnp.sum(
        jnp.where(example[:, None] == jnp.arange(instruction_ids.shape[0])[None, :], instruction_ids[None, :], 0), 1
    )
    entries = jnp.arange(TABLE)[None, :]
    choose = ((entries == instr_img[:, None]) | (entries == INSTR + camera_ids[:, None])).astype(bf16)
    film_mult = 16.0 / math.sqrt(D)
    cvec = nt(choose, table_w).astype(bf16)
    film = nn(cvec, film_w) * film_mult
    gamma, beta = film[:, None, :D], film[:, None, D:]
    feature = frames.astype(f32) + proj3 * (1.0 + gamma) + beta
    tok, learn_pull = jax.vjp(learn_tokens, feature, small_f[3:])
    tok = tok.reshape(IMAGES * NTOK, D).astype(bf16).astype(f32)
    mask_f = lax.dynamic_slice_in_dim(final_mask, mp_idx * IMAGES, IMAGES).astype(f32)
    bins = lax.dynamic_slice_in_dim(action_bins, mp_idx * IMAGES, IMAGES)
    loss_part, dtok, dgains, done_one, done_two = transformer(tok, weights_one, weights_two, small_f[:3], bins, mask_f)

    dfeature, dlearner = learn_pull(dtok.reshape(IMAGES, NTOK, D))
    dproj = (dfeature * (1.0 + gamma)).astype(bf16).transpose(1, 0, 2)
    other = swap_cores(dproj)
    both = jnp.where(core == 0, jnp.stack([dproj, other], 1), jnp.stack([other, dproj], 1))
    dcells = both.reshape(PIX * PAIR, D)
    dfilm = jnp.concatenate([jnp.sum(dfeature * proj3, 1), jnp.sum(dfeature, 1)], 1).astype(bf16)
    dcvec = nt(dfilm, film_w) * film_mult
    dfilm_w = tn(cvec, dfilm) * film_mult
    dtable = lax.dot_general(
        dcvec, choose.astype(f32), (((0,), (0,)), ((), ())), precision=HIGH, preferred_element_type=f32
    )
    dexpand, dproject, dtaps = conv_backward(cells, dcells, project, taps, pre, deep)
    dtaps = dtaps.T.reshape(64, 1, 4, 54)
    dtaps = jnp.where(jnp.arange(2)[None, :, None, None] == core, dtaps, 0.0).reshape(128, 4, 54)
    dsmall = jnp.concatenate([jnp.stack(dgains), dlearner], 0)
    dmisc = pack_misc(
        dfilm_w.reshape(128, 4, 2 * D), dtable.reshape(128, 4, TABLE), dsmall.T.reshape(128, 4, 11), dtaps
    ).astype(bf16)
    stats = jnp.pad(
        jnp.stack([loss_part, jnp.sum(mask_f)])[:, None, None], ((0, 0), (0, 7), (0, 127))
    ).reshape(16, 128)
    parts = [
        g.reshape(*lead(dims), *s.shape)
        for g, s, (dims, _) in zip((dexpand, dproject, dmisc, done_one, done_two), shards, PLAN)
    ]
    totals, gexpand, gproject, gmisc, gone, gtwo = scatter_all(stats, parts, PLAN, 2)
    gfilm, gtable, gsmall, gtaps = unpack_misc(gmisc[None])
    grads = (
        jnp.concatenate([gexpand, gproject, gtaps.reshape(24, 9)], 1).T,
        jnp.concatenate([gfilm[0], gtable[0]], 1).T,
        gsmall[0].T,
        jnp.stack([gone[:, 128 * j : 128 * j + 128] for j in range(4)]),
        jnp.moveaxis(gtwo.reshape(16, 2, 512), 1, 0),
        gone[:, 512 : 512 + DIMS * 64].reshape(16, DIMS, 64),
    )
    loss_sum, count, square = (jnp.sum(totals[8 * i : 8 * i + 8]) for i in range(3))
    norm = jnp.sqrt(square) / count
    factor = jnp.minimum(1.0, CLIP_NORM / norm) / count
    steps_done = step_count[0].astype(f32)
    masters = (conv_w, cond_w, small_w, attn_w, mlp_w, head_w)
    firsts = (conv_m1, cond_m1, small_m1, attn_m1, mlp_m1, head_m1)
    seconds = (conv_m2, cond_m2, small_m2, attn_m2, mlp_m2, head_m2)
    outs = [loss_sum / count, norm]
    for idx in range(6):
        outs.extend(adam(masters[idx], firsts[idx], seconds[idx], grads[idx] * factor, steps_done, RATES[idx]))
    return tuple(outs)


def solution(mesh):
    torus = Mesh(mesh.devices.reshape(2, 4, 4, 2, 2), NAMES)
    weights = (
        *[P(None, DP_MP)] * 9,
        *[P(None, DP, MP)] * 6,
        *[P(DP, None, MP)] * 3,
    )
    data = (P(DP_MP, None, None), P(DP_MP), P(DP), P(DP, None), P(DP), P())
    return jax.shard_map(
        per_device, mesh=torus, in_specs=(*data, *weights), out_specs=(P(), P(), *weights), check_vma=False
    )
```

```python
import functools
import math

import jax
import jax.numpy as jnp
from jax import lax
from jax.experimental import pallas as pl
from jax.experimental.pallas import tpu as pltpu
from jax.sharding import Mesh
from jax.sharding import PartitionSpec as P

f32 = jnp.float32
bf16 = jnp.bfloat16

NAMES = ("dp_0", "dp_1", "dp_2", "mp_0", "mp_1")
SIZES = {"l": 2, "z": 4, "x": 4, "h": 2, "c": 2}
RING = 4
MESH_ID = pl.DeviceIdType.MESH
ANY = pl.BlockSpec(memory_space=pl.ANY)
INVMEM = pl.BlockSpec(memory_space=pltpu.VMEM)


def here():
    low, z, x, high, core = (lax.axis_index(n) for n in NAMES)
    return {"x": x, "y": high * 2 + low, "z": z, "c": core}


def device_of(axis, at):
    if axis == "y":
        return {"dp_0": lax.rem(at, 2), "mp_0": at // 2}
    return {{"x": "dp_2", "z": "dp_1", "c": "mp_1"}[axis]: at}


def spot(dims, at):
    index = []
    for d in dims:
        if d == "l":
            index.append(lax.rem(at["y"], 2) if "y" in at else slice(None))
        elif d == "h":
            index.append(at["y"] // 2 if "y" in at else slice(None))
        else:
            index.append(at.get(d, slice(None)))
    return tuple(index)


def without(dims, axis):
    return tuple(d for d in dims if d not in ("lh" if axis == "y" else axis))


def lead(dims):
    return tuple(SIZES[d] for d in dims)


def greet(me):
    barrier = pltpu.get_barrier_semaphore()
    for axis in "xyz":
        for k in range(1, RING):
            pl.semaphore_signal(barrier, inc=1, device_id=device_of(axis, lax.rem(me[axis] + k, RING)), device_id_type=MESH_ID)
    pl.semaphore_signal(barrier, inc=1, device_id=device_of("c", 1 - me["c"]), device_id_type=MESH_ID)
    pl.semaphore_wait(barrier, 10)


def remote(src, dst, send, recv, axis, at):
    return pltpu.make_async_remote_copy(
        src_ref=src, dst_ref=dst, send_sem=send, recv_sem=recv, device_id=device_of(axis, at), device_id_type=MESH_ID
    )


def gather_kernel(plan, *refs):
    n = len(plan)
    pairs, shards = refs[0:2], refs[2 : 2 + n]
    both, outs = refs[2 + n : 4 + n], refs[4 + n : 4 + 2 * n]
    send, recv, fsend, frecv, local = refs[4 + 2 * n :]
    me = here()
    greet(me)
    swaps = []
    for i in range(2):
        mine = pltpu.make_async_copy(pairs[i], both[i].at[me["c"]], local.at[n + i])
        mine.start()
        swap = remote(pairs[i], both[i].at[me["c"]], fsend.at[n, i], frecv.at[n, i], "c", 1 - me["c"])
        swap.start()
        swaps += [mine, swap]

    def region(b, phase, pos=None):
        dims, order = plan[b]
        at = {a: me[a] for a in order[phase:]}
        if pos is not None:
            at[order[phase]] = pos
        if "c" in dims:
            at["c"] = me["c"]
        return spot(dims, at)

    def start(b, phase):
        dims, order = plan[b]
        where = outs[b].at[region(b, phase)]
        src = shards[b] if phase == 0 else where
        copies = []
        for k in (2, 1, 3):
            c = remote(src, where, send.at[b, phase, k - 1], recv.at[b, phase, k - 1], order[phase], lax.rem(me[order[phase]] + k, RING))
            c.start()
            copies.append((k, c))
        return copies

    kept = []
    for b in range(n):
        c = pltpu.make_async_copy(shards[b], outs[b].at[region(b, 0)], local.at[b])
        c.start()
        kept.append(c)
    going = [start(b, 0) for b in range(n)]
    forwards = []

    def forward(b, number, where):
        c = remote(outs[b].at[where], outs[b].at[where], fsend.at[b, number], frecv.at[b, number], "c", 1 - me["c"])
        c.start()
        forwards.append(c)

    for phase in range(3):
        for b in range(n):
            dims, order = plan[b]
            if phase == 0:
                kept[b].wait()
            nxt = None
            for k, c in going[b]:
                c.wait()
                if phase > 0 and "c" in dims:
                    forward(b, 3 * (phase - 1) + k, region(b, phase, lax.rem(me[order[phase]] + RING - k, RING)))
            if phase == 0 and "c" in dims:
                forward(b, 0, region(b, 1))
            if phase < 2:
                going[b] = start(b, phase + 1)
    for c in forwards + swaps:
        c.wait()


def gather_all(pairs, shards, plan, collective_id):
    n = len(plan)
    outs = [jax.ShapeDtypeStruct((2, *p.shape), p.dtype) for p in pairs]
    for s, (dims, _) in zip(shards, plan):
        outs.append(jax.ShapeDtypeStruct((*lead(dims), *s.shape), s.dtype))
    return pl.pallas_call(
        functools.partial(gather_kernel, plan),
        out_shape=outs,
        in_specs=[ANY] * (2 + n),
        out_specs=[ANY] * (2 + n),
        scratch_shapes=[
            pltpu.SemaphoreType.DMA((n, 3, 3)),
            pltpu.SemaphoreType.DMA((n, 3, 3)),
            pltpu.SemaphoreType.DMA((n + 1, 7)),
            pltpu.SemaphoreType.DMA((n + 1, 7)),
            pltpu.SemaphoreType.DMA((n + 2,)),
        ],
        compiler_params=pltpu.CompilerParams(collective_id=collective_id, has_side_effects=True),
    )(*pairs, *shards)


def split_index(i, sizes):
    index = []
    for s in reversed(sizes):
        index.append(lax.rem(i, s))
        i = i // s
    return tuple(reversed(index))


def add_slabs(acc, others, dims):
    sizes = lead(dims)

    def one(i, _):
        at = split_index(i, sizes)
        total = acc[at].astype(f32)
        for o in others:
            total = total + o[at].astype(f32)
        acc[at] = total.astype(acc.dtype)
        return 0

    lax.fori_loop(0, math.prod(sizes), one, 0)


def folded(v):
    total = None
    for r in range(0, v.shape[0], 8):
        for c in range(0, v.shape[1], 128):
            part = v[r : r + 8, c : c + 128]
            total = part if total is None else total + part
    return total


def scatter_kernel(plan, *refs):
    n = len(plan)
    stats, parts, stats_out, outs = refs[0], refs[1 : 1 + n], refs[1 + n], refs[2 + n : 2 + 2 * n]
    at = 2 + 2 * n
    halves, arrived = refs[at : at + n], refs[at + n : at + 2 * n]
    accs, boxes = [], []
    at += 2 * n
    for b in range(n):
        accs.append(refs[at : at + 3])
        boxes.append(refs[at + 3 : at + 6])
        at += 6
    tile, tile_box, send, recv, csend, crecv, local, tsend, trecv = refs[at:]
    me = here()
    greet(me)
    first, kept = [], []
    for b, (dims, order) in enumerate(plan):
        if "c" in dims:
            c = remote(parts[b].at[spot(dims, {"c": 1 - me["c"]})], arrived[b], csend.at[b], crecv.at[b], "c", 1 - me["c"])
            c.start()
            first.append(c)
            mine = pltpu.make_async_copy(parts[b].at[spot(dims, {"c": me["c"]})], halves[b], local.at[b])
        else:
            first.append(None)
            mine = pltpu.make_async_copy(parts[b].at[spot(dims, {order[0]: me[order[0]]})], accs[b][0], local.at[b])
        mine.start()
        kept.append(mine)

    def start(b, phase, src, dims):
        axis = plan[b][1][phase]
        copies = []
        for k in (2, 1, 3):
            pos = lax.rem(me[axis] + k, RING)
            c = remote(src.at[spot(dims, {axis: pos})], boxes[b][phase].at[k - 1], send.at[b, phase, k - 1], recv.at[b, phase, k - 1], axis, pos)
            c.start()
            copies.append(c)
        return copies

    going = [None] * n
    left = [None] * n
    ordered = [b for b in range(n) if first[b] is None] + [b for b in range(n) if first[b] is not None]
    for b in ordered:
        dims, order = plan[b]
        if first[b] is None:
            left[b] = dims
            going[b] = start(b, 0, parts[b], dims)
    for b in ordered:
        dims, order = plan[b]
        if first[b] is not None:
            left[b] = without(dims, "c")
            kept[b].wait()
            first[b].wait()
            add_slabs(halves[b], [arrived[b]], left[b])
            going[b] = start(b, 0, halves[b], left[b])
    square = jnp.zeros((8, 128), f32)
    for phase in range(3):
        for b in ordered:
            axis = plan[b][1][phase]
            rest = without(left[b], axis)
            acc, box = accs[b][phase], boxes[b][phase]
            if phase == 0 and first[b] is None:
                kept[b].wait()
            for c in going[b]:
                c.wait()
            if phase == 0:
                if first[b] is not None:
                    mine = pltpu.make_async_copy(halves[b].at[spot(left[b], {axis: me[axis]})], acc, local.at[b])
                    mine.start()
                    mine.wait()
                add_slabs(acc, [box.at[k] for k in range(3)], rest)
            elif phase == 1:
                before = accs[b][0]
                source = before.at[spot(left[b], {axis: me[axis]})]
                for i in range(math.prod(lead(rest))):
                    w = split_index(i, lead(rest))
                    total = source[w].astype(f32)
                    for k in range(3):
                        total = total + box[(k, *w)].astype(f32)
                    acc[w] = total.astype(acc.dtype)
            else:
                total = accs[b][1][spot(left[b], {axis: me[axis]})].astype(f32)
                for k in range(3):
                    total = total + box[k].astype(f32)
                outs[b][...] = total
                square = square + folded(total * total)
            left[b] = rest
            if phase < 2:
                going[b] = start(b, phase + 1, acc, rest)
    tile[0, 0:16, :] = stats[...]
    tile[0, 16:24, :] = square
    for phase, axis in enumerate("cxyz"):
        ring = 2 if axis == "c" else RING
        copies = []
        for k in range(1, ring):
            c = remote(tile.at[phase], tile_box.at[phase, k - 1], tsend.at[phase, k - 1], trecv.at[phase, k - 1], axis, lax.rem(me[axis] + k, ring))
            c.start()
            copies.append(c)
        total = tile[phase]
        for k, c in enumerate(copies):
            c.wait()
        for k, c in enumerate(copies):
            total = total + tile_box[phase, k]
        tile[phase + 1] = total
    stats_out[...] = tile[4]


def scatter_all(stats, parts, plan, collective_id):
    n = len(plan)
    outs = [jax.ShapeDtypeStruct((24, 128), f32)]
    halves, arrived, later = [], [], []
    for p, (dims, order) in zip(parts, plan):
        slab = p.shape[-2:]
        outs.append(jax.ShapeDtypeStruct(slab, f32))
        rest = dims
        if "c" in dims:
            rest = without(dims, "c")
            halves.append(pltpu.VMEM((*lead(rest), *slab), p.dtype))
            arrived.append(pltpu.VMEM((*lead(rest), *slab), p.dtype))
        else:
            halves.append(pltpu.VMEM((8, 128), p.dtype))
            arrived.append(pltpu.VMEM((8, 128), p.dtype))
        accs, boxes = [], []
        for axis in order:
            rest = without(rest, axis)
            accs.append(pltpu.VMEM((*lead(rest), *slab), p.dtype))
            boxes.append(pltpu.VMEM((3, *lead(rest), *slab), p.dtype))
        later += accs + boxes
    return pl.pallas_call(
        functools.partial(scatter_kernel, plan),
        out_shape=outs,
        in_specs=[INVMEM] + [ANY] * n,
        out_specs=[INVMEM] * (1 + n),
        scratch_shapes=[
            *halves,
            *arrived,
            *later,
            pltpu.VMEM((5, 24, 128), f32),
            pltpu.VMEM((4, 3, 24, 128), f32),
            pltpu.SemaphoreType.DMA((n, 3, 3)),
            pltpu.SemaphoreType.DMA((n, 3, 3)),
            pltpu.SemaphoreType.DMA((n,)),
            pltpu.SemaphoreType.DMA((n,)),
            pltpu.SemaphoreType.DMA((n,)),
            pltpu.SemaphoreType.DMA((4, 3)),
            pltpu.SemaphoreType.DMA((4, 3)),
        ],
        compiler_params=pltpu.CompilerParams(collective_id=collective_id, has_side_effects=True, vmem_limit_bytes=56 * 2**20),
    )(stats, *parts)


OWNED = ("l", "z", "x", "h")
GATHER = (
    (OWNED, ("x", "z", "y")),
    (OWNED, ("x", "z", "y")),
    (OWNED, ("x", "z", "y")),
    (("c", *OWNED), ("z", "y", "x")),
    (("h", "c", "l", "z", "x"), ("y", "x", "z")),
    (("h", "c", "l", "z", "x"), ("z", "y", "x")),
)
SCATTER = (
    (OWNED, ("x", "z", "y")),
    (OWNED, ("x", "z", "y")),
    (OWNED, ("x", "z", "y")),
    (OWNED, ("z", "y", "x")),
    (("h", "l", "z", "x"), ("y", "x", "z")),
    (("h", "l", "z", "x"), ("z", "y", "x")),
)

D, EXP, MAP, PIX = 512, 3072, 9, 81
PAIR = 24
WIDTH = 384
OWNERS = WIDTH // 24
CHUNK = 3
SPAN = CHUNK * MAP * PAIR
EXPAND = 8.0 / math.sqrt(D)
PROJECT = 8.0 / math.sqrt(EXP)
VMEM_BYTES = 60 * 2**20


def sigmoid(v):
    return 0.5 + 0.5 * jnp.tanh(0.5 * v)


def nt(left, right):
    return lax.dot_general(left, right, (((1,), (1,)), ((), ())), preferred_element_type=f32)


def nn(left, right):
    return lax.dot_general(left, right, (((1,), (0,)), ((), ())), preferred_element_type=f32)


def tn(left, right):
    return lax.dot_general(left, right, (((0,), (0,)), ((), ())), preferred_element_type=f32)


def clear_borders(padded):
    zero = jnp.zeros((MAP, PAIR, WIDTH), f32)
    padded[0] = zero
    padded[MAP + 1] = zero


def each_block(body):
    def one(row, _):
        for lane in range(WIDTH // 128):
            for group in range(PAIR // 8):
                body(row, slice(8 * group, 8 * group + 8), slice(128 * lane, 128 * lane + 128))
        return 0

    lax.fori_loop(0, MAP, one, 0)


def forward_kernel(frames, expand, project, taps, pre, deep, out, act):
    step = pl.program_id(0)

    @pl.when(step == 0)
    def _():
        clear_borders(act)
        out[...] = jnp.zeros_like(out)

    weight = expand[...].reshape(WIDTH, D)
    back = project[...].reshape(WIDTH, D)

    def enter(i, _):
        rows = pl.ds(pl.multiple_of(i * SPAN, SPAN), SPAN)
        e = nt(frames[rows, :], weight) * EXPAND
        e = e.reshape(CHUNK * MAP, PAIR, WIDTH)
        pre[pl.ds(i * CHUNK * MAP, CHUNK * MAP)] = e
        act[pl.ds(1 + i * CHUNK, CHUNK)] = (e * sigmoid(e)).reshape(CHUNK, MAP, PAIR, WIDTH)
        return 0

    lax.fori_loop(0, MAP // CHUNK, enter, 0)

    def mix(row, subs, lanes):
        near = act[pl.ds(row, 3), :, subs, lanes]
        tap = [jnp.broadcast_to(taps[t : t + 1, lanes], (8, 128)) for t in range(9)]
        for col in range(MAP):
            total = None
            for t in range(9):
                at = col + t % 3 - 1
                if 0 <= at < MAP:
                    term = near[t // 3, at] * tap[t]
                    total = term if total is None else total + term
            deep[row * MAP + col, subs, lanes] = total

    each_block(mix)

    def leave(i, _):
        rows = pl.ds(pl.multiple_of(i * SPAN, SPAN), SPAN)
        v = deep[pl.ds(i * CHUNK * MAP, CHUNK * MAP)].reshape(SPAN, WIDTH)
        out[rows, :] += nn((v * sigmoid(v)).astype(bf16), back) * PROJECT
        return 0

    lax.fori_loop(0, MAP // CHUNK, leave, 0)


def conv_forward(frames, expand, project, taps):
    steps = expand.shape[0] // OWNERS
    channels = steps * WIDTH
    whole = pl.BlockSpec((PIX * PAIR, D), lambda i: (0, 0))
    weights = pl.BlockSpec((OWNERS, 24, D), lambda i: (i, 0, 0))
    maps = pl.BlockSpec((PIX, PAIR, WIDTH), lambda i: (0, 0, i))
    small = pl.BlockSpec((9, WIDTH), lambda i: (0, i))
    kept = jax.ShapeDtypeStruct((PIX, PAIR, channels), f32)
    return pl.pallas_call(
        forward_kernel,
        grid=(steps,),
        out_shape=[kept, kept, jax.ShapeDtypeStruct((PIX * PAIR, D), f32)],
        in_specs=[whole, weights, weights, small],
        out_specs=[maps, maps, whole],
        scratch_shapes=[pltpu.VMEM((MAP + 2, MAP, PAIR, WIDTH), f32)],
        compiler_params=pltpu.CompilerParams(vmem_limit_bytes=VMEM_BYTES),
    )(frames, expand, project, taps)


def backward_kernel(frames, grads, project, taps, pre, deep, dexpand, dproject, dtaps, spread, mid, dpre, acc):
    step = pl.program_id(0)

    @pl.when(step == 0)
    def _():
        clear_borders(spread)

    back = project[...].reshape(WIDTH, D)

    def enter(i, _):
        rows = pl.ds(pl.multiple_of(i * SPAN, SPAN), SPAN)
        dmid = nt(grads[rows, :], back) * PROJECT
        v = deep[pl.ds(i * CHUNK * MAP, CHUNK * MAP)].reshape(SPAN, WIDTH)
        s = sigmoid(v)
        m = v * s
        mid[rows, :] = m.astype(bf16)
        dv = dmid * (s + m * (1.0 - s))
        spread[pl.ds(1 + i * CHUNK, CHUNK)] = dv.reshape(CHUNK, MAP, PAIR, WIDTH)
        return 0

    lax.fori_loop(0, MAP // CHUNK, enter, 0)
    acc[...] = jnp.zeros_like(acc)

    def mix(row, subs, lanes):
        near = spread[pl.ds(row, 3), :, subs, lanes]
        tap = [jnp.broadcast_to(taps[t : t + 1, lanes], (8, 128)) for t in range(9)]
        sums = [None] * 9
        for col in range(MAP):
            e = pre[row * MAP + col, subs, lanes]
            s = sigmoid(e)
            a = e * s
            total = None
            for t in range(9):
                at = col + 1 - t % 3
                if 0 <= at < MAP:
                    g = near[2 - t // 3, at]
                    term = g * tap[t]
                    total = term if total is None else total + term
                    term = g * a
                    sums[t] = term if sums[t] is None else sums[t] + term
            dpre[row * MAP + col, subs, lanes] = total * (s + a * (1.0 - s))
        for t in range(9):
            acc[t, :, lanes] += sums[t]

    each_block(mix)
    dtaps[...] = jnp.sum(acc[...], axis=1) * (8.0 / 3.0)
    low = dpre[...].reshape(PIX * PAIR, WIDTH).astype(bf16)
    dexpand[...] = (tn(low, frames[...]) * EXPAND).astype(bf16).reshape(OWNERS, 24, D)
    dproject[...] = (tn(mid[...], grads[...]) * PROJECT).astype(bf16).reshape(OWNERS, 24, D)


def conv_backward(frames, grads, project, taps, pre, deep):
    steps = project.shape[0] // OWNERS
    channels = steps * WIDTH
    whole = pl.BlockSpec((PIX * PAIR, D), lambda i: (0, 0))
    weights = pl.BlockSpec((OWNERS, 24, D), lambda i: (i, 0, 0))
    maps = pl.BlockSpec((PIX, PAIR, WIDTH), lambda i: (0, 0, i))
    small = pl.BlockSpec((9, WIDTH), lambda i: (0, i))
    owned = jax.ShapeDtypeStruct((OWNERS * steps, 24, D), bf16)
    return pl.pallas_call(
        backward_kernel,
        grid=(steps,),
        out_shape=[owned, owned, jax.ShapeDtypeStruct((9, channels), f32)],
        in_specs=[whole, whole, weights, small, maps, maps],
        out_specs=[weights, weights, small],
        scratch_shapes=[
            pltpu.VMEM((MAP + 2, MAP, PAIR, WIDTH), f32),
            pltpu.VMEM((PIX * PAIR, WIDTH), bf16),
            pltpu.VMEM((PIX, PAIR, WIDTH), f32),
            pltpu.VMEM((9, 8, WIDTH), f32),
        ],
        compiler_params=pltpu.CompilerParams(vmem_limit_bytes=VMEM_BYTES),
    )(frames, grads, project, taps, pre, deep)

INSTR, DIMS, BINS, NTOK, FRAMES, HEADS, HD = 744, 11, 256, 8, 6, 8, 64
TABLE = INSTR + 2
ROWS = PAIR * NTOK
SMALL_AT = TABLE - D
LN_EPS = 1e-06
OUT_MULT = 2.0
HIGH = lax.Precision.HIGHEST
FILM = 16.0 / math.sqrt(D)
LEARN = 4.0 / math.sqrt(D)


def norm_fwd(x, gain):
    centre = x - jnp.mean(x, -1, keepdims=True)
    inverse = lax.rsqrt(jnp.mean(centre * centre, -1, keepdims=True) + LN_EPS)
    normed = centre * inverse
    return normed * (1.0 + gain), normed, inverse


def norm_back(normed, inverse, gain, grad_out):
    dnormed = grad_out * (1.0 + gain)
    grad_in = inverse * (
        dnormed
        - jnp.mean(dnormed, -1, keepdims=True)
        - normed * jnp.mean(dnormed * normed, -1, keepdims=True)
    )
    return grad_in, jnp.sum(grad_out * normed, 0, keepdims=True)


def gelu_parts(u):
    c = math.sqrt(2.0 / math.pi)
    square = u * u
    t = jnp.tanh(c * u * (1.0 + 0.044715 * square))
    half = 0.5 * (1.0 + t)
    return u * half, half + 0.5 * u * (1.0 - t * t) * c * (1.0 + 3.0 * 0.044715 * square)


def iota(shape, axis):
    return lax.broadcasted_iota(jnp.int32, shape, axis)


def shifted(v, places):
    tiles = [pltpu.roll(v[:, i : i + 128], (128 - places) % 128, 1) for i in range(0, v.shape[1], 128)]
    return jnp.concatenate(tiles, axis=1)


def only(v, first):
    place = iota(v.shape, 1) & 15
    return jnp.where((place >= first) & (place < first + 4), v, 0.0)


def place_of_feature(start, rows):
    d = iota((rows, D), 1)
    owner = d >> 2
    row = (owner & 1) * 1024 + (owner >> 1) * 16 + 12 + (d & 3)
    return (iota((rows, D), 0) + start == row).astype(bf16)


def middle_kernel(
    core_ref, own, other, cells, misc, one, two, instr, cam, bins, mask,
    dcells, dmisc, done_one, done_two, stats,
    y, logit, att, qkv, prob, ctx, up, hid, acc, dlog, lowgrad,
):
    core = core_ref[0]
    lanes = iota((PAIR, 128), 1)

    def chosen(tile):
        at = lanes + 128 * tile
        return ((at == instr[...]) | (at == INSTR + cam[0] + cam[1])).astype(f32)

    choose_lo = jnp.concatenate([chosen(i) for i in range(4)], axis=1).astype(bf16)
    choose_hi = jnp.concatenate([chosen(i) for i in range(4, 8)], axis=1).astype(bf16)
    flat = misc[...]
    cvec = only(shifted(nt(choose_lo, flat), 8) + shifted(nt(choose_hi, flat), 12), 0).astype(bf16).astype(f32)
    cvec_4 = shifted(cvec, 124)
    cvec_low, cvec_4_low = cvec.astype(bf16), cvec_4.astype(bf16)
    gamma = nn(cvec_low, flat) * FILM
    beta = nn(cvec_4_low, flat) * FILM
    scale = 1.0 + gamma
    pick = (iota((16, D), 1) == SMALL_AT + iota((16, D), 0)).astype(bf16)
    small = nn(nt(pick, flat).astype(bf16), place_of_feature(0, 2048))
    gains = [small[i : i + 1] for i in range(3)]
    learner = jnp.concatenate([small[3:11], jnp.zeros((120, D), f32)], axis=0)

    def feature(cell, _):
        rows = pl.ds(pl.multiple_of(cell * PAIR, PAIR), PAIR)
        v = cells[rows, :].astype(f32) + (own[rows, :] + other[rows, :]) * scale + beta
        y[rows, :] = v
        return 0

    lax.fori_loop(0, PIX, feature, 0)
    logit[...] = (
        lax.dot_general(y[...], learner, (((1,), (1,)), ((), ())), precision=HIGH, preferred_element_type=f32) * LEARN
    )

    def softmax_over_cells(v):
        v = v.reshape(PIX, PAIR, 128)
        e = jnp.exp(v - jnp.max(v, 0, keepdims=True))
        return e / jnp.sum(e, 0, keepdims=True)

    att[...] = softmax_over_cells(logit[...]).reshape(PIX * PAIR, 128)
    acc[...] = jnp.zeros_like(acc)
    for half in range(2):
        columns = slice(256 * half, 256 * half + 256)

        zero = jnp.zeros((PAIR, 256), f32)
        for t0 in range(0, NTOK, 4):

            def gather_some(cell, totals, t0=t0, columns=columns):
                rows = pl.ds(pl.multiple_of(cell * PAIR, PAIR), PAIR)
                a, v = att[rows, :], y[rows, columns]
                return tuple(t + a[:, t0 + i : t0 + i + 1] * v for i, t in enumerate(totals))

            totals = lax.fori_loop(0, PIX, gather_some, (zero,) * 4)
            for i in range(4):
                acc[(t0 + i) * PAIR : (t0 + i + 1) * PAIR, columns] = totals[i]
    tok = acc[...].astype(bf16).astype(f32)

    h1, normed1, inverse1 = norm_fwd(tok, gains[0])
    h1_low = h1.astype(bf16)
    row_q, row_k = iota((ROWS, ROWS), 0), iota((ROWS, ROWS), 1)
    image_q, image_k = lax.rem(row_q, PAIR), lax.rem(row_k, PAIR)
    order_q = image_q * NTOK + lax.div(row_q, PAIR)
    order_k = image_k * NTOK + lax.div(row_k, PAIR)
    seen = (lax.div(image_q, FRAMES) == lax.div(image_k, FRAMES)) & (order_k <= order_q)
    root = HD**-0.5
    acc[...] = jnp.zeros_like(acc)

    def attend(m, _):
        p = nn(h1_low, one[m, :, 0:384]).astype(bf16)
        qkv[m] = p
        outs = []
        for head in range(2):
            q, k, v = (p[:, 128 * j + 64 * head : 128 * j + 64 * head + 64] for j in range(3))
            s = jnp.where(seen, nt(q, k) * root, -1e30)
            e = jnp.exp(s - jnp.max(s, -1, keepdims=True))
            w = e / jnp.sum(e, -1, keepdims=True)
            prob[m, head] = w
            outs.append(nn(w.astype(bf16), v))
        o = jnp.concatenate(outs, axis=1).astype(bf16)
        ctx[m] = o
        acc[...] += nt(o, one[m, :, 384:512])
        return 0

    lax.fori_loop(0, 4, attend, 0)
    x1 = tok + OUT_MULT * acc[...]
    h2, normed2, inverse2 = norm_fwd(x1, gains[1])
    h2_low = h2.astype(bf16)
    acc[...] = x1

    def feed(m, _):
        u = nn(h2_low, two[m, :, 0:512])
        up[m] = u
        low = gelu_parts(u)[0].astype(bf16)
        hid[m] = low
        acc[...] += nt(low, two[m, :, 512:1024])
        return 0

    lax.fori_loop(0, 4, feed, 0)
    x2 = acc[...]
    normed_out, normed3, inverse3 = norm_fwd(x2, gains[2])
    pooled = (jnp.sum(normed_out.reshape(NTOK, PAIR, D), axis=0) * (1.0 / NTOK)).astype(bf16)

    low_half = lanes < 64
    scores = [nn(pooled, one[m, :, 512:1280]) for m in range(4)]
    weight = mask[...]
    loss = jnp.zeros((PAIR, 128), f32)
    for u in range(6):
        tiles = [s[:, 128 * u : 128 * u + 128] for s in scores]
        top = jnp.maximum(jnp.maximum(tiles[0], tiles[1]), jnp.maximum(tiles[2], tiles[3]))
        left = jnp.max(jnp.where(low_half, top, -jnp.inf), -1, keepdims=True)
        right = jnp.max(jnp.where(low_half, -jnp.inf, top), -1, keepdims=True)
        top = jnp.where(low_half, left, right)
        total = sum(jnp.exp(t - top) for t in tiles)
        left = jnp.sum(jnp.where(low_half, total, 0.0), -1, keepdims=True)
        right = jnp.sum(jnp.where(low_half, 0.0, total), -1, keepdims=True)
        lse = top + jnp.log(jnp.where(low_half, left, right))
        label = jnp.where(low_half, bins[:, 2 * u : 2 * u + 1], bins[:, 2 * u + 1 : 2 * u + 2])
        real = low_half | (2 * u + 1 < DIMS)
        target = jnp.zeros((PAIR, 128), f32)
        for m, t in enumerate(tiles):
            hit = label == (lanes & 63) + 64 * m
            target = target + jnp.where(hit, t, 0.0)
            slope = weight * (jnp.exp(t - lse) - hit.astype(f32))
            dlog[m, :, 128 * u : 128 * u + 128] = jnp.where(real, slope, 0.0).astype(bf16)
        counted = real & ((lanes & 63) == 0)
        loss = loss + weight * (jnp.where(counted, lse, 0.0) - target)
    stats[...] = jnp.zeros_like(stats)
    stats[0:8] = loss[0:8] + loss[8:16] + loss[16:24]
    counts = jnp.where(lanes == 0, weight, 0.0)
    stats[8:16] = counts[0:8] + counts[8:16] + counts[16:24]
    dpooled = jnp.zeros((PAIR, D), f32)
    for m in range(4):
        dpooled = dpooled + nt(dlog[m], one[m, :, 512:1280])
    dnormed = jnp.broadcast_to(dpooled * (1.0 / NTOK), (NTOK, PAIR, D)).reshape(ROWS, D)
    dx2, dgain2 = norm_back(normed3, inverse3, gains[2], dnormed)
    dbranch = dx2.astype(bf16)
    acc[...] = jnp.zeros_like(acc)

    def feed_back(m, _):
        slope = gelu_parts(up[m])[1]
        dup = (nn(dbranch, two[m, :, 512:1024]) * slope).astype(bf16)
        lowgrad[m] = dup
        acc[...] += nt(dup, two[m, :, 0:512])
        return 0

    lax.fori_loop(0, 4, feed_back, 0)
    dx1_norm, dgain1 = norm_back(normed2, inverse2, gains[1], acc[...])
    dx1 = dx2 + dx1_norm
    dattn = dx1.astype(bf16)

    def feed_weights(h, _):
        m = 2 * h + core
        done_one[h, :, 512:1280] = tn(pooled, dlog[m]).astype(bf16)
        done_two[h, :, 0:512] = tn(h2_low, lowgrad[m]).astype(bf16)
        done_two[h, :, 512:1024] = tn(dbranch, hid[m]).astype(bf16)
        done_one[h, :, 384:512] = (tn(dattn, ctx[m]) * OUT_MULT).astype(bf16)
        return 0

    lax.fori_loop(0, 2, feed_weights, 0)
    acc[...] = jnp.zeros_like(acc)

    def attend_back(m, _):
        do = (nn(dattn, one[m, :, 384:512]) * OUT_MULT).astype(bf16)
        p = qkv[m]
        dq, dk, dv = [], [], []
        for head in range(2):
            q, k, v = (p[:, 128 * j + 64 * head : 128 * j + 64 * head + 64] for j in range(3))
            w = prob[m, head]
            d = do[:, 64 * head : 64 * head + 64]
            dp = nt(d, v)
            dv.append(tn(w.astype(bf16), d))
            ds = (w * (dp - jnp.sum(w * dp, -1, keepdims=True))).astype(bf16)
            dq.append(nn(ds, k) * root)
            dk.append(tn(ds, q) * root)
        g = jnp.concatenate([*dq, *dk, *dv], axis=1).astype(bf16)
        lowgrad[m, :, 0:384] = g
        acc[...] += nt(g, one[m, :, 0:384])
        return 0

    lax.fori_loop(0, 4, attend_back, 0)

    def attend_weights(h, _):
        done_one[h, :, 0:384] = tn(h1_low, lowgrad[2 * h + core, :, 0:384]).astype(bf16)
        return 0

    lax.fori_loop(0, 2, attend_weights, 0)
    dtok_norm, dgain0 = norm_back(normed1, inverse1, gains[0], acc[...])
    acc[...] = dx1 + dtok_norm

    def slope_of(cell, _):
        rows = pl.ds(pl.multiple_of(cell * PAIR, PAIR), PAIR)
        v = y[rows, :]
        found = jnp.zeros((PAIR, 128), f32)
        for t in range(NTOK):
            s = jnp.sum(v * acc[t * PAIR : (t + 1) * PAIR, :], -1, keepdims=True)
            found = jnp.where(lanes == t, s, found)
        logit[rows, :] = found
        return 0

    lax.fori_loop(0, PIX, slope_of, 0)
    a = att[...].reshape(PIX, PAIR, 128)
    da = logit[...].reshape(PIX, PAIR, 128)
    logit[...] = (a * (da - jnp.sum(a * da, 0, keepdims=True)) * LEARN).reshape(PIX * PAIR, 128)
    dlearner = lax.dot_general(logit[...], y[...], (((0,), (0,)), ((), ())), precision=HIGH, preferred_element_type=f32)

    def spread(cell, sums):
        rows = pl.ds(pl.multiple_of(cell * PAIR, PAIR), PAIR)
        a, dl = att[rows, :], logit[rows, :]
        dy = jnp.zeros((PAIR, D), f32)
        for t in range(NTOK):
            dy = dy + a[:, t : t + 1] * acc[t * PAIR : (t + 1) * PAIR, :] + dl[:, t : t + 1] * learner[t : t + 1]
        dcells[rows, :] = (dy * scale).astype(bf16)
        return sums[0] + dy * (own[rows, :] + other[rows, :]), sums[1] + dy

    zero = jnp.zeros((PAIR, D), f32)
    dgamma, dbeta = lax.fori_loop(0, PIX, spread, (zero, zero))
    dgamma, dbeta = dgamma.astype(bf16), dbeta.astype(bf16)
    dcvec = only(nt(dgamma, flat) + shifted(nt(dbeta, flat), 4), 0) * FILM
    high = dcvec.astype(bf16).astype(f32)
    rest = dcvec - high
    dsmall = jnp.concatenate([dgain0, dgain1, dgain2, dlearner[0:8], jnp.zeros((5, D), f32)], axis=0).astype(bf16)
    mine = pl.ds(pl.multiple_of(core * 1024, 1024), 1024)
    lhs = jnp.concatenate(
        [cvec, cvec_4, shifted(high, 120), shifted(rest, 120), shifted(high, 116), shifted(rest, 116)], axis=0
    )
    lhs = jnp.where(core == 0, lhs[:, 0:1024], lhs[:, 1024:2048])
    lhs = jnp.concatenate([lhs, nt(dsmall, place_of_feature(core * 1024, 1024))], axis=0).astype(bf16)
    rhs = jnp.concatenate([dgamma, dbeta, choose_lo, choose_lo, choose_hi, choose_hi, pick], axis=0)
    result = tn(lhs, rhs)
    film_rows = (iota((1024, D), 0) & 15) < 8
    dmisc[...] = jnp.where(film_rows, result * FILM, result).astype(bf16)


def middle(core, own, other, cells, misc, one, two, instr, cam, bins, mask):
    vmem = pl.BlockSpec(memory_space=pltpu.VMEM)
    return pl.pallas_call(
        middle_kernel,
        out_shape=[
            jax.ShapeDtypeStruct((PIX * PAIR, D), bf16),
            jax.ShapeDtypeStruct((1024, D), bf16),
            jax.ShapeDtypeStruct((2, D, 1280), bf16),
            jax.ShapeDtypeStruct((2, D, 1024), bf16),
            jax.ShapeDtypeStruct((16, 128), f32),
        ],
        in_specs=[pl.BlockSpec(memory_space=pltpu.SMEM)] + [vmem] * 10,
        out_specs=[vmem] * 5,
        scratch_shapes=[
            pltpu.VMEM((PIX * PAIR, D), f32),
            pltpu.VMEM((PIX * PAIR, 128), f32),
            pltpu.VMEM((PIX * PAIR, 128), f32),
            pltpu.VMEM((4, ROWS, 384), bf16),
            pltpu.VMEM((4, 2, ROWS, ROWS), f32),
            pltpu.VMEM((4, ROWS, 128), bf16),
            pltpu.VMEM((4, ROWS, 512), f32),
            pltpu.VMEM((4, ROWS, 512), bf16),
            pltpu.VMEM((ROWS, D), f32),
            pltpu.VMEM((4, PAIR, 768), bf16),
            pltpu.VMEM((4, ROWS, 512), bf16),
        ],
        compiler_params=pltpu.CompilerParams(vmem_limit_bytes=VMEM_BYTES),
    )(core, own, other, cells, misc, one, two, instr, cam, bins, mask)

TAIL = TABLE + 11
IMAGES = 12
MP = ("mp_0", "mp_1")
DP_MP = NAMES
DP = ("dp_0", "dp_1", "dp_2")
CLIP_NORM = 0.02
BETA_ONE = 0.9
BETA_TWO = 0.999
ADAM_EPS = 1e-08
DECAY = 0.01
RATES = (0.1, 0.1, 0.2, 0.05, 0.05, 0.2)


def adam(master, first, second, grad, t, rate):
    first_new = BETA_ONE * first + (1.0 - BETA_ONE) * grad
    second_new = BETA_TWO * second + (1.0 - BETA_TWO) * grad * grad
    m_hat = first_new / (1.0 - BETA_ONE**t)
    v_hat = second_new / (1.0 - BETA_TWO**t)
    master_new = master - rate * (m_hat / (jnp.sqrt(v_hat) + ADAM_EPS) + DECAY * master)
    return [master_new, first_new, second_new]


def pack_misc(film, table, small):
    tail = jnp.concatenate([table, small], axis=1)
    tail = jnp.pad(tail, ((0, 0), (0, 2 * D - tail.shape[1])))
    return jnp.concatenate([film[:, :D], film[:, D:], tail[:, :D], tail[:, D:]], axis=0)


def unpack_misc(misc):
    film = jnp.concatenate([misc[0:4], misc[4:8]], axis=1)
    tail = jnp.concatenate([misc[8:12], misc[12:16]], axis=1)
    return film, tail[:, :TABLE], tail[:, TABLE:TAIL]


def pack_attn_head(attn, head):
    both = jnp.concatenate([*attn, head], axis=-1)
    return jnp.pad(both, [(0, 0)] * (both.ndim - 1) + [(0, 1280 - both.shape[-1])])


def swap_cores(value):
    return lax.ppermute(value, "mp_1", [(0, 1), (1, 0)])


def per_device(
    frames, camera_ids, instruction_ids, action_bins, final_mask, step_count,
    conv_w, conv_m1, conv_m2, cond_w, cond_m1, cond_m2, small_w, small_m1, small_m2,
    attn_w, attn_m1, attn_m2, mlp_w, mlp_m1, mlp_m2, head_w, head_m1, head_m2,
):
    core, high = lax.axis_index("mp_1"), lax.axis_index("mp_0")
    conv_t = conv_w.T.astype(bf16)
    cond_t = cond_w.T.astype(bf16)
    attn_l = attn_w.astype(bf16)
    shards = (
        conv_t[:, :D],
        conv_t[:, D : 2 * D],
        jnp.pad(conv_w[2 * D :].astype(bf16), ((0, 7), (0, 104))),
        pack_misc(cond_t[:, : 2 * D], cond_t[:, 2 * D :], small_w.T.astype(bf16)),
        pack_attn_head([attn_l[j] for j in range(4)], head_w.astype(bf16).reshape(16, DIMS * 64)),
        jnp.moveaxis(mlp_w.astype(bf16), 0, 1).reshape(16, 1024),
    )
    image = jnp.arange(PAIR)
    cam = jnp.where(image // IMAGES == core, jnp.tile(camera_ids, 2), 0)
    cam = jnp.broadcast_to(cam[:, None], (PAIR, 128))
    frames2, cam2, expand, project, taps_all, misc_all, one_all, two_all = gather_all(
        (frames, cam), shards, GATHER, 1
    )
    expand = expand.reshape(64, 24, D)
    project = project.reshape(64, 24, D)
    taps = taps_all.reshape(64, 16, 128)[:, :9, :24].astype(f32) * (8.0 / 3.0)
    taps = taps.transpose(1, 0, 2).reshape(9, 1536)

    cells = frames2.transpose(2, 0, 1, 3).reshape(PIX * PAIR, D)
    pre, deep, part = conv_forward(cells, expand, project, taps)
    other = swap_cores(part)
    instr = jnp.repeat(lax.dynamic_slice_in_dim(instruction_ids, high * 4, 4), FRAMES)
    bins = jnp.pad(
        lax.dynamic_slice_in_dim(action_bins, high * PAIR, PAIR), ((0, 0), (0, 128 - DIMS)), constant_values=-1
    )
    mask = lax.dynamic_slice_in_dim(final_mask, high * PAIR, PAIR).astype(f32)
    dcells, dmisc, done_one, done_two, stats = middle(
        core[None],
        part,
        other,
        cells,
        misc_all.reshape(2048, D),
        one_all.reshape(4, D, 1280),
        two_all.reshape(4, D, 1024),
        jnp.broadcast_to(instr[:, None], (PAIR, 128)),
        cam2,
        bins,
        jnp.broadcast_to(mask[:, None], (PAIR, 128)),
    )
    dexpand, dproject, dtaps = conv_backward(cells, dcells, project, taps, pre, deep)
    dtaps = dtaps.astype(bf16).reshape(9, 64, 24).transpose(1, 0, 2)
    dtaps = jnp.pad(dtaps, ((0, 0), (0, 7), (0, 104)))
    parts = [
        g.reshape(*lead(dims), *s.shape)
        for g, s, (dims, _) in zip((dexpand, dproject, dtaps, dmisc, done_one, done_two), shards, SCATTER)
    ]
    totals, gexpand, gproject, gtaps, gmisc, gone, gtwo = scatter_all(stats, parts, SCATTER, 2)
    gfilm, gtable, gsmall = unpack_misc(gmisc)
    grads = (
        jnp.concatenate([gexpand.T, gproject.T, gtaps[:9, :24]], 0),
        jnp.concatenate([gfilm, gtable], 1).T,
        gsmall.T,
        jnp.stack([gone[:, 128 * j : 128 * j + 128] for j in range(4)]),
        jnp.moveaxis(gtwo.reshape(16, 2, 512), 1, 0),
        gone[:, 512 : 512 + DIMS * 64].reshape(16, DIMS, 64),
    )
    loss_sum, count, square = (jnp.sum(totals[8 * i : 8 * i + 8]) for i in range(3))
    loss_sum, count = 0.5 * loss_sum, 0.5 * count
    norm = jnp.sqrt(square) / count
    factor = jnp.minimum(1.0, CLIP_NORM / norm) / count
    steps_done = step_count[0].astype(f32)
    masters = (conv_w, cond_w, small_w, attn_w, mlp_w, head_w)
    firsts = (conv_m1, cond_m1, small_m1, attn_m1, mlp_m1, head_m1)
    seconds = (conv_m2, cond_m2, small_m2, attn_m2, mlp_m2, head_m2)
    outs = [loss_sum / count, norm]
    for idx in range(6):
        outs.extend(adam(masters[idx], firsts[idx], seconds[idx], grads[idx] * factor, steps_done, RATES[idx]))
    return tuple(outs)


def solution(mesh):
    torus = Mesh(mesh.devices.reshape(2, 4, 4, 2, 2), NAMES)
    weights = (
        *[P(None, DP_MP)] * 9,
        *[P(None, DP, MP)] * 6,
        *[P(DP, None, MP)] * 3,
    )
    data = (P(DP_MP, None, None), P(DP_MP), P(DP), P(DP, None), P(DP), P())
    return jax.shard_map(
        per_device, mesh=torus, in_specs=(*data, *weights), out_specs=(P(), P(), *weights), check_vma=False
    )
```

```python
import functools
import math

import jax
import jax.numpy as jnp
from jax import lax
from jax.experimental import pallas as pl
from jax.experimental.pallas import tpu as pltpu
from jax.sharding import Mesh
from jax.sharding import PartitionSpec as P

f32 = jnp.float32
bf16 = jnp.bfloat16
NAMES = ("dp_0", "dp_1", "dp_2", "mp_0", "mp_1")
SIZES = {"l": 2, "z": 4, "x": 4, "h": 2, "c": 2}
RING = 4
MESH_ID = pl.DeviceIdType.MESH
ANY = pl.BlockSpec(memory_space=pl.ANY)
INVMEM = pl.BlockSpec(memory_space=pltpu.VMEM)


def here():
    low, z, x, high, core = (lax.axis_index(n) for n in NAMES)
    return {"x": x, "y": high * 2 + low, "z": z, "c": core}


def ring(at, step):
    return lax.rem(at + step + RING, RING)


def device_of(axis, at):
    if axis == "y":
        return {"dp_0": lax.rem(at, 2), "mp_0": at // 2}
    return {{"x": "dp_2", "z": "dp_1", "c": "mp_1"}[axis]: at}


def extents(dims, at):
    found = []
    for d in dims:
        if d in at:
            v = at[d]
        elif d == "l" and "y" in at:
            v = lax.rem(at["y"], 2)
        elif d == "h" and "y" in at:
            v = at["y"] // 2
        else:
            v = (0, SIZES[d])
        found.append(v if isinstance(v, tuple) else (v, None))
    return found


def spot(dims, at):
    return tuple(start if size is None else pl.ds(start, size) for start, size in extents(dims, at))


def free_sizes(dims, at):
    return tuple(size for _, size in extents(dims, at) if size is not None)


def half(axis, side):
    return {"h": side} if axis == "y" else {axis: (2 * side, 2)}


def without(dims, axis):
    return tuple(d for d in dims if d not in ("lh" if axis == "y" else axis))


def lead(dims):
    return tuple(SIZES[d] for d in dims)


def greet(me):
    barrier = pltpu.get_barrier_semaphore()
    for axis in "xyz":
        for k in range(1, RING):
            pl.semaphore_signal(barrier, inc=1, device_id=device_of(axis, ring(me[axis], k)), device_id_type=MESH_ID)
    pl.semaphore_signal(barrier, inc=1, device_id=device_of("c", 1 - me["c"]), device_id_type=MESH_ID)
    pl.semaphore_wait(barrier, 10)


def remote(src, dst, send, recv, axis, at):
    copy = pltpu.make_async_remote_copy(
        src_ref=src, dst_ref=dst, send_sem=send, recv_sem=recv, device_id=device_of(axis, at), device_id_type=MESH_ID
    )
    copy.start()
    return copy


class Gather:
    def __init__(self, me, dims, order, shard, out, send, recv, fsend, frecv, local):
        self.me, self.dims, self.order, self.shard, self.out = me, dims, order, shard, out
        self.send, self.recv, self.fsend, self.frecv, self.local = send, recv, fsend, frecv, local
        self.forwards = []

    def region(self, phase, step=0, part=None):
        at = {a: self.me[a] for a in self.order[phase:]}
        at[self.order[phase]] = ring(self.me[self.order[phase]], step)
        if "c" in self.dims:
            at["c"] = self.me["c"]
        if part is not None:
            at.update(half(self.order[0], part))
        return self.out.at[spot(self.dims, at)]

    def push(self, phase, slot, where, step):
        axis = self.order[phase]
        src = self.shard if phase == 0 else where
        return remote(src, where, self.send.at[phase, slot], self.recv.at[phase, slot], axis, ring(self.me[axis], step))

    def forward(self, number, where):
        if "c" in self.dims:
            self.forwards.append(
                remote(where, where, self.fsend.at[number], self.frecv.at[number], "c", 1 - self.me["c"])
            )

    def begin(self):
        self.kept = pltpu.make_async_copy(self.shard, self.region(0), self.local)
        self.kept.start()
        self.launch(0)

    def launch(self, phase):
        where = self.region(phase)
        self.going = [self.push(phase, 0, where, 1), self.push(phase, 1, where, -1)]
        if phase == 0:
            self.going.append(self.push(0, 2, where, 2))

    def relay(self, phase):
        for slot, step in ((0, 1), (1, -1)):
            self.going[slot].wait()
            if phase > 0:
                self.going.append(self.push(phase, 2 + slot, self.region(phase, -step, slot), step))
                self.forward(3 * phase - 2 + slot, self.region(phase, -step))

    def finish(self, phase):
        for copy in self.going[2:]:
            copy.wait()
        if phase == 0:
            self.kept.wait()
            if "c" in self.dims:
                at = {a: self.me[a] for a in (*self.order[1:], "c")}
                self.forward(0, self.out.at[spot(self.dims, at)])
        else:
            self.forward(3 * phase, self.region(phase, 2))
        if phase < 2:
            self.launch(phase + 1)

    def end(self):
        for copy in self.forwards:
            copy.wait()


def add_into(full, dims, at, others):
    found = extents(dims, at)
    sizes = free_sizes(dims, at)

    def one(i, _):
        index, place = [], []
        for start, size in reversed(found):
            if size is None:
                index.append(start)
            else:
                index.append(start + lax.rem(i, size))
                place.append(lax.rem(i, size))
                i = i // size
        index, place = tuple(reversed(index)), tuple(reversed(place))
        total = full[index].astype(f32)
        for o in others:
            total = total + o[place].astype(f32)
        full[index] = total.astype(full.dtype)
        return 0

    lax.fori_loop(0, math.prod(sizes), one, 0)


def folded(v):
    total = None
    for r in range(0, v.shape[0], 8):
        for c in range(0, v.shape[1], 128):
            part = v[r : r + 8, c : c + 128]
            total = part if total is None else total + part
    return total


class Scatter:
    def __init__(self, me, dims, order, part, full, boxes, send, recv, local):
        self.me, self.dims, self.order, self.part, self.full, self.boxes = me, dims, order, part, full, boxes
        self.send, self.recv, self.local = send, recv, local

    def at(self, phase, step, side=None):
        at = {a: self.me[a] for a in self.order[:phase]}
        axis = self.order[phase]
        at[axis] = ring(self.me[axis], step)
        if side is not None:
            at.update(half(self.order[phase + 1], side))
        return at

    def push(self, phase, slot, src, step):
        axis = self.order[phase]
        return remote(
            src, self.boxes[phase][slot], self.send.at[phase, slot], self.recv.at[phase, slot], axis, ring(self.me[axis], step)
        )

    def begin(self):
        self.kept = pltpu.make_async_copy(self.part, self.full, self.local)
        self.kept.start()
        self.launch(0)

    def launch(self, phase):
        src = self.part if phase == 0 else self.full
        if phase < 2:
            self.going = [
                self.push(phase, side, src.at[spot(self.dims, self.at(phase, 2, side))], 1 - 2 * side) for side in range(2)
            ]
        else:
            self.going = [
                self.push(phase, slot, src.at[spot(self.dims, self.at(phase, step))], step)
                for slot, step in ((0, 2), (2, 1), (3, -1))
            ]

    def relay(self, phase):
        if phase == 0:
            self.kept.wait()
        if phase == 2:
            return
        for side, step in ((0, 1), (1, -1)):
            self.going[side].wait()
            add_into(self.full, self.dims, self.at(phase, step, side), [self.boxes[phase][side]])
            self.going.append(self.push(phase, 2 + side, self.full.at[spot(self.dims, self.at(phase, step))], step))

    def finish(self, phase):
        if phase < 2:
            for copy in self.going[2:]:
                copy.wait()
            add_into(self.full, self.dims, self.at(phase, 0), self.boxes[phase][2:4])
            self.launch(phase + 1)
            return None
        for copy in self.going:
            copy.wait()
        total = self.full[spot(self.dims, self.at(2, 0))].astype(f32)
        for slot in (0, 2, 3):
            total = total + self.boxes[2][slot][...].astype(f32)
        return total

    @staticmethod
    def scratch(dims, order, slab, dtype):
        shapes = [(*lead(dims), *slab)]
        rest = dims
        for phase, axis in enumerate(order):
            rest = without(rest, axis)
            if phase < 2:
                small = free_sizes(rest, half(order[phase + 1], 0))
            else:
                small = ()
            shapes += [(*small, *slab)] * 2 + [(*lead(rest), *slab)] * 2
        return [pltpu.VMEM(s, dtype) for s in shapes]


OWNED = ("x", "l", "z", "h")
GATHER = (
    (OWNED, ("z", "y", "x")),
    (OWNED, ("y", "z", "x")),
    (OWNED, ("z", "y", "x")),
    (("c", "l", "z", "x", "h"), ("x", "y", "z")),
    (("h", "c", "l", "z", "x"), ("x", "z", "y")),
    (("h", "c", "l", "z", "x"), ("x", "y", "z")),
)
SCATTER = (
    (OWNED, ("z", "y", "x")),
    (OWNED, ("y", "z", "x")),
    (OWNED, ("z", "y", "x")),
    (("l", "z", "x", "h"), ("z", "y", "x")),
    (("h", "l", "z", "x"), ("x", "y", "z")),
    (("h", "l", "z", "x"), ("y", "x", "z")),
)


D, EXP, MAP, PIX = 512, 3072, 9, 81
PAIR = 24
WIDTH = 384
OWNERS = WIDTH // 24
CHUNK = 3
SPAN = CHUNK * MAP * PAIR
EXPAND = 8.0 / math.sqrt(D)
PROJECT = 8.0 / math.sqrt(EXP)
VMEM_BYTES = 60 * 2**20


def sigmoid(v):
    return 0.5 + 0.5 * jnp.tanh(0.5 * v)


def nt(left, right):
    return lax.dot_general(left, right, (((1,), (1,)), ((), ())), preferred_element_type=f32)


def nn(left, right):
    return lax.dot_general(left, right, (((1,), (0,)), ((), ())), preferred_element_type=f32)


def tn(left, right):
    return lax.dot_general(left, right, (((0,), (0,)), ((), ())), preferred_element_type=f32)


def clear_borders(padded):
    zero = jnp.zeros((MAP, PAIR, WIDTH), f32)
    padded[0] = zero
    padded[MAP + 1] = zero


def each_block(body):
    def one(row, _):
        for lane in range(WIDTH // 128):
            for group in range(PAIR // 8):
                body(row, slice(8 * group, 8 * group + 8), slice(128 * lane, 128 * lane + 128))
        return 0

    lax.fori_loop(0, MAP, one, 0)


INSTR, DIMS, BINS, NTOK, FRAMES, HEADS, HD = 744, 11, 256, 8, 6, 8, 64
TABLE = INSTR + 2
ROWS = PAIR * NTOK
SMALL_AT = TABLE - D
LN_EPS = 1e-06
OUT_MULT = 2.0
HIGH = lax.Precision.HIGHEST
FILM = 16.0 / math.sqrt(D)
LEARN = 4.0 / math.sqrt(D)


def norm_fwd(x, gain):
    centre = x - jnp.mean(x, -1, keepdims=True)
    inverse = lax.rsqrt(jnp.mean(centre * centre, -1, keepdims=True) + LN_EPS)
    normed = centre * inverse
    return normed * (1.0 + gain), normed, inverse


def norm_back(normed, inverse, gain, grad_out):
    dnormed = grad_out * (1.0 + gain)
    grad_in = inverse * (
        dnormed
        - jnp.mean(dnormed, -1, keepdims=True)
        - normed * jnp.mean(dnormed * normed, -1, keepdims=True)
    )
    return grad_in, jnp.sum(grad_out * normed, 0, keepdims=True)


def gelu_parts(u):
    c = math.sqrt(2.0 / math.pi)
    square = u * u
    t = jnp.tanh(c * u * (1.0 + 0.044715 * square))
    half = 0.5 * (1.0 + t)
    return u * half, half + 0.5 * u * (1.0 - t * t) * c * (1.0 + 3.0 * 0.044715 * square)


def iota(shape, axis):
    return lax.broadcasted_iota(jnp.int32, shape, axis)


def shifted(v, places):
    tiles = [pltpu.roll(v[:, i : i + 128], (128 - places) % 128, 1) for i in range(0, v.shape[1], 128)]
    return jnp.concatenate(tiles, axis=1)


def only(v, first):
    place = iota(v.shape, 1) & 15
    return jnp.where((place >= first) & (place < first + 4), v, 0.0)


def place_of_feature(start, rows):
    d = iota((rows, D), 1)
    owner = d >> 2
    row = (owner & 1) * 1024 + (owner >> 1) * 16 + 12 + (d & 3)
    return (iota((rows, D), 0) + start == row).astype(bf16)


def middle_kernel(
    core_ref, part, cells, misc, one, two, instr, cam, bins, mask,
    dcells, dmisc, done_one, done_two, stats,
    y, logit, att, qkv, prob, ctx, up, hid, acc, dlog, lowgrad,
):
    core = core_ref[0]
    lanes = iota((PAIR, 128), 1)

    def chosen(tile):
        at = lanes + 128 * tile
        return ((at == instr[...]) | (at == INSTR + cam[0] + cam[1])).astype(f32)

    choose_lo = jnp.concatenate([chosen(i) for i in range(4)], axis=1).astype(bf16)
    choose_hi = jnp.concatenate([chosen(i) for i in range(4, 8)], axis=1).astype(bf16)
    flat = misc[...]
    cvec = only(shifted(nt(choose_lo, flat), 8) + shifted(nt(choose_hi, flat), 12), 0).astype(bf16).astype(f32)
    cvec_4 = shifted(cvec, 124)
    cvec_low, cvec_4_low = cvec.astype(bf16), cvec_4.astype(bf16)
    gamma = nn(cvec_low, flat) * FILM
    beta = nn(cvec_4_low, flat) * FILM
    scale = 1.0 + gamma
    pick = (iota((16, D), 1) == SMALL_AT + iota((16, D), 0)).astype(bf16)
    small = nn(nt(pick, flat).astype(bf16), place_of_feature(0, 2048))
    gains = [small[i : i + 1] for i in range(3)]
    learner = jnp.concatenate([small[3:11], jnp.zeros((120, D), f32)], axis=0)

    def feature(cell, _):
        rows = pl.ds(pl.multiple_of(cell * PAIR, PAIR), PAIR)
        v = cells[rows, :].astype(f32) + part[rows, :] * scale + beta
        y[rows, :] = v
        return 0

    lax.fori_loop(0, PIX, feature, 0)
    logit[...] = (
        lax.dot_general(y[...], learner, (((1,), (1,)), ((), ())), precision=HIGH, preferred_element_type=f32) * LEARN
    )

    def softmax_over_cells(v):
        v = v.reshape(PIX, PAIR, 128)
        e = jnp.exp(v - jnp.max(v, 0, keepdims=True))
        return e / jnp.sum(e, 0, keepdims=True)

    att[...] = softmax_over_cells(logit[...]).reshape(PIX * PAIR, 128)
    acc[...] = jnp.zeros_like(acc)
    for half in range(2):
        columns = slice(256 * half, 256 * half + 256)

        zero = jnp.zeros((PAIR, 256), f32)
        for t0 in range(0, NTOK, 4):

            def gather_some(cell, totals, t0=t0, columns=columns):
                rows = pl.ds(pl.multiple_of(cell * PAIR, PAIR), PAIR)
                a, v = att[rows, :], y[rows, columns]
                return tuple(t + a[:, t0 + i : t0 + i + 1] * v for i, t in enumerate(totals))

            totals = lax.fori_loop(0, PIX, gather_some, (zero,) * 4)
            for i in range(4):
                acc[(t0 + i) * PAIR : (t0 + i + 1) * PAIR, columns] = totals[i]
    tok = acc[...].astype(bf16).astype(f32)

    h1, normed1, inverse1 = norm_fwd(tok, gains[0])
    h1_low = h1.astype(bf16)
    row_q, row_k = iota((ROWS, ROWS), 0), iota((ROWS, ROWS), 1)
    image_q, image_k = lax.rem(row_q, PAIR), lax.rem(row_k, PAIR)
    order_q = image_q * NTOK + lax.div(row_q, PAIR)
    order_k = image_k * NTOK + lax.div(row_k, PAIR)
    seen = (lax.div(image_q, FRAMES) == lax.div(image_k, FRAMES)) & (order_k <= order_q)
    root = HD**-0.5
    acc[...] = jnp.zeros_like(acc)

    def attend(m, _):
        p = nn(h1_low, one[m, :, 0:384]).astype(bf16)
        qkv[m] = p
        outs = []
        for head in range(2):
            q, k, v = (p[:, 128 * j + 64 * head : 128 * j + 64 * head + 64] for j in range(3))
            s = jnp.where(seen, nt(q, k) * root, -1e30)
            e = jnp.exp(s - jnp.max(s, -1, keepdims=True))
            w = e / jnp.sum(e, -1, keepdims=True)
            prob[m, head] = w
            outs.append(nn(w.astype(bf16), v))
        o = jnp.concatenate(outs, axis=1).astype(bf16)
        ctx[m] = o
        acc[...] += nt(o, one[m, :, 384:512])
        return 0

    lax.fori_loop(0, 4, attend, 0)
    x1 = tok + OUT_MULT * acc[...]
    h2, normed2, inverse2 = norm_fwd(x1, gains[1])
    h2_low = h2.astype(bf16)
    acc[...] = x1

    def feed(m, _):
        u = nn(h2_low, two[m, :, 0:512])
        up[m] = u
        low = gelu_parts(u)[0].astype(bf16)
        hid[m] = low
        acc[...] += nt(low, two[m, :, 512:1024])
        return 0

    lax.fori_loop(0, 4, feed, 0)
    x2 = acc[...]
    normed_out, normed3, inverse3 = norm_fwd(x2, gains[2])
    pooled = (jnp.sum(normed_out.reshape(NTOK, PAIR, D), axis=0) * (1.0 / NTOK)).astype(bf16)

    low_half = lanes < 64
    scores = [nn(pooled, one[m, :, 512:1280]) for m in range(4)]
    weight = mask[...]
    loss = jnp.zeros((PAIR, 128), f32)
    for u in range(6):
        tiles = [s[:, 128 * u : 128 * u + 128] for s in scores]
        top = jnp.maximum(jnp.maximum(tiles[0], tiles[1]), jnp.maximum(tiles[2], tiles[3]))
        left = jnp.max(jnp.where(low_half, top, -jnp.inf), -1, keepdims=True)
        right = jnp.max(jnp.where(low_half, -jnp.inf, top), -1, keepdims=True)
        top = jnp.where(low_half, left, right)
        total = sum(jnp.exp(t - top) for t in tiles)
        left = jnp.sum(jnp.where(low_half, total, 0.0), -1, keepdims=True)
        right = jnp.sum(jnp.where(low_half, 0.0, total), -1, keepdims=True)
        lse = top + jnp.log(jnp.where(low_half, left, right))
        label = jnp.where(low_half, bins[:, 2 * u : 2 * u + 1], bins[:, 2 * u + 1 : 2 * u + 2])
        real = low_half | (2 * u + 1 < DIMS)
        target = jnp.zeros((PAIR, 128), f32)
        for m, t in enumerate(tiles):
            hit = label == (lanes & 63) + 64 * m
            target = target + jnp.where(hit, t, 0.0)
            slope = weight * (jnp.exp(t - lse) - hit.astype(f32))
            dlog[m, :, 128 * u : 128 * u + 128] = jnp.where(real, slope, 0.0).astype(bf16)
        counted = real & ((lanes & 63) == 0)
        loss = loss + weight * (jnp.where(counted, lse, 0.0) - target)
    stats[...] = jnp.zeros_like(stats)
    stats[0:8] = loss[0:8] + loss[8:16] + loss[16:24]
    counts = jnp.where(lanes == 0, weight, 0.0)
    stats[8:16] = counts[0:8] + counts[8:16] + counts[16:24]
    dpooled = jnp.zeros((PAIR, D), f32)
    for m in range(4):
        dpooled = dpooled + nt(dlog[m], one[m, :, 512:1280])
    dnormed = jnp.broadcast_to(dpooled * (1.0 / NTOK), (NTOK, PAIR, D)).reshape(ROWS, D)
    dx2, dgain2 = norm_back(normed3, inverse3, gains[2], dnormed)
    dbranch = dx2.astype(bf16)
    acc[...] = jnp.zeros_like(acc)

    def feed_back(m, _):
        slope = gelu_parts(up[m])[1]
        dup = (nn(dbranch, two[m, :, 512:1024]) * slope).astype(bf16)
        lowgrad[m] = dup
        acc[...] += nt(dup, two[m, :, 0:512])
        return 0

    lax.fori_loop(0, 4, feed_back, 0)
    dx1_norm, dgain1 = norm_back(normed2, inverse2, gains[1], acc[...])
    dx1 = dx2 + dx1_norm
    dattn = dx1.astype(bf16)

    def feed_weights(h, _):
        m = 2 * h + core
        done_one[h, :, 512:1280] = tn(pooled, dlog[m]).astype(bf16)
        done_two[h, :, 0:512] = tn(h2_low, lowgrad[m]).astype(bf16)
        done_two[h, :, 512:1024] = tn(dbranch, hid[m]).astype(bf16)
        done_one[h, :, 384:512] = (tn(dattn, ctx[m]) * OUT_MULT).astype(bf16)
        return 0

    lax.fori_loop(0, 2, feed_weights, 0)
    acc[...] = jnp.zeros_like(acc)

    def attend_back(m, _):
        do = (nn(dattn, one[m, :, 384:512]) * OUT_MULT).astype(bf16)
        p = qkv[m]
        dq, dk, dv = [], [], []
        for head in range(2):
            q, k, v = (p[:, 128 * j + 64 * head : 128 * j + 64 * head + 64] for j in range(3))
            w = prob[m, head]
            d = do[:, 64 * head : 64 * head + 64]
            dp = nt(d, v)
            dv.append(tn(w.astype(bf16), d))
            ds = (w * (dp - jnp.sum(w * dp, -1, keepdims=True))).astype(bf16)
            dq.append(nn(ds, k) * root)
            dk.append(tn(ds, q) * root)
        g = jnp.concatenate([*dq, *dk, *dv], axis=1).astype(bf16)
        lowgrad[m, :, 0:384] = g
        acc[...] += nt(g, one[m, :, 0:384])
        return 0

    lax.fori_loop(0, 4, attend_back, 0)

    def attend_weights(h, _):
        done_one[h, :, 0:384] = tn(h1_low, lowgrad[2 * h + core, :, 0:384]).astype(bf16)
        return 0

    lax.fori_loop(0, 2, attend_weights, 0)
    dtok_norm, dgain0 = norm_back(normed1, inverse1, gains[0], acc[...])
    acc[...] = dx1 + dtok_norm

    def slope_of(cell, _):
        rows = pl.ds(pl.multiple_of(cell * PAIR, PAIR), PAIR)
        v = y[rows, :]
        found = jnp.zeros((PAIR, 128), f32)
        for t in range(NTOK):
            s = jnp.sum(v * acc[t * PAIR : (t + 1) * PAIR, :], -1, keepdims=True)
            found = jnp.where(lanes == t, s, found)
        logit[rows, :] = found
        return 0

    lax.fori_loop(0, PIX, slope_of, 0)
    a = att[...].reshape(PIX, PAIR, 128)
    da = logit[...].reshape(PIX, PAIR, 128)
    logit[...] = (a * (da - jnp.sum(a * da, 0, keepdims=True)) * LEARN).reshape(PIX * PAIR, 128)
    dlearner = lax.dot_general(logit[...], y[...], (((0,), (0,)), ((), ())), precision=HIGH, preferred_element_type=f32)

    def spread(cell, sums):
        rows = pl.ds(pl.multiple_of(cell * PAIR, PAIR), PAIR)
        a, dl = att[rows, :], logit[rows, :]
        dy = jnp.zeros((PAIR, D), f32)
        for t in range(NTOK):
            dy = dy + a[:, t : t + 1] * acc[t * PAIR : (t + 1) * PAIR, :] + dl[:, t : t + 1] * learner[t : t + 1]
        dcells[rows, :] = (dy * scale).astype(bf16)
        return sums[0] + dy * part[rows, :], sums[1] + dy

    zero = jnp.zeros((PAIR, D), f32)
    dgamma, dbeta = lax.fori_loop(0, PIX, spread, (zero, zero))
    dgamma, dbeta = dgamma.astype(bf16), dbeta.astype(bf16)
    dcvec = only(nt(dgamma, flat) + shifted(nt(dbeta, flat), 4), 0) * FILM
    high = dcvec.astype(bf16).astype(f32)
    rest = dcvec - high
    dsmall = jnp.concatenate([dgain0, dgain1, dgain2, dlearner[0:8], jnp.zeros((5, D), f32)], axis=0).astype(bf16)
    mine = pl.ds(pl.multiple_of(core * 1024, 1024), 1024)
    lhs = jnp.concatenate(
        [cvec, cvec_4, shifted(high, 120), shifted(rest, 120), shifted(high, 116), shifted(rest, 116)], axis=0
    )
    lhs = jnp.where(core == 0, lhs[:, 0:1024], lhs[:, 1024:2048])
    lhs = jnp.concatenate([lhs, nt(dsmall, place_of_feature(core * 1024, 1024))], axis=0).astype(bf16)
    rhs = jnp.concatenate([dgamma, dbeta, choose_lo, choose_lo, choose_hi, choose_hi, pick], axis=0)
    result = tn(lhs, rhs)
    film_rows = (iota((1024, D), 0) & 15) < 8
    dmisc[...] = jnp.where(film_rows, result * FILM, result).astype(bf16)


def middle(core, part, cells, misc, one, two, instr, cam, bins, mask):
    vmem = pl.BlockSpec(memory_space=pltpu.VMEM)
    return pl.pallas_call(
        middle_kernel,
        out_shape=[
            jax.ShapeDtypeStruct((PIX * PAIR, D), bf16),
            jax.ShapeDtypeStruct((1024, D), bf16),
            jax.ShapeDtypeStruct((2, D, 1280), bf16),
            jax.ShapeDtypeStruct((2, D, 1024), bf16),
            jax.ShapeDtypeStruct((16, 128), f32),
        ],
        in_specs=[pl.BlockSpec(memory_space=pltpu.SMEM)] + [vmem] * 9,
        out_specs=[vmem] * 5,
        scratch_shapes=[
            pltpu.VMEM((PIX * PAIR, D), f32),
            pltpu.VMEM((PIX * PAIR, 128), f32),
            pltpu.VMEM((PIX * PAIR, 128), f32),
            pltpu.VMEM((4, ROWS, 384), bf16),
            pltpu.VMEM((4, 2, ROWS, ROWS), f32),
            pltpu.VMEM((4, ROWS, 128), bf16),
            pltpu.VMEM((4, ROWS, 512), f32),
            pltpu.VMEM((4, ROWS, 512), bf16),
            pltpu.VMEM((ROWS, D), f32),
            pltpu.VMEM((4, PAIR, 768), bf16),
            pltpu.VMEM((4, ROWS, 512), bf16),
        ],
        compiler_params=pltpu.CompilerParams(vmem_limit_bytes=VMEM_BYTES),
    )(core, part, cells, misc, one, two, instr, cam, bins, mask)


STEPS = 4
BLOCK = (PIX, PAIR, WIDTH)


def tap_places():
    row, col = iota((OWNERS * 128, WIDTH), 0), iota((OWNERS * 128, WIDTH), 1)
    return (((row >> 7) * 24 + (row & 127) == col) & ((row & 127) < 24)).astype(bf16)


def to_cells(frames, cells):
    rows = 8 * PAIR
    at, of = iota((rows, rows), 0), iota((rows, rows), 1)
    turn = (lax.rem(at, PAIR) * 8 + lax.div(at, PAIR) == of).astype(bf16)
    for first in (*range(0, PIX - 8, 8), PIX - 8):
        block = frames[:, :, first : first + 8, :].reshape(rows, D)
        cells[first * PAIR : first * PAIR + rows, :] = nn(turn, block).astype(bf16)


def forward_kernel(plan, *refs):
    n = len(plan)
    pairs, shards = refs[0:2], refs[2 : 2 + n]
    refs = refs[2 + n :]
    cam2, cells_out, project_out, taps_out, misc_out, one_out, two_out, pre_out, deep_out, total_out = refs[:10]
    frames2, cells, expand, project, slabs, taps, places, act, pre, deep, part, other = refs[10:22]
    send, recv, fsend, frecv, local, kept, swap_send, swap_recv = refs[22:]
    me = here()
    greet(me)
    swaps = []
    for i, out in enumerate((frames2, cam2)):
        mine = pltpu.make_async_copy(pairs[i], out.at[me["c"]], local.at[n + i])
        mine.start()
        swaps += [mine, remote(pairs[i], out.at[me["c"]], swap_send.at[i], swap_recv.at[i], "c", 1 - me["c"])]
    outs = (expand, project, slabs, misc_out, one_out, two_out)
    jobs = [
        Gather(me, dims, order, shards[b], outs[b], send.at[b], recv.at[b], fsend.at[b], frecv.at[b], local.at[b])
        for b, (dims, order) in enumerate(plan)
    ]
    first, rest = jobs[:3], jobs[3:]

    def relay(some, phase):
        for job in some:
            job.relay(phase)

    def finish(some, phase):
        for job in some:
            job.finish(phase)

    for job in jobs:
        job.begin()
    clear_borders(act)
    part[...] = jnp.zeros_like(part)
    places[...] = tap_places()
    relay(first, 0)
    finish(first, 0)
    swaps[0].wait()
    swaps[1].wait()
    to_cells(frames2, cells)
    relay(first, 1)
    finish(first, 1)
    relay(rest, 0)
    finish(rest, 0)
    saves = []

    def save(src, dst, number):
        copy = pltpu.make_async_copy(src, dst, kept.at[number])
        copy.start()
        saves.append(copy)

    save(cells, cells_out, 0)
    spans = [None] * STEPS
    for step in range(STEPS):
        slot = step % 2
        at = ring(me["x"], (0, -1, 1, 2)[step])
        if step == 1:
            relay(first, 2)
        if step == 3:
            finish(first, 2)
            save(project, project_out, 1)
        if step >= 2:
            for copy in spans[step - 2]:
                copy.wait()
        weight = expand[at].reshape(WIDTH, D)
        back = project[at].reshape(WIDTH, D)
        tap = slabs[at].reshape(OWNERS, 16, 128)
        side = jnp.concatenate([tap[i] for i in range(OWNERS)], axis=1)
        taps[at] = nn(side, places[...]) * (8.0 / 3.0)

        def enter(i, _, weight=weight, slot=slot):
            rows = pl.ds(pl.multiple_of(i * SPAN, SPAN), SPAN)
            e = (nt(cells[rows, :], weight) * EXPAND).reshape(CHUNK * MAP, PAIR, WIDTH)
            pre[slot, pl.ds(i * CHUNK * MAP, CHUNK * MAP)] = e
            act[pl.ds(1 + i * CHUNK, CHUNK)] = (e * sigmoid(e)).reshape(CHUNK, MAP, PAIR, WIDTH)
            return 0

        lax.fori_loop(0, MAP // CHUNK, enter, 0)
        out = [pltpu.make_async_copy(pre.at[slot], pre_out.at[at], kept.at[3 + 2 * step])]
        out[0].start()
        if step == 0:
            relay(rest, 1)
        if step == 2:
            relay(rest, 2)

        def mix(row, subs, cols, slot=slot, at=at):
            near = act[pl.ds(row, 3), :, subs, cols]
            tap = [jnp.broadcast_to(taps[at, t : t + 1, cols], (8, 128)) for t in range(9)]
            for col in range(MAP):
                total = None
                for t in range(9):
                    p = col + t % 3 - 1
                    if 0 <= p < MAP:
                        term = near[t // 3, p] * tap[t]
                        total = term if total is None else total + term
                deep[slot, row * MAP + col, subs, cols] = total

        each_block(mix)
        out.append(pltpu.make_async_copy(deep.at[slot], deep_out.at[at], kept.at[4 + 2 * step]))
        out[1].start()
        spans[step] = out
        if step == 0:
            finish(rest, 1)
        if step == 3:
            finish(rest, 2)

        def leave(i, _, back=back, slot=slot):
            rows = pl.ds(pl.multiple_of(i * SPAN, SPAN), SPAN)
            v = deep[slot, pl.ds(i * CHUNK * MAP, CHUNK * MAP)].reshape(SPAN, WIDTH)
            part[rows, :] += nn((v * sigmoid(v)).astype(bf16), back) * PROJECT
            return 0

        if step < STEPS - 1:
            lax.fori_loop(0, MAP // CHUNK, leave, 0)
    save(taps, taps_out, 2)
    trades = []
    for i in range(MAP // CHUNK):
        leave(i, 0)
        rows = pl.ds(i * SPAN, SPAN)
        trades.append(
            remote(part.at[rows], other.at[rows], swap_send.at[2 + i], swap_recv.at[2 + i], "c", 1 - me["c"])
        )
    for i, copy in enumerate(trades):
        copy.wait()
        rows = slice(i * SPAN, (i + 1) * SPAN)
        other[rows, :] += part[rows, :]
        save(other.at[rows], total_out.at[rows], 3 + 2 * STEPS + i)
    for step in (STEPS - 2, STEPS - 1):
        saves += spans[step]
    for job in jobs:
        job.end()
    for copy in saves + swaps[2:]:
        copy.wait()


def forward(pairs, shards, plan, collective_id):
    n = len(plan)
    frames, cam = pairs
    maps = jax.ShapeDtypeStruct((STEPS, *BLOCK), f32)
    shape = jax.ShapeDtypeStruct
    full = [shape((*lead(dims), *s.shape), s.dtype) for s, (dims, _) in zip(shards, plan)]
    rows = PIX * PAIR
    return pl.pallas_call(
        functools.partial(forward_kernel, plan),
        out_shape=[
            shape((2, *cam.shape), cam.dtype),
            shape((rows, D), bf16),
            full[1],
            shape((STEPS, 16, WIDTH), f32),
            *full[3:],
            maps,
            maps,
            shape((rows, D), f32),
        ],
        in_specs=[ANY] * (2 + n),
        out_specs=[ANY] * 10,
        scratch_shapes=[
            pltpu.VMEM((2, *frames.shape), bf16),
            pltpu.VMEM((rows, D), bf16),
            pltpu.VMEM(full[0].shape, bf16),
            pltpu.VMEM(full[1].shape, bf16),
            pltpu.VMEM(full[2].shape, bf16),
            pltpu.VMEM((STEPS, 16, WIDTH), f32),
            pltpu.VMEM((OWNERS * 128, WIDTH), bf16),
            pltpu.VMEM((MAP + 2, MAP, PAIR, WIDTH), f32),
            pltpu.VMEM((2, *BLOCK), f32),
            pltpu.VMEM((2, *BLOCK), f32),
            pltpu.VMEM((rows, D), f32),
            pltpu.VMEM((rows, D), f32),
            pltpu.SemaphoreType.DMA((n, 3, 4)),
            pltpu.SemaphoreType.DMA((n, 3, 4)),
            pltpu.SemaphoreType.DMA((n, 7)),
            pltpu.SemaphoreType.DMA((n, 7)),
            pltpu.SemaphoreType.DMA((n + 2,)),
            pltpu.SemaphoreType.DMA((3 + 2 * STEPS + MAP // CHUNK,)),
            pltpu.SemaphoreType.DMA((2 + MAP // CHUNK,)),
            pltpu.SemaphoreType.DMA((2 + MAP // CHUNK,)),
        ],
        compiler_params=pltpu.CompilerParams(
            collective_id=collective_id, has_side_effects=True, vmem_limit_bytes=VMEM_BYTES
        ),
    )(*pairs, *shards)


class Blocks:
    def __init__(self, me, dims, order, full, room, send, recv):
        self.me, self.dims, self.order, self.full = me, dims, order, full
        self.halves, self.wholes, self.slabs, self.last = room
        self.send, self.recv = send, recv
        self.going = [None] * STEPS
        self.sent = []

    def at(self, step, **more):
        return {"x": ring(self.me["x"], BACK[step]), **more}

    def push(self, step, slot, src, box, axis, move):
        return remote(src, box, self.send.at[step, slot], self.recv.at[step, slot], axis, ring(self.me[axis], move))

    def launch(self, step):
        a, b, _ = self.order
        self.going[step] = [
            self.push(
                step, side, self.full.at[spot(self.dims, self.at(step, **{a: ring(self.me[a], 2)}, **half(b, side)))],
                self.halves.at[step, side], a, 1 - 2 * side,
            )
            for side in range(2)
        ]

    def relay(self, step):
        a, b, _ = self.order
        for side, move in ((0, 1), (1, -1)):
            self.going[step][side].wait()
            pos = {a: ring(self.me[a], move)}
            add_into(self.full, self.dims, self.at(step, **pos, **half(b, side)), [self.halves.at[step, side]])
            where = self.full.at[spot(self.dims, self.at(step, **pos))]
            self.going[step].append(self.push(step, 2 + side, where, self.wholes.at[step, side], a, move))

    def middle(self, step):
        a, b, _ = self.order
        for copy in self.going[step][2:]:
            copy.wait()
        own = {a: self.me[a]}
        add_into(self.full, self.dims, self.at(step, **own), [self.wholes.at[step, side] for side in range(2)])
        self.going[step] = [
            self.push(
                step, 4 + i, self.full.at[spot(self.dims, self.at(step, **own, **{b: ring(self.me[b], move)}))],
                self.slabs.at[step, i], b, move,
            )
            for i, move in enumerate((2, 1, -1))
        ]

    def finish(self, step):
        a, b, _ = self.order
        for copy in self.going[step]:
            copy.wait()
        index = spot(self.dims, self.at(step, **{a: self.me[a], b: self.me[b]}))
        total = self.full[index].astype(f32)
        for i in range(3):
            total = total + self.slabs[step, i].astype(f32)
        if BACK[step] != 0:
            self.full[index] = total.astype(bf16)
            self.sent.append(self.push(step, 7, self.full.at[index], self.last.at[step], "x", BACK[step]))
        return total

    def close(self, total):
        for copy in self.sent:
            copy.wait()
        for i in range(STEPS - 1):
            total = total + self.last[i].astype(f32)
        return total

    @staticmethod
    def scratch(dims, order, slab):
        rest = without(without(dims, "x"), order[0])
        small = free_sizes(rest, half(order[1], 0))
        shapes = [
            (*lead(dims), *slab), (STEPS, 2, *small, *slab), (STEPS, 2, *lead(rest), *slab), (STEPS, 3, *slab),
            (STEPS - 1, *slab),
        ]
        return [pltpu.VMEM(s, bf16) for s in shapes]


BACK = (2, 1, -1, 0)


def backward_kernel(plan, *refs):
    n = len(plan)
    cells_in, dcells_in, project_in, taps_in, pre_in, deep_in, stats = refs[:7]
    parts = refs[7 : 7 + n - 3]
    refs = refs[4 + n :]
    stats_out, outs = refs[0], refs[1 : 1 + n]
    refs = refs[1 + n :]
    cells, dcells, project, taps, places, pre, deep, spread, mid, dpre, acc = refs[:11]
    refs = refs[11:]
    blocks_room, rest_room = refs[:15], refs[15 : 15 + 13 * (n - 3)]
    tile, tile_box, bsend, brecv, send, recv, local, kept, tsend, trecv = refs[15 + 13 * (n - 3) :]
    me = here()
    loads = []
    for i, (src, dst) in enumerate(((cells_in, cells), (dcells_in, dcells), (project_in, project), (taps_in, taps))):
        copy = pltpu.make_async_copy(src, dst, kept.at[i])
        copy.start()
        loads.append(copy)

    def fetch(step):
        at = ring(me["x"], BACK[step])
        pair = []
        for i, (src, dst) in enumerate(((pre_in, pre), (deep_in, deep))):
            copy = pltpu.make_async_copy(src.at[at], dst.at[step % 2], kept.at[4 + 2 * step + i])
            copy.start()
            pair.append(copy)
        return pair

    maps = [fetch(0), fetch(1), None, None]
    greet(me)
    rest = []
    for b, (dims, order) in enumerate(plan[3:]):
        own = rest_room[13 * b : 13 * b + 13]
        boxes = [own[1:5], own[5:9], own[9:13]]
        rest.append(Scatter(me, dims, order, parts[b], own[0], boxes, send.at[b], recv.at[b], local.at[b]))
    first = [
        Blocks(me, dims, order, blocks_room[5 * b], blocks_room[5 * b + 1 : 5 * b + 5], bsend.at[b], brecv.at[b])
        for b, (dims, order) in enumerate(plan[:3])
    ]
    for job in rest:
        job.begin()
    clear_borders(spread)
    places[...] = tap_places()
    for copy in loads:
        copy.wait()
    square = jnp.zeros((8, 128), f32)

    def close_rest(square):
        for b, job in enumerate(rest):
            total = job.finish(2)
            outs[3 + b][...] = total
            square = square + folded(total * total)
        return square

    for step in range(STEPS):
        slot = step % 2
        at = ring(me["x"], BACK[step])
        for copy in maps[step]:
            copy.wait()
        back = project[at].reshape(WIDTH, D)

        def enter(i, _, back=back, slot=slot):
            rows = pl.ds(pl.multiple_of(i * SPAN, SPAN), SPAN)
            dmid = nt(dcells[rows, :], back) * PROJECT
            v = deep[slot, pl.ds(i * CHUNK * MAP, CHUNK * MAP)].reshape(SPAN, WIDTH)
            s = sigmoid(v)
            m = v * s
            mid[rows, :] = m.astype(bf16)
            spread[pl.ds(1 + i * CHUNK, CHUNK)] = (dmid * (s + m * (1.0 - s))).reshape(CHUNK, MAP, PAIR, WIDTH)
            return 0

        lax.fori_loop(0, MAP // CHUNK, enter, 0)
        if step > 0:
            for job in first:
                job.relay(step - 1)
        if step > 1:
            for job in first:
                job.finish(step - 2)
        if step == 2:
            for job in rest:
                job.relay(1)
        if step == 3:
            square = close_rest(square)
        acc[...] = jnp.zeros_like(acc)

        def mix(row, subs, cols, slot=slot, at=at):
            near = spread[pl.ds(row, 3), :, subs, cols]
            tap = [jnp.broadcast_to(taps[at, t : t + 1, cols], (8, 128)) for t in range(9)]
            sums = [None] * 9
            for col in range(MAP):
                e = pre[slot, row * MAP + col, subs, cols]
                s = sigmoid(e)
                a = e * s
                total = None
                for t in range(9):
                    p = col + 1 - t % 3
                    if 0 <= p < MAP:
                        g = near[2 - t // 3, p]
                        term = g * tap[t]
                        total = term if total is None else total + term
                        term = g * a
                        sums[t] = term if sums[t] is None else sums[t] + term
                dpre[row * MAP + col, subs, cols] = total * (s + a * (1.0 - s))
            for t in range(9):
                acc[t, :, cols] += sums[t]

        each_block(mix)
        if step + 2 < STEPS:
            maps[step + 2] = fetch(step + 2)
        if step == 0:
            for job in rest:
                job.relay(0)
        if step == 1:
            for job in rest:
                job.finish(0)
        if step == 2:
            for job in rest:
                job.finish(1)
        if step > 0:
            for job in first:
                job.middle(step - 1)
        owned = (2, 4, 2, 24, D)
        low = dpre[...].reshape(PIX * PAIR, WIDTH).astype(bf16)
        first[0].full[at] = (tn(low, cells[...]) * EXPAND).astype(bf16).reshape(owned)
        first[1].full[at] = (tn(mid[...], dcells[...]) * PROJECT).astype(bf16).reshape(owned)
        dtaps = jnp.concatenate([jnp.sum(acc[...], axis=1) * (8.0 / 3.0), jnp.zeros((7, WIDTH), f32)], axis=0)
        side = nt(dtaps.astype(bf16), places[...]).astype(bf16)
        for i in range(OWNERS):
            first[2].full[at, i // 8, (i // 2) % 4, i % 2] = side[:, 128 * i : 128 * i + 128]
        for job in first:
            job.launch(step)
    for job in first:
        job.relay(STEPS - 1)
    for job in first:
        job.finish(STEPS - 2)
    for job in first:
        job.middle(STEPS - 1)
    for b, job in enumerate(first):
        total = job.close(job.finish(STEPS - 1))
        outs[b][...] = total
        square = square + folded(total * total)
    tile[0, 0:16, :] = stats[...]
    tile[0, 16:24, :] = square
    for phase, axis in enumerate("cxyz"):
        size = 2 if axis == "c" else RING
        copies = [
            remote(
                tile.at[phase], tile_box.at[phase, k - 1], tsend.at[phase, k - 1], trecv.at[phase, k - 1],
                axis, lax.rem(me[axis] + k, size),
            )
            for k in range(1, size)
        ]
        for copy in copies:
            copy.wait()
        total = tile[phase]
        for k in range(size - 1):
            total = total + tile_box[phase, k]
        tile[phase + 1] = total
    stats_out[...] = tile[4]


def backward(cells, dcells, project, taps, pre, deep, stats, parts, slabs, plan, collective_id):
    n = len(plan)
    shape = jax.ShapeDtypeStruct
    rows = PIX * PAIR
    room = []
    for (dims, order), slab in zip(plan[:3], slabs[:3]):
        room += Blocks.scratch(dims, order, slab)
    for (dims, order), slab in zip(plan[3:], slabs[3:]):
        room += Scatter.scratch(dims, order, slab, bf16)
    return pl.pallas_call(
        functools.partial(backward_kernel, plan),
        out_shape=[shape((24, 128), f32)] + [shape(s, f32) for s in slabs],
        in_specs=[ANY] * 6 + [INVMEM] + [ANY] * (n - 3),
        out_specs=[INVMEM] * (1 + n),
        scratch_shapes=[
            pltpu.VMEM((rows, D), bf16),
            pltpu.VMEM((rows, D), bf16),
            pltpu.VMEM(project.shape, bf16),
            pltpu.VMEM(taps.shape, f32),
            pltpu.VMEM((OWNERS * 128, WIDTH), bf16),
            pltpu.VMEM((2, *BLOCK), f32),
            pltpu.VMEM((2, *BLOCK), f32),
            pltpu.VMEM((MAP + 2, MAP, PAIR, WIDTH), f32),
            pltpu.VMEM((rows, WIDTH), bf16),
            pltpu.VMEM(BLOCK, f32),
            pltpu.VMEM((9, 8, WIDTH), f32),
            *room,
            pltpu.VMEM((5, 24, 128), f32),
            pltpu.VMEM((4, 3, 24, 128), f32),
            pltpu.SemaphoreType.DMA((3, STEPS, 8)),
            pltpu.SemaphoreType.DMA((3, STEPS, 8)),
            pltpu.SemaphoreType.DMA((n - 3, 3, 4)),
            pltpu.SemaphoreType.DMA((n - 3, 3, 4)),
            pltpu.SemaphoreType.DMA((n - 3,)),
            pltpu.SemaphoreType.DMA((4 + 2 * STEPS,)),
            pltpu.SemaphoreType.DMA((4, 3)),
            pltpu.SemaphoreType.DMA((4, 3)),
        ],
        compiler_params=pltpu.CompilerParams(
            collective_id=collective_id, has_side_effects=True, vmem_limit_bytes=VMEM_BYTES
        ),
    )(cells, dcells, project, taps, pre, deep, stats, *parts)


TAIL = TABLE + 11
IMAGES = 12
MP = ("mp_0", "mp_1")
DP_MP = NAMES
DP = ("dp_0", "dp_1", "dp_2")
CLIP_NORM = 0.02
BETA_ONE = 0.9
BETA_TWO = 0.999
ADAM_EPS = 1e-08
DECAY = 0.01
RATES = (0.1, 0.1, 0.2, 0.05, 0.05, 0.2)


def adam(master, first, second, grad, t, rate):
    first_new = BETA_ONE * first + (1.0 - BETA_ONE) * grad
    second_new = BETA_TWO * second + (1.0 - BETA_TWO) * grad * grad
    m_hat = first_new / (1.0 - BETA_ONE**t)
    v_hat = second_new / (1.0 - BETA_TWO**t)
    master_new = master - rate * (m_hat / (jnp.sqrt(v_hat) + ADAM_EPS) + DECAY * master)
    return [master_new, first_new, second_new]


def pack_misc(film, table, small):
    tail = jnp.concatenate([table, small], axis=1)
    tail = jnp.pad(tail, ((0, 0), (0, 2 * D - tail.shape[1])))
    return jnp.concatenate([film[:, :D], film[:, D:], tail[:, :D], tail[:, D:]], axis=0)


def unpack_misc(misc):
    film = jnp.concatenate([misc[0:4], misc[4:8]], axis=1)
    tail = jnp.concatenate([misc[8:12], misc[12:16]], axis=1)
    return film, tail[:, :TABLE], tail[:, TABLE:TAIL]


def pack_attn_head(attn, head):
    both = jnp.concatenate([*attn, head], axis=-1)
    return jnp.pad(both, [(0, 0)] * (both.ndim - 1) + [(0, 1280 - both.shape[-1])])


def per_device(
    frames, camera_ids, instruction_ids, action_bins, final_mask, step_count,
    conv_w, conv_m1, conv_m2, cond_w, cond_m1, cond_m2, small_w, small_m1, small_m2,
    attn_w, attn_m1, attn_m2, mlp_w, mlp_m1, mlp_m2, head_w, head_m1, head_m2,
):
    core, high = lax.axis_index("mp_1"), lax.axis_index("mp_0")
    conv_t = conv_w.T.astype(bf16)
    cond_t = cond_w.T.astype(bf16)
    attn_l = attn_w.astype(bf16)
    shards = (
        conv_t[:, :D],
        conv_t[:, D : 2 * D],
        jnp.pad(conv_w[2 * D :].astype(bf16), ((0, 7), (0, 104))),
        pack_misc(cond_t[:, : 2 * D], cond_t[:, 2 * D :], small_w.T.astype(bf16)),
        pack_attn_head([attn_l[j] for j in range(4)], head_w.astype(bf16).reshape(16, DIMS * 64)),
        jnp.moveaxis(mlp_w.astype(bf16), 0, 1).reshape(16, 1024),
    )
    image = jnp.arange(PAIR)
    cam = jnp.where(image // IMAGES == core, jnp.tile(camera_ids, 2), 0)
    cam = jnp.broadcast_to(cam[:, None], (PAIR, 128))
    cam2, cells, project, taps, misc_all, one_all, two_all, pre, deep, part = forward((frames, cam), shards, GATHER, 1)
    instr = jnp.repeat(lax.dynamic_slice_in_dim(instruction_ids, high * 4, 4), FRAMES)
    bins = jnp.pad(
        lax.dynamic_slice_in_dim(action_bins, high * PAIR, PAIR), ((0, 0), (0, 128 - DIMS)), constant_values=-1
    )
    mask = lax.dynamic_slice_in_dim(final_mask, high * PAIR, PAIR).astype(f32)
    dcells, dmisc, done_one, done_two, stats = middle(
        core[None],
        part,
        cells,
        misc_all.reshape(2048, D),
        one_all.reshape(4, D, 1280),
        two_all.reshape(4, D, 1024),
        jnp.broadcast_to(instr[:, None], (PAIR, 128)),
        cam2,
        bins,
        jnp.broadcast_to(mask[:, None], (PAIR, 128)),
    )
    parts = [
        g.reshape(*lead(dims), *s.shape)
        for g, s, (dims, _) in zip((dmisc, done_one, done_two), shards[3:], SCATTER[3:])
    ]
    totals, gexpand, gproject, gtaps, gmisc, gone, gtwo = backward(
        cells, dcells, project, taps, pre, deep, stats, parts, [s.shape for s in shards], SCATTER, 2
    )
    gfilm, gtable, gsmall = unpack_misc(gmisc)
    grads = (
        jnp.concatenate([gexpand.T, gproject.T, gtaps[:9, :24]], 0),
        jnp.concatenate([gfilm, gtable], 1).T,
        gsmall.T,
        jnp.stack([gone[:, 128 * j : 128 * j + 128] for j in range(4)]),
        jnp.moveaxis(gtwo.reshape(16, 2, 512), 1, 0),
        gone[:, 512 : 512 + DIMS * 64].reshape(16, DIMS, 64),
    )
    loss_sum, count, square = (jnp.sum(totals[8 * i : 8 * i + 8]) for i in range(3))
    loss_sum, count = 0.5 * loss_sum, 0.5 * count
    norm = jnp.sqrt(square) / count
    factor = jnp.minimum(1.0, CLIP_NORM / norm) / count
    steps_done = step_count[0].astype(f32)
    masters = (conv_w, cond_w, small_w, attn_w, mlp_w, head_w)
    firsts = (conv_m1, cond_m1, small_m1, attn_m1, mlp_m1, head_m1)
    seconds = (conv_m2, cond_m2, small_m2, attn_m2, mlp_m2, head_m2)
    outs = [loss_sum / count, norm]
    for idx in range(6):
        outs.extend(adam(masters[idx], firsts[idx], seconds[idx], grads[idx] * factor, steps_done, RATES[idx]))
    return tuple(outs)


def solution(mesh):
    torus = Mesh(mesh.devices.reshape(2, 4, 4, 2, 2), NAMES)
    weights = (
        *[P(None, DP_MP)] * 9,
        *[P(None, DP, MP)] * 6,
        *[P(DP, None, MP)] * 3,
    )
    data = (P(DP_MP, None, None), P(DP_MP), P(DP), P(DP, None), P(DP), P())
    return jax.shard_map(
        per_device, mesh=torus, in_specs=(*data, *weights), out_specs=(P(), P(), *weights), check_vma=False
    )
```

```python
import functools
import math

import jax
import jax.numpy as jnp
from jax import lax
from jax.experimental import pallas as pl
from jax.experimental.pallas import tpu as pltpu
from jax.sharding import Mesh
from jax.sharding import PartitionSpec as P

f32 = jnp.float32
bf16 = jnp.bfloat16
NAMES = ("dp_0", "dp_1", "dp_2", "mp_0", "mp_1")
SIZES = {"l": 2, "z": 4, "x": 4, "h": 2, "c": 2}
RING = 4
MESH_ID = pl.DeviceIdType.MESH
ANY = pl.BlockSpec(memory_space=pl.ANY)
INVMEM = pl.BlockSpec(memory_space=pltpu.VMEM)


def here():
    low, z, x, high, core = (lax.axis_index(n) for n in NAMES)
    return {"x": x, "y": high * 2 + low, "z": z, "c": core}


def ring(at, step):
    return lax.rem(at + step + RING, RING)


def device_of(axis, at):
    if axis == "y":
        return {"dp_0": lax.rem(at, 2), "mp_0": at // 2}
    return {{"x": "dp_2", "z": "dp_1", "c": "mp_1"}[axis]: at}


def extents(dims, at):
    found = []
    for d in dims:
        if d in at:
            v = at[d]
        elif d == "l" and "y" in at:
            v = lax.rem(at["y"], 2)
        elif d == "h" and "y" in at:
            v = at["y"] // 2
        else:
            v = (0, SIZES[d])
        found.append(v if isinstance(v, tuple) else (v, None))
    return found


def spot(dims, at):
    return tuple(start if size is None else pl.ds(start, size) for start, size in extents(dims, at))


def free_sizes(dims, at):
    return tuple(size for _, size in extents(dims, at) if size is not None)


def half(axis, side):
    return {"h": side} if axis == "y" else {axis: (2 * side, 2)}


def without(dims, axis):
    return tuple(d for d in dims if d not in ("lh" if axis == "y" else axis))


def lead(dims):
    return tuple(SIZES[d] for d in dims)


def announce(me, wide=False):
    barrier = pltpu.get_barrier_semaphore()
    peers = [{a: k} for a in "xyz" for k in range(1, RING)] + [{"c": 1}]
    if wide:
        peers += [{"x": k, "c": 1} for k in range(1, RING)]
        peers += [{"y": j, "z": k} for j in range(1, RING) for k in range(1, RING)]
    for moves in peers:
        pl.semaphore_signal(barrier, inc=1, device_id=moved(me, moves), device_id_type=MESH_ID)
    return len(peers)


def moved(me, moves):
    found = {}
    for axis, k in moves.items():
        found.update(device_of(axis, lax.rem(me[axis] + k, 2 if axis == "c" else RING)))
    return found


def meet(count):
    pl.semaphore_wait(pltpu.get_barrier_semaphore(), count)


def remote(src, dst, send, recv, axis, at):
    copy = pltpu.make_async_remote_copy(
        src_ref=src, dst_ref=dst, send_sem=send, recv_sem=recv, device_id=device_of(axis, at), device_id_type=MESH_ID
    )
    copy.start()
    return copy


class Gather:
    def __init__(self, me, dims, order, shard, out, send, recv, fsend, frecv, local):
        self.me, self.dims, self.order, self.shard, self.out = me, dims, order, shard, out
        self.send, self.recv, self.fsend, self.frecv, self.local = send, recv, fsend, frecv, local
        self.forwards = []

    def region(self, phase, step=0, part=None):
        at = {a: self.me[a] for a in self.order[phase:]}
        at[self.order[phase]] = ring(self.me[self.order[phase]], step)
        if "c" in self.dims:
            at["c"] = self.me["c"]
        if part is not None:
            at.update(half(self.order[0], part))
        return self.out.at[spot(self.dims, at)]

    def push(self, phase, slot, where, step):
        axis = self.order[phase]
        src = self.shard if phase == 0 else where
        return remote(src, where, self.send.at[phase, slot], self.recv.at[phase, slot], axis, ring(self.me[axis], step))

    def forward(self, number, where):
        if "c" in self.dims:
            self.forwards.append(
                remote(where, where, self.fsend.at[number], self.frecv.at[number], "c", 1 - self.me["c"])
            )

    def begin(self):
        self.kept = pltpu.make_async_copy(self.shard, self.region(0), self.local)
        self.kept.start()
        self.launch(0)

    def launch(self, phase):
        where = self.region(phase)
        self.going = [self.push(phase, 0, where, 1), self.push(phase, 1, where, -1)]
        if phase == 0:
            self.going.append(self.push(0, 2, where, 2))

    def relay(self, phase):
        for slot, step in ((0, 1), (1, -1)):
            self.going[slot].wait()
            if phase > 0:
                self.going.append(self.push(phase, 2 + slot, self.region(phase, -step, slot), step))
                self.forward(3 * phase - 2 + slot, self.region(phase, -step))

    def finish(self, phase):
        for copy in self.going[2:]:
            copy.wait()
        if phase == 0:
            self.kept.wait()
            if "c" in self.dims:
                at = {a: self.me[a] for a in (*self.order[1:], "c")}
                self.forward(0, self.out.at[spot(self.dims, at)])
        else:
            self.forward(3 * phase, self.region(phase, 2))
        if phase < 2:
            self.launch(phase + 1)

    def end(self):
        for copy in self.forwards:
            copy.wait()


def add_into(full, dims, at, others):
    found = extents(dims, at)
    sizes = free_sizes(dims, at)

    def one(i, _):
        index, place = [], []
        for start, size in reversed(found):
            if size is None:
                index.append(start)
            else:
                index.append(start + lax.rem(i, size))
                place.append(lax.rem(i, size))
                i = i // size
        index, place = tuple(reversed(index)), tuple(reversed(place))
        total = full[index].astype(f32)
        for o in others:
            total = total + o[place].astype(f32)
        full[index] = total.astype(full.dtype)
        return 0

    lax.fori_loop(0, math.prod(sizes), one, 0)


def folded(v):
    total = None
    for r in range(0, v.shape[0], 8):
        for c in range(0, v.shape[1], 128):
            part = v[r : r + 8, c : c + 128]
            total = part if total is None else total + part
    return total


class Scatter:
    def __init__(self, me, dims, order, part, full, boxes, send, recv, local):
        self.me, self.dims, self.order, self.part, self.full, self.boxes = me, dims, order, part, full, boxes
        self.send, self.recv, self.local = send, recv, local

    def at(self, phase, step, side=None):
        at = {a: self.me[a] for a in self.order[:phase]}
        axis = self.order[phase]
        at[axis] = ring(self.me[axis], step)
        if side is not None:
            at.update(half(self.order[phase + 1], side))
        return at

    def push(self, phase, slot, src, step):
        axis = self.order[phase]
        return remote(
            src, self.boxes[phase][slot], self.send.at[phase, slot], self.recv.at[phase, slot], axis, ring(self.me[axis], step)
        )

    def begin(self):
        self.kept = pltpu.make_async_copy(self.part, self.full, self.local)
        self.kept.start()
        self.launch(0)

    def launch(self, phase):
        src = self.part if phase == 0 else self.full
        if phase < 2:
            self.going = [
                self.push(phase, side, src.at[spot(self.dims, self.at(phase, 2, side))], 1 - 2 * side) for side in range(2)
            ]
        else:
            self.going = [
                self.push(phase, slot, src.at[spot(self.dims, self.at(phase, step))], step)
                for slot, step in ((0, 2), (2, 1), (3, -1))
            ]

    def relay(self, phase):
        if phase == 0:
            self.kept.wait()
        if phase == 2:
            return
        for side, step in ((0, 1), (1, -1)):
            self.going[side].wait()
            add_into(self.full, self.dims, self.at(phase, step, side), [self.boxes[phase][side]])
            self.going.append(self.push(phase, 2 + side, self.full.at[spot(self.dims, self.at(phase, step))], step))

    def finish(self, phase):
        if phase < 2:
            for copy in self.going[2:]:
                copy.wait()
            add_into(self.full, self.dims, self.at(phase, 0), self.boxes[phase][2:4])
            self.launch(phase + 1)
            return None
        for copy in self.going:
            copy.wait()
        total = self.full[spot(self.dims, self.at(2, 0))].astype(f32)
        for slot in (0, 2, 3):
            total = total + self.boxes[2][slot][...].astype(f32)
        return total

    @staticmethod
    def scratch(dims, order, slab, dtype):
        shapes = [(*lead(dims), *slab)]
        rest = dims
        for phase, axis in enumerate(order):
            rest = without(rest, axis)
            if phase < 2:
                small = free_sizes(rest, half(order[phase + 1], 0))
            else:
                small = ()
            shapes += [(*small, *slab)] * 2 + [(*lead(rest), *slab)] * 2
        return [pltpu.VMEM(s, dtype) for s in shapes]


OWNED = ("x", "l", "z", "h")
GATHER = (
    (OWNED, ("z", "y", "x")),
    (OWNED, ("x", "z", "y")),
    (OWNED, ("z", "y", "x")),
    (("c", "l", "z", "x", "h"), ("z", "x", "y")),
    (("h", "c", "l", "z", "x"), ("y", "x", "z")),
    (("h", "c", "l", "z", "x"), ("z", "y", "x")),
)
SCATTER = (
    (OWNED, ("z", "y", "x")),
    (OWNED, ("y", "z", "x")),
    (OWNED, ("z", "y", "x")),
    (("l", "z", "x", "h"), ("z", "y", "x")),
    (("h", "l", "z", "x"), ("x", "y", "z")),
    (("h", "l", "z", "x"), ("y", "x", "z")),
)
SLABS = ((24, 512), (24, 512), (16, 128), (16, 512), (16, 1280), (16, 1024))


D, EXP, MAP, PIX = 512, 3072, 9, 81
PAIR = 24
WIDTH = 384
OWNERS = WIDTH // 24
CHUNK = 3
SPAN = CHUNK * MAP * PAIR
EXPAND = 8.0 / math.sqrt(D)
PROJECT = 8.0 / math.sqrt(EXP)
VMEM_BYTES = 60 * 2**20


def sigmoid(v):
    return 0.5 + 0.5 * jnp.tanh(0.5 * v)


def nt(left, right):
    return lax.dot_general(left, right, (((1,), (1,)), ((), ())), preferred_element_type=f32)


def nn(left, right):
    return lax.dot_general(left, right, (((1,), (0,)), ((), ())), preferred_element_type=f32)


def tn(left, right):
    return lax.dot_general(left, right, (((0,), (0,)), ((), ())), preferred_element_type=f32)


def clear_borders(padded):
    zero = jnp.zeros((MAP, PAIR, WIDTH), f32)
    padded[0] = zero
    padded[MAP + 1] = zero


def each_block(body):
    def one(row, _):
        for lane in range(WIDTH // 128):
            for group in range(PAIR // 8):
                body(row, slice(8 * group, 8 * group + 8), slice(128 * lane, 128 * lane + 128))
        return 0

    lax.fori_loop(0, MAP, one, 0)


INSTR, DIMS, BINS, NTOK, FRAMES, HEADS, HD = 744, 11, 256, 8, 6, 8, 64
TABLE = INSTR + 2
ROWS = PAIR * NTOK
PADDED = 2048
SMALL_AT = TABLE - D
LN_EPS = 1e-06
OUT_MULT = 2.0
HIGH = lax.Precision.HIGHEST
FILM = 16.0 / math.sqrt(D)
LEARN = 4.0 / math.sqrt(D)


def norm_fwd(x, gain):
    centre = x - jnp.mean(x, -1, keepdims=True)
    inverse = lax.rsqrt(jnp.mean(centre * centre, -1, keepdims=True) + LN_EPS)
    normed = centre * inverse
    return normed * (1.0 + gain), normed, inverse


def norm_back(normed, inverse, gain, grad_out):
    dnormed = grad_out * (1.0 + gain)
    grad_in = inverse * (
        dnormed
        - jnp.mean(dnormed, -1, keepdims=True)
        - normed * jnp.mean(dnormed * normed, -1, keepdims=True)
    )
    return grad_in, jnp.sum(grad_out * normed, 0, keepdims=True)


def gelu_parts(u):
    c = math.sqrt(2.0 / math.pi)
    square = u * u
    t = jnp.tanh(c * u * (1.0 + 0.044715 * square))
    half = 0.5 * (1.0 + t)
    return u * half, half + 0.5 * u * (1.0 - t * t) * c * (1.0 + 3.0 * 0.044715 * square)


def iota(shape, axis):
    return lax.broadcasted_iota(jnp.int32, shape, axis)


def shifted(v, places):
    tiles = [pltpu.roll(v[:, i : i + 128], (128 - places) % 128, 1) for i in range(0, v.shape[1], 128)]
    return jnp.concatenate(tiles, axis=1)


def only(v, first):
    place = iota(v.shape, 1) & 15
    return jnp.where((place >= first) & (place < first + 4), v, 0.0)


def place_of_feature(start, rows):
    d = iota((rows, D), 1)
    owner = d >> 2
    row = (owner & 1) * 1024 + (owner >> 1) * 16 + 12 + (d & 3)
    return (iota((rows, D), 0) + start == row).astype(bf16)


def over_cells(body, carry):
    many = 16 * PAIR
    carry = lax.fori_loop(
        0, PIX // 16, lambda i, c: body(pl.ds(pl.multiple_of(i * many, many), many), many, c), carry
    )
    return body(slice(PIX // 16 * many, PIX * PAIR), PAIR, carry)


def middle_kernel(
    core_ref, part, cells, misc, one_in, two_in, instr, cam, bins, mask,
    dcells, dmisc, one_out, two_out, stats,
    one, two, done_one, done_two, y_hi, y_lo, logit, att, qkv, prob, ctx, up, hid, acc, dlog, lowgrad, sems,
):
    core = core_ref[0]
    fetch_one = pltpu.make_async_copy(one_in, one, sems.at[0])
    fetch_two = pltpu.make_async_copy(two_in, two, sems.at[1])
    fetch_one.start()
    fetch_two.start()
    lanes = iota((PAIR, 128), 1)

    def chosen(tile):
        at = lanes + 128 * tile
        return ((at == instr[...]) | (at == INSTR + cam[0] + cam[1])).astype(f32)

    choose_lo = jnp.concatenate([chosen(i) for i in range(4)], axis=1).astype(bf16)
    choose_hi = jnp.concatenate([chosen(i) for i in range(4, 8)], axis=1).astype(bf16)
    flat = misc[...]
    cvec = only(shifted(nt(choose_lo, flat), 8) + shifted(nt(choose_hi, flat), 12), 0).astype(bf16).astype(f32)
    cvec_4 = shifted(cvec, 124)
    cvec_low, cvec_4_low = cvec.astype(bf16), cvec_4.astype(bf16)
    gamma = nn(cvec_low, flat) * FILM
    beta = nn(cvec_4_low, flat) * FILM
    scale = 1.0 + gamma
    pick = (iota((16, D), 1) == SMALL_AT + iota((16, D), 0)).astype(bf16)
    small = nn(nt(pick, flat).astype(bf16), place_of_feature(0, 2048))
    gains = [small[i : i + 1] for i in range(3)]
    learner = jnp.concatenate([small[3:11], jnp.zeros((120, D), f32)], axis=0).astype(bf16)

    def feature(rows, size, _):
        v = part[rows, :].reshape(size // PAIR, PAIR, D) * scale + beta
        v = v.reshape(size, D) + cells[rows, :].astype(f32)
        hi = v.astype(bf16)
        y_hi[rows, :] = hi
        y_lo[rows, :] = (v - hi.astype(f32)).astype(bf16)
        return 0

    over_cells(feature, 0)
    tail = slice(PIX * PAIR, PADDED)
    for ref in (y_hi, y_lo, att, logit):
        ref[tail, :] = jnp.zeros((PADDED - PIX * PAIR, ref.shape[1]), ref.dtype)
    used = slice(0, PIX * PAIR)
    logit[used, :] = (nt(y_hi[used, :], learner) + nt(y_lo[used, :], learner)) * LEARN

    def softmax_over_cells(v):
        v = v.reshape(PIX, PAIR, 128)
        e = jnp.exp(v - jnp.max(v, 0, keepdims=True))
        return e / jnp.sum(e, 0, keepdims=True)

    att[used, :] = softmax_over_cells(logit[used, :]).reshape(PIX * PAIR, 128)
    acc[...] = jnp.zeros_like(acc)

    def gather(i, _):
        rows = pl.ds(pl.multiple_of(i * 512, 512), 512)
        turned = jnp.concatenate(
            [att[pl.ds(pl.multiple_of(i * 512 + 128 * k, 128), 128), :].T[0:NTOK] for k in range(4)], axis=1
        )
        hi = turned.astype(bf16).astype(f32)
        lo = turned - hi
        image = lax.rem(i * 512 + iota((8, 512), 1), PAIR)
        own = [image == 8 * g + iota((8, 512), 0) for g in range(3)]

        def wide(v):
            pieces = [jnp.where(m, v[t : t + 1], 0.0) for t in range(NTOK) for m in own]
            return jnp.concatenate(pieces, axis=0).astype(bf16)

        wide_hi = wide(hi)
        upper = y_hi[rows, :]
        acc[...] += nn(wide_hi, upper) + nn(wide(lo), upper) + nn(wide_hi, y_lo[rows, :])
        return 0

    lax.fori_loop(0, PADDED // 512, gather, 0)
    tok = acc[...].astype(bf16).astype(f32)
    fetch_one.wait()
    fetch_two.wait()

    h1, normed1, inverse1 = norm_fwd(tok, gains[0])
    h1_low = h1.astype(bf16)
    row_q, row_k = iota((ROWS, ROWS), 0), iota((ROWS, ROWS), 1)
    image_q, image_k = lax.rem(row_q, PAIR), lax.rem(row_k, PAIR)
    order_q = image_q * NTOK + lax.div(row_q, PAIR)
    order_k = image_k * NTOK + lax.div(row_k, PAIR)
    seen = (lax.div(image_q, FRAMES) == lax.div(image_k, FRAMES)) & (order_k <= order_q)
    root = HD**-0.5
    acc[...] = jnp.zeros_like(acc)

    def attend(m, _):
        p = nn(h1_low, one[m, :, 0:384]).astype(bf16)
        qkv[m] = p
        outs = []
        for head in range(2):
            q, k, v = (p[:, 128 * j + 64 * head : 128 * j + 64 * head + 64] for j in range(3))
            s = jnp.where(seen, nt(q, k) * root, -1e30)
            e = jnp.exp(s - jnp.max(s, -1, keepdims=True))
            w = e / jnp.sum(e, -1, keepdims=True)
            prob[m, head] = w
            outs.append(nn(w.astype(bf16), v))
        o = jnp.concatenate(outs, axis=1).astype(bf16)
        ctx[m] = o
        acc[...] += nt(o, one[m, :, 384:512])
        return 0

    lax.fori_loop(0, 4, attend, 0)
    x1 = tok + OUT_MULT * acc[...]
    h2, normed2, inverse2 = norm_fwd(x1, gains[1])
    h2_low = h2.astype(bf16)
    acc[...] = x1

    def feed(m, _):
        u = nn(h2_low, two[m, :, 0:512])
        up[m] = u
        low = gelu_parts(u)[0].astype(bf16)
        hid[m] = low
        acc[...] += nt(low, two[m, :, 512:1024])
        return 0

    lax.fori_loop(0, 4, feed, 0)
    x2 = acc[...]
    normed_out, normed3, inverse3 = norm_fwd(x2, gains[2])
    pooled = (jnp.sum(normed_out.reshape(NTOK, PAIR, D), axis=0) * (1.0 / NTOK)).astype(bf16)

    low_half = lanes < 64
    scores = [nn(pooled, one[m, :, 512:1280]) for m in range(4)]
    weight = mask[...]
    loss = jnp.zeros((PAIR, 128), f32)
    for u in range(6):
        tiles = [s[:, 128 * u : 128 * u + 128] for s in scores]
        top = jnp.maximum(jnp.maximum(tiles[0], tiles[1]), jnp.maximum(tiles[2], tiles[3]))
        left = jnp.max(jnp.where(low_half, top, -jnp.inf), -1, keepdims=True)
        right = jnp.max(jnp.where(low_half, -jnp.inf, top), -1, keepdims=True)
        top = jnp.where(low_half, left, right)
        total = sum(jnp.exp(t - top) for t in tiles)
        left = jnp.sum(jnp.where(low_half, total, 0.0), -1, keepdims=True)
        right = jnp.sum(jnp.where(low_half, 0.0, total), -1, keepdims=True)
        lse = top + jnp.log(jnp.where(low_half, left, right))
        label = jnp.where(low_half, bins[:, 2 * u : 2 * u + 1], bins[:, 2 * u + 1 : 2 * u + 2])
        real = low_half | (2 * u + 1 < DIMS)
        target = jnp.zeros((PAIR, 128), f32)
        for m, t in enumerate(tiles):
            hit = label == (lanes & 63) + 64 * m
            target = target + jnp.where(hit, t, 0.0)
            slope = weight * (jnp.exp(t - lse) - hit.astype(f32))
            dlog[m, :, 128 * u : 128 * u + 128] = jnp.where(real, slope, 0.0).astype(bf16)
        counted = real & ((lanes & 63) == 0)
        loss = loss + weight * (jnp.where(counted, lse, 0.0) - target)
    stats[...] = jnp.zeros_like(stats)
    stats[0:8] = loss[0:8] + loss[8:16] + loss[16:24]
    counts = jnp.where(lanes == 0, weight, 0.0)
    stats[8:16] = counts[0:8] + counts[8:16] + counts[16:24]
    dpooled = jnp.zeros((PAIR, D), f32)
    for m in range(4):
        dpooled = dpooled + nt(dlog[m], one[m, :, 512:1280])
    dnormed = jnp.broadcast_to(dpooled * (1.0 / NTOK), (NTOK, PAIR, D)).reshape(ROWS, D)
    dx2, dgain2 = norm_back(normed3, inverse3, gains[2], dnormed)
    dbranch = dx2.astype(bf16)
    acc[...] = jnp.zeros_like(acc)

    def feed_back(m, _):
        slope = gelu_parts(up[m])[1]
        dup = (nn(dbranch, two[m, :, 512:1024]) * slope).astype(bf16)
        lowgrad[m] = dup
        acc[...] += nt(dup, two[m, :, 0:512])
        return 0

    lax.fori_loop(0, 4, feed_back, 0)
    dx1_norm, dgain1 = norm_back(normed2, inverse2, gains[1], acc[...])
    dx1 = dx2 + dx1_norm
    dattn = dx1.astype(bf16)

    def feed_weights(h, _):
        m = 2 * h + core
        done_one[h, :, 512:1280] = tn(pooled, dlog[m]).astype(bf16)
        done_two[h, :, 0:512] = tn(h2_low, lowgrad[m]).astype(bf16)
        done_two[h, :, 512:1024] = tn(dbranch, hid[m]).astype(bf16)
        done_one[h, :, 384:512] = (tn(dattn, ctx[m]) * OUT_MULT).astype(bf16)
        return 0

    lax.fori_loop(0, 2, feed_weights, 0)
    acc[...] = jnp.zeros_like(acc)

    def attend_back(m, _):
        do = (nn(dattn, one[m, :, 384:512]) * OUT_MULT).astype(bf16)
        p = qkv[m]
        dq, dk, dv = [], [], []
        for head in range(2):
            q, k, v = (p[:, 128 * j + 64 * head : 128 * j + 64 * head + 64] for j in range(3))
            w = prob[m, head]
            d = do[:, 64 * head : 64 * head + 64]
            dp = nt(d, v)
            dv.append(tn(w.astype(bf16), d))
            ds = (w * (dp - jnp.sum(w * dp, -1, keepdims=True))).astype(bf16)
            dq.append(nn(ds, k) * root)
            dk.append(tn(ds, q) * root)
        g = jnp.concatenate([*dq, *dk, *dv], axis=1).astype(bf16)
        lowgrad[m, :, 0:384] = g
        acc[...] += nt(g, one[m, :, 0:384])
        return 0

    lax.fori_loop(0, 4, attend_back, 0)

    def attend_weights(h, _):
        done_one[h, :, 0:384] = tn(h1_low, lowgrad[2 * h + core, :, 0:384]).astype(bf16)
        return 0

    lax.fori_loop(0, 2, attend_weights, 0)
    dtok_norm, dgain0 = norm_back(normed1, inverse1, gains[0], acc[...])
    acc[...] = dx1 + dtok_norm

    send_one = pltpu.make_async_copy(done_one, one_out, sems.at[0])
    send_two = pltpu.make_async_copy(done_two, two_out, sems.at[1])
    send_one.start()
    send_two.start()
    dtok_hi = acc[...].astype(bf16)
    dtok_lo = (acc[...] - dtok_hi.astype(f32)).astype(bf16)
    same = lax.rem(iota((PAIR, ROWS), 1), PAIR) == iota((PAIR, ROWS), 0)
    token_of = (lax.div(iota((128, ROWS), 1), PAIR) == iota((128, ROWS), 0)).astype(bf16)

    def own_image(v):
        return jnp.where(same, v.reshape(-1, PAIR, ROWS), 0.0).reshape(-1, ROWS)

    def halves(v):
        hi = v.astype(bf16)
        return hi, (v - hi.astype(f32)).astype(bf16)

    def slope_of(rows, size, _):
        upper = y_hi[rows, :]
        g = own_image(nt(upper, dtok_hi) + nt(upper, dtok_lo) + nt(y_lo[rows, :], dtok_hi))
        hi, lo = halves(g)
        logit[rows, :] = nt(hi, token_of) + nt(lo, token_of)
        return 0

    over_cells(slope_of, 0)
    a = att[used, :].reshape(PIX, PAIR, 128)
    da = logit[used, :].reshape(PIX, PAIR, 128)
    logit[used, :] = (a * (da - jnp.sum(a * da, 0, keepdims=True)) * LEARN).reshape(PIX * PAIR, 128)
    turned = jnp.concatenate([logit[128 * k : 128 * k + 128, :].T[0:NTOK] for k in range(PADDED // 128)], axis=1)
    upper = turned.astype(bf16).astype(f32)
    both = jnp.concatenate([upper, turned - upper], axis=0).astype(bf16)
    sums = nn(both, y_hi[...])
    dlearner = sums[0:8] + sums[8:16] + nn(both, y_lo[...])[0:8]

    def spread(rows, size, sums):
        hi, lo = halves(att[rows, :])
        hi, lo = own_image(nn(hi, token_of)).astype(bf16), own_image(nn(lo, token_of)).astype(bf16)
        slope_hi, slope_lo = halves(logit[rows, :])
        dy = nn(hi, dtok_hi) + nn(lo, dtok_hi) + nn(hi, dtok_lo) + nn(slope_hi, learner) + nn(slope_lo, learner)
        dy = dy.reshape(size // PAIR, PAIR, D)
        dcells[rows, :] = (dy * scale).astype(bf16).reshape(size, D)
        p = part[rows, :].reshape(size // PAIR, PAIR, D)
        return sums[0] + jnp.sum(dy * p, 0), sums[1] + jnp.sum(dy, 0)

    zero = jnp.zeros((PAIR, D), f32)
    dgamma, dbeta = over_cells(spread, (zero, zero))
    dgamma, dbeta = dgamma.astype(bf16), dbeta.astype(bf16)
    dcvec = only(nt(dgamma, flat) + shifted(nt(dbeta, flat), 4), 0) * FILM
    high = dcvec.astype(bf16).astype(f32)
    rest = dcvec - high
    dsmall = jnp.concatenate([dgain0, dgain1, dgain2, dlearner, jnp.zeros((5, D), f32)], axis=0).astype(bf16)
    mine = pl.ds(pl.multiple_of(core * 1024, 1024), 1024)
    lhs = jnp.concatenate(
        [cvec, cvec_4, shifted(high, 120), shifted(rest, 120), shifted(high, 116), shifted(rest, 116)], axis=0
    )
    lhs = jnp.where(core == 0, lhs[:, 0:1024], lhs[:, 1024:2048])
    lhs = jnp.concatenate([lhs, nt(dsmall, place_of_feature(core * 1024, 1024))], axis=0).astype(bf16)
    rhs = jnp.concatenate([dgamma, dbeta, choose_lo, choose_lo, choose_hi, choose_hi, pick], axis=0)
    result = tn(lhs, rhs)
    film_rows = (iota((1024, D), 0) & 15) < 8
    dmisc[...] = jnp.where(film_rows, result * FILM, result).astype(bf16)
    send_one.wait()
    send_two.wait()


def middle(core, part, cells, misc, one, two, instr, cam, bins, mask):
    vmem = pl.BlockSpec(memory_space=pltpu.VMEM)
    return pl.pallas_call(
        middle_kernel,
        out_shape=[
            jax.ShapeDtypeStruct((PIX * PAIR, D), bf16),
            jax.ShapeDtypeStruct((1024, D), bf16),
            jax.ShapeDtypeStruct((2, D, 1280), bf16),
            jax.ShapeDtypeStruct((2, D, 1024), bf16),
            jax.ShapeDtypeStruct((16, 128), f32),
        ],
        in_specs=[pl.BlockSpec(memory_space=pltpu.SMEM)] + [vmem] * 3 + [ANY] * 2 + [vmem] * 4,
        out_specs=[vmem, vmem, ANY, ANY, vmem],
        scratch_shapes=[
            pltpu.VMEM((4, D, 1280), bf16),
            pltpu.VMEM((4, D, 1024), bf16),
            pltpu.VMEM((2, D, 1280), bf16),
            pltpu.VMEM((2, D, 1024), bf16),
            pltpu.VMEM((PADDED, D), bf16),
            pltpu.VMEM((PADDED, D), bf16),
            pltpu.VMEM((PADDED, 128), f32),
            pltpu.VMEM((PADDED, 128), f32),
            pltpu.VMEM((4, ROWS, 384), bf16),
            pltpu.VMEM((4, 2, ROWS, ROWS), f32),
            pltpu.VMEM((4, ROWS, 128), bf16),
            pltpu.VMEM((4, ROWS, 512), f32),
            pltpu.VMEM((4, ROWS, 512), bf16),
            pltpu.VMEM((ROWS, D), f32),
            pltpu.VMEM((4, PAIR, 768), bf16),
            pltpu.VMEM((4, ROWS, 512), bf16),
            pltpu.SemaphoreType.DMA((2,)),
        ],
        compiler_params=pltpu.CompilerParams(vmem_limit_bytes=VMEM_BYTES),
    )(core, part, cells, misc, one, two, instr, cam, bins, mask)


STEPS = 4
BLOCK = (PIX, PAIR, WIDTH)


def tap_places():
    row, col = iota((OWNERS * 128, WIDTH), 0), iota((OWNERS * 128, WIDTH), 1)
    return (((row >> 7) * 24 + (row & 127) == col) & ((row & 127) < 24)).astype(bf16)


def to_cells(frames, cells):
    rows = 8 * PAIR
    at, of = iota((rows, rows), 0), iota((rows, rows), 1)
    turn = (lax.rem(at, PAIR) * 8 + lax.div(at, PAIR) == of).astype(bf16)
    for first in (*range(0, PIX - 8, 8), PIX - 8):
        block = frames[:, :, first : first + 8, :].reshape(rows, D)
        cells[first * PAIR : first * PAIR + rows, :] = nn(turn, block).astype(bf16)


def fill_shards(conv, cond, small, attn, mlp, head, camera, core, shards, staged, tap_tile, cam):
    shards[0][...] = conv[:, 0:D].astype(bf16)
    shards[1][...] = conv[:, D : 2 * D].astype(bf16)
    tap_tile[...] = jnp.zeros_like(tap_tile)
    tap_tile[0:24, 0:9] = conv[:, 2 * D :]
    shards[2][...] = tap_tile[...].T[0:16].astype(bf16)
    staged[...] = jnp.zeros_like(staged)
    for i in range(3):
        staged[4 * i : 4 * i + 4, :] = cond[:, D * i : D * i + D]
    staged[12:16, 0:SMALL_AT] = cond[:, 3 * D :]
    staged[12:16, SMALL_AT : SMALL_AT + 11] = small[...]
    shards[3][...] = staged[...].astype(bf16)
    for j in range(4):
        shards[4][:, 128 * j : 128 * j + 128] = attn[j].astype(bf16)
    for k in range(0, DIMS - 1, 2):
        both = jnp.concatenate([head[k], head[k + 1]], axis=1)
        shards[4][:, 512 + 64 * k : 640 + 64 * k] = both.astype(bf16)
    last = jnp.concatenate([head[DIMS - 1], jnp.zeros((16, 64), f32)], axis=1)
    shards[4][:, 1152:1280] = last.astype(bf16)
    for j in range(2):
        shards[5][:, 512 * j : 512 * j + 512] = mlp[j].astype(bf16)
    row = iota((PAIR, 128), 0)
    found = jnp.zeros((PAIR, 128), jnp.int32)
    for i in range(PAIR // 2):
        found = jnp.where(row == core * (PAIR // 2) + i, camera[i], found)
    cam[...] = found


def forward_kernel(plan, *refs):
    n = len(plan)
    frames, camera = refs[0:2]
    masters = refs[2 : 2 + n]
    refs = refs[2 + n :]
    cam2, cells_out, project_out, taps_out, misc_out, one_out, two_out, pre_out, deep_out, total_out = refs[:10]
    frames2, cells, expand, project, slabs, taps, places, act, pre, deep, part, other = refs[10:22]
    shards, staged, tap_tile, cam = refs[22 : 22 + n], refs[22 + n], refs[23 + n], refs[24 + n]
    send, recv, fsend, frecv, local, kept, swap_send, swap_recv = refs[25 + n :]
    me = here()
    count = announce(me)
    fill_shards(*masters, camera, me["c"], shards, staged, tap_tile, cam)
    meet(count)
    swaps = []
    for i, (src, out) in enumerate(((frames, frames2), (cam, cam2))):
        mine = pltpu.make_async_copy(src, out.at[me["c"]], local.at[n + i])
        mine.start()
        swaps += [mine, remote(src, out.at[me["c"]], swap_send.at[i], swap_recv.at[i], "c", 1 - me["c"])]
    outs = (expand, project, slabs, misc_out, one_out, two_out)
    jobs = [
        Gather(me, dims, order, shards[b], outs[b], send.at[b], recv.at[b], fsend.at[b], frecv.at[b], local.at[b])
        for b, (dims, order) in enumerate(plan)
    ]
    early, late, rest = (jobs[0], jobs[2]), (jobs[1],), jobs[3:]
    first = jobs[:3]

    def relay(some, phase):
        for job in some:
            job.relay(phase)

    def finish(some, phase):
        for job in some:
            job.finish(phase)

    for job in jobs:
        job.begin()
    relay(first, 0)
    finish(first, 0)
    clear_borders(act)
    places[...] = tap_places()
    relay(first, 1)
    finish(first, 1)
    relay(rest, 0)
    finish(rest, 0)
    part[...] = jnp.zeros_like(part)
    swaps[0].wait()
    swaps[1].wait()
    to_cells(frames2, cells)
    saves = []

    def save(src, dst, number):
        copy = pltpu.make_async_copy(src, dst, kept.at[number])
        copy.start()
        saves.append(copy)

    save(cells, cells_out, 0)
    spans, leaves = [None] * STEPS, []
    for step in range(STEPS):
        slot = step % 2
        at = ring(me["x"], (0, -1, 1, 2)[step])
        if step == 1:
            relay(early, 2)
            relay(late, 2)
        if step == 3:
            finish(early, 2)
        if step >= 2:
            for copy in spans[step - 2]:
                copy.wait()
        weight = expand[at].reshape(WIDTH, D)
        tap = slabs[at].reshape(OWNERS, 16, 128)
        side = jnp.concatenate([tap[i] for i in range(OWNERS)], axis=1)
        taps[at] = nn(side, places[...]) * (8.0 / 3.0)

        def enter(i, _, weight=weight, slot=slot):
            rows = pl.ds(pl.multiple_of(i * SPAN, SPAN), SPAN)
            e = (nt(cells[rows, :], weight) * EXPAND).reshape(CHUNK * MAP, PAIR, WIDTH)
            pre[slot, pl.ds(i * CHUNK * MAP, CHUNK * MAP)] = e
            act[pl.ds(1 + i * CHUNK, CHUNK)] = (e * sigmoid(e)).reshape(CHUNK, MAP, PAIR, WIDTH)
            return 0

        lax.fori_loop(0, MAP // CHUNK, enter, 0)
        out = [pltpu.make_async_copy(pre.at[slot], pre_out.at[at], kept.at[3 + 2 * step])]
        out[0].start()
        if step == 0:
            relay(rest, 1)
        if step == 2:
            relay(rest, 2)

        def mix(row, subs, cols, slot=slot, at=at):
            near = act[pl.ds(row, 3), :, subs, cols]
            tap = [jnp.broadcast_to(taps[at, t : t + 1, cols], (8, 128)) for t in range(9)]
            for col in range(MAP):
                total = None
                for t in range(9):
                    p = col + t % 3 - 1
                    if 0 <= p < MAP:
                        term = near[t // 3, p] * tap[t]
                        total = term if total is None else total + term
                deep[slot, row * MAP + col, subs, cols] = total

        each_block(mix)
        out.append(pltpu.make_async_copy(deep.at[slot], deep_out.at[at], kept.at[4 + 2 * step]))
        out[1].start()
        spans[step] = out
        if step == 0:
            finish(rest, 1)
        if step == 3:
            finish(rest, 2)

        def leave(i, _, at=at, slot=slot):
            back = project[at].reshape(WIDTH, D)
            rows = pl.ds(pl.multiple_of(i * SPAN, SPAN), SPAN)
            v = deep[slot, pl.ds(i * CHUNK * MAP, CHUNK * MAP)].reshape(SPAN, WIDTH)
            part[rows, :] += nn((v * sigmoid(v)).astype(bf16), back) * PROJECT
            return 0

        leaves.append(leave)
        if step == 1:
            finish(late, 2)
            save(project, project_out, 1)
            lax.fori_loop(0, MAP // CHUNK, leaves[0], 0)
        if 0 < step < STEPS - 1:
            lax.fori_loop(0, MAP // CHUNK, leave, 0)
    save(taps, taps_out, 2)
    trades = []
    for i in range(MAP // CHUNK):
        leave(i, 0)
        rows = pl.ds(i * SPAN, SPAN)
        trades.append(
            remote(part.at[rows], other.at[rows], swap_send.at[2 + i], swap_recv.at[2 + i], "c", 1 - me["c"])
        )
    for i, copy in enumerate(trades):
        copy.wait()
        rows = slice(i * SPAN, (i + 1) * SPAN)
        other[rows, :] += part[rows, :]
        save(other.at[rows], total_out.at[rows], 3 + 2 * STEPS + i)
    for step in (STEPS - 2, STEPS - 1):
        saves += spans[step]
    for job in jobs:
        job.end()
    for copy in saves + swaps[2:]:
        copy.wait()


def forward(frames, camera, masters, plan, collective_id):
    n = len(plan)
    maps = jax.ShapeDtypeStruct((STEPS, *BLOCK), f32)
    shape = jax.ShapeDtypeStruct
    full = [shape((*lead(dims), *slab), bf16) for slab, (dims, _) in zip(SLABS, plan)]
    rows = PIX * PAIR
    return pl.pallas_call(
        functools.partial(forward_kernel, plan),
        out_shape=[
            shape((2, PAIR, 128), jnp.int32),
            shape((rows, D), bf16),
            full[1],
            shape((STEPS, 16, WIDTH), f32),
            *full[3:],
            maps,
            maps,
            shape((rows, D), f32),
        ],
        in_specs=[ANY, pl.BlockSpec(memory_space=pltpu.SMEM)] + [INVMEM] * n,
        out_specs=[ANY] * 10,
        scratch_shapes=[
            pltpu.VMEM((2, *frames.shape), bf16),
            pltpu.VMEM((rows, D), bf16),
            pltpu.VMEM(full[0].shape, bf16),
            pltpu.VMEM(full[1].shape, bf16),
            pltpu.VMEM(full[2].shape, bf16),
            pltpu.VMEM((STEPS, 16, WIDTH), f32),
            pltpu.VMEM((OWNERS * 128, WIDTH), bf16),
            pltpu.VMEM((MAP + 2, MAP, PAIR, WIDTH), f32),
            pltpu.VMEM((2, *BLOCK), f32),
            pltpu.VMEM((2, *BLOCK), f32),
            pltpu.VMEM((rows, D), f32),
            pltpu.VMEM((rows, D), f32),
            *[pltpu.VMEM(slab, bf16) for slab in SLABS],
            pltpu.VMEM((16, D), f32),
            pltpu.VMEM((128, 128), f32),
            pltpu.VMEM((PAIR, 128), jnp.int32),
            pltpu.SemaphoreType.DMA((n, 3, 4)),
            pltpu.SemaphoreType.DMA((n, 3, 4)),
            pltpu.SemaphoreType.DMA((n, 7)),
            pltpu.SemaphoreType.DMA((n, 7)),
            pltpu.SemaphoreType.DMA((n + 2,)),
            pltpu.SemaphoreType.DMA((3 + 2 * STEPS + MAP // CHUNK,)),
            pltpu.SemaphoreType.DMA((2 + MAP // CHUNK,)),
            pltpu.SemaphoreType.DMA((2 + MAP // CHUNK,)),
        ],
        compiler_params=pltpu.CompilerParams(
            collective_id=collective_id, has_side_effects=True, vmem_limit_bytes=VMEM_BYTES
        ),
    )(frames, camera, *masters)


class Blocks:
    def __init__(self, me, dims, order, full, room, send, recv):
        self.me, self.dims, self.order, self.full = me, dims, order, full
        self.halves, self.wholes, self.slabs, self.last = room
        self.send, self.recv = send, recv
        self.going = [None] * STEPS
        self.sent = []

    def at(self, step, **more):
        return {"x": ring(self.me["x"], BACK[step]), **more}

    def push(self, step, slot, src, box, axis, move):
        return remote(src, box, self.send.at[step, slot], self.recv.at[step, slot], axis, ring(self.me[axis], move))

    def launch(self, step):
        a, b, _ = self.order
        self.going[step] = [
            self.push(
                step, side, self.full.at[spot(self.dims, self.at(step, **{a: ring(self.me[a], 2)}, **half(b, side)))],
                self.halves.at[step, side], a, 1 - 2 * side,
            )
            for side in range(2)
        ]

    def relay(self, step):
        a, b, _ = self.order
        for side, move in ((0, 1), (1, -1)):
            self.going[step][side].wait()
            pos = {a: ring(self.me[a], move)}
            add_into(self.full, self.dims, self.at(step, **pos, **half(b, side)), [self.halves.at[step, side]])
            where = self.full.at[spot(self.dims, self.at(step, **pos))]
            self.going[step].append(self.push(step, 2 + side, where, self.wholes.at[step, side], a, move))

    def middle(self, step):
        a, b, _ = self.order
        for copy in self.going[step][2:]:
            copy.wait()
        own = {a: self.me[a]}
        add_into(self.full, self.dims, self.at(step, **own), [self.wholes.at[step, side] for side in range(2)])
        self.going[step] = [
            self.push(
                step, 4 + i, self.full.at[spot(self.dims, self.at(step, **own, **{b: ring(self.me[b], move)}))],
                self.slabs.at[step, i], b, move,
            )
            for i, move in enumerate((2, 1, -1))
        ]

    def finish(self, step):
        a, b, _ = self.order
        for copy in self.going[step]:
            copy.wait()
        index = spot(self.dims, self.at(step, **{a: self.me[a], b: self.me[b]}))
        total = self.full[index].astype(f32)
        for i in range(3):
            total = total + self.slabs[step, i].astype(f32)
        if BACK[step] != 0:
            self.full[index] = total.astype(bf16)
            self.sent.append(self.push(step, 7, self.full.at[index], self.last.at[step], "x", BACK[step]))
        return total

    def close(self, total):
        for copy in self.sent:
            copy.wait()
        for i in range(STEPS - 1):
            total = total + self.last[i].astype(f32)
        return total

    @staticmethod
    def scratch(dims, order, slab):
        rest = without(without(dims, "x"), order[0])
        small = free_sizes(rest, half(order[1], 0))
        shapes = [
            (*lead(dims), *slab), (STEPS, 2, *small, *slab), (STEPS, 2, *lead(rest), *slab), (STEPS, 3, *slab),
            (STEPS - 1, *slab),
        ]
        return [pltpu.VMEM(s, bf16) for s in shapes]


BACK = (2, 1, -1, 0)


def backward_kernel(plan, *refs):
    n = len(plan)
    cells_in, dcells_in, project_in, taps_in, pre_in, deep_in, stats = refs[:7]
    parts = refs[7 : 7 + n - 3]
    refs = refs[4 + n :]
    stats_out, outs = refs[0], refs[1 : 1 + n]
    refs = refs[1 + n :]
    cells, dcells, project, taps, places, pre, deep, spread, mid, dpre, acc = refs[:11]
    refs = refs[11:]
    blocks_room, rest_room = refs[:15], refs[15 : 15 + 13 * (n - 3)]
    tile, tile_box, bsend, brecv, send, recv, local, kept, tsend, trecv = refs[15 + 13 * (n - 3) :]
    me = here()
    loads = []
    for i, (src, dst) in enumerate(((cells_in, cells), (dcells_in, dcells), (project_in, project), (taps_in, taps))):
        copy = pltpu.make_async_copy(src, dst, kept.at[i])
        copy.start()
        loads.append(copy)

    def fetch(step):
        at = ring(me["x"], BACK[step])
        pair = []
        for i, (src, dst) in enumerate(((pre_in, pre), (deep_in, deep))):
            copy = pltpu.make_async_copy(src.at[at], dst.at[step % 2], kept.at[4 + 2 * step + i])
            copy.start()
            pair.append(copy)
        return pair

    maps = [fetch(0), fetch(1), None, None]
    meet(announce(me, wide=True))
    rest = []
    for b, (dims, order) in enumerate(plan[3:]):
        own = rest_room[13 * b : 13 * b + 13]
        boxes = [own[1:5], own[5:9], own[9:13]]
        rest.append(Scatter(me, dims, order, parts[b], own[0], boxes, send.at[b], recv.at[b], local.at[b]))
    first = [
        Blocks(me, dims, order, blocks_room[5 * b], blocks_room[5 * b + 1 : 5 * b + 5], bsend.at[b], brecv.at[b])
        for b, (dims, order) in enumerate(plan[:3])
    ]
    for job in rest:
        job.begin()
    clear_borders(spread)
    places[...] = tap_places()
    for copy in loads:
        copy.wait()
    square = jnp.zeros((8, 128), f32)

    def close_rest(square):
        for b, job in enumerate(rest):
            total = job.finish(2)
            outs[3 + b][...] = total
            square = square + folded(total * total)
        return square

    for step in range(STEPS):
        slot = step % 2
        at = ring(me["x"], BACK[step])
        for copy in maps[step]:
            copy.wait()
        back = project[at].reshape(WIDTH, D)

        def enter(i, _, back=back, slot=slot):
            rows = pl.ds(pl.multiple_of(i * SPAN, SPAN), SPAN)
            dmid = nt(dcells[rows, :], back) * PROJECT
            v = deep[slot, pl.ds(i * CHUNK * MAP, CHUNK * MAP)].reshape(SPAN, WIDTH)
            s = sigmoid(v)
            m = v * s
            mid[rows, :] = m.astype(bf16)
            spread[pl.ds(1 + i * CHUNK, CHUNK)] = (dmid * (s + m * (1.0 - s))).reshape(CHUNK, MAP, PAIR, WIDTH)
            return 0

        lax.fori_loop(0, MAP // CHUNK, enter, 0)
        if step > 0:
            for job in first:
                job.relay(step - 1)
        if step > 1:
            for job in first:
                job.finish(step - 2)
        if step == 2:
            for job in rest:
                job.finish(0)
        if step == 3:
            for job in rest:
                job.finish(1)
        acc[...] = jnp.zeros_like(acc)

        def mix(row, subs, cols, slot=slot, at=at):
            near = spread[pl.ds(row, 3), :, subs, cols]
            tap = [jnp.broadcast_to(taps[at, t : t + 1, cols], (8, 128)) for t in range(9)]
            sums = [None] * 9
            for col in range(MAP):
                e = pre[slot, row * MAP + col, subs, cols]
                s = sigmoid(e)
                a = e * s
                total = None
                for t in range(9):
                    p = col + 1 - t % 3
                    if 0 <= p < MAP:
                        g = near[2 - t // 3, p]
                        term = g * tap[t]
                        total = term if total is None else total + term
                        term = g * a
                        sums[t] = term if sums[t] is None else sums[t] + term
                dpre[row * MAP + col, subs, cols] = total * (s + a * (1.0 - s))
            for t in range(9):
                acc[t, :, cols] += sums[t]

        each_block(mix)
        if step + 2 < STEPS:
            maps[step + 2] = fetch(step + 2)
        if step == 0:
            for job in rest:
                job.relay(0)
        if step == 2:
            for job in rest:
                job.relay(1)
        if step > 0:
            for job in first:
                job.middle(step - 1)
        owned = (2, 4, 2, 24, D)
        low = dpre[...].reshape(PIX * PAIR, WIDTH).astype(bf16)
        first[0].full[at] = (tn(low, cells[...]) * EXPAND).astype(bf16).reshape(owned)
        first[1].full[at] = (tn(mid[...], dcells[...]) * PROJECT).astype(bf16).reshape(owned)
        dtaps = jnp.concatenate([jnp.sum(acc[...], axis=1) * (8.0 / 3.0), jnp.zeros((7, WIDTH), f32)], axis=0)
        side = nt(dtaps.astype(bf16), places[...]).astype(bf16)
        for i in range(OWNERS):
            first[2].full[at, i // 8, (i // 2) % 4, i % 2] = side[:, 128 * i : 128 * i + 128]
        for job in first:
            job.launch(step)
    for job in first:
        job.finish(STEPS - 2)
    square = close_rest(square)
    for job in first:
        job.relay(STEPS - 1)
    for job in first:
        job.middle(STEPS - 1)
    for b, job in enumerate(first):
        total = job.close(job.finish(STEPS - 1))
        outs[b][...] = total
        square = square + folded(total * total)
    lines = [jnp.sum(v, 0, keepdims=True) for v in (stats[0:8], stats[8:16], square)]
    tile[0] = jnp.concatenate([*lines, jnp.zeros((5, 128), f32)], axis=0)
    number = 0
    for phase, (one, two) in enumerate((("c", "x"), ("y", "z"))):
        spans = [range(2 if a == "c" else RING) for a in (one, two)]
        moves = [{a: k for a, k in ((one, j), (two, k)) if k} for j in spans[0] for k in spans[1] if j or k]
        copies = []
        for move in moves:
            copy = pltpu.make_async_remote_copy(
                src_ref=tile.at[phase], dst_ref=tile_box.at[number], send_sem=tsend.at[number],
                recv_sem=trecv.at[number], device_id=moved(me, move), device_id_type=MESH_ID,
            )
            copy.start()
            copies.append(copy)
            number += 1
        for copy in copies:
            copy.wait()
        total = tile[phase]
        for i in range(number - len(copies), number):
            total = total + tile_box[i]
        tile[phase + 1] = total
    stats_out[...] = tile[2]


def backward(cells, dcells, project, taps, pre, deep, stats, parts, slabs, plan, collective_id):
    n = len(plan)
    shape = jax.ShapeDtypeStruct
    rows = PIX * PAIR
    room = []
    for (dims, order), slab in zip(plan[:3], slabs[:3]):
        room += Blocks.scratch(dims, order, slab)
    for (dims, order), slab in zip(plan[3:], slabs[3:]):
        room += Scatter.scratch(dims, order, slab, bf16)
    return pl.pallas_call(
        functools.partial(backward_kernel, plan),
        out_shape=[shape((8, 128), f32)] + [shape(s, f32) for s in slabs],
        in_specs=[ANY] * 6 + [INVMEM] + [ANY] * (n - 3),
        out_specs=[INVMEM] * (1 + n),
        scratch_shapes=[
            pltpu.VMEM((rows, D), bf16),
            pltpu.VMEM((rows, D), bf16),
            pltpu.VMEM(project.shape, bf16),
            pltpu.VMEM(taps.shape, f32),
            pltpu.VMEM((OWNERS * 128, WIDTH), bf16),
            pltpu.VMEM((2, *BLOCK), f32),
            pltpu.VMEM((2, *BLOCK), f32),
            pltpu.VMEM((MAP + 2, MAP, PAIR, WIDTH), f32),
            pltpu.VMEM((rows, WIDTH), bf16),
            pltpu.VMEM(BLOCK, f32),
            pltpu.VMEM((9, 8, WIDTH), f32),
            *room,
            pltpu.VMEM((3, 8, 128), f32),
            pltpu.VMEM((22, 8, 128), f32),
            pltpu.SemaphoreType.DMA((3, STEPS, 8)),
            pltpu.SemaphoreType.DMA((3, STEPS, 8)),
            pltpu.SemaphoreType.DMA((n - 3, 3, 4)),
            pltpu.SemaphoreType.DMA((n - 3, 3, 4)),
            pltpu.SemaphoreType.DMA((n - 3,)),
            pltpu.SemaphoreType.DMA((4 + 2 * STEPS,)),
            pltpu.SemaphoreType.DMA((22,)),
            pltpu.SemaphoreType.DMA((22,)),
        ],
        compiler_params=pltpu.CompilerParams(
            collective_id=collective_id, has_side_effects=True, vmem_limit_bytes=VMEM_BYTES
        ),
    )(cells, dcells, project, taps, pre, deep, stats, *parts)


IMAGES = 12
DP_MP = NAMES
DP = ("dp_0", "dp_1", "dp_2")
MP = ("mp_0", "mp_1")
CLIP_NORM = 0.02
BETA_ONE = 0.9
BETA_TWO = 0.999
ADAM_EPS = 1e-08
DECAY = 0.01
RATES = (0.1, 0.1, 0.2, 0.05, 0.05, 0.2)


def adam_kernel(count_ref, totals, gexpand, gproject, gtaps, gmisc, gone, gtwo, *refs):
    states = [refs[3 * i : 3 * i + 3] for i in range(6)]
    loss_ref, norm_ref = refs[18:20]
    outs = [refs[20 + 3 * i : 23 + 3 * i] for i in range(6)]

    def total(line):
        return jnp.sum(totals[line : line + 1, :], axis=(0, 1), keepdims=True)

    scored = 0.5 * total(1)
    norm = jnp.sqrt(total(2)) / scored
    factor = jnp.minimum(1.0, CLIP_NORM / norm) / scored
    loss_ref[0] = (0.5 * total(0) / scored)[0, 0]
    norm_ref[0] = norm[0, 0]
    steps = jnp.full((1, 1), count_ref[0], jnp.int32).astype(f32)
    z = steps * math.log(BETA_TWO)
    grown_two = -z * (1.0 + z / 2.0 * (1.0 + z / 3.0 * (1.0 + z / 4.0 * (1.0 + z / 5.0))))
    grown_one = 1.0 - jnp.exp(steps * math.log(BETA_ONE))

    def update(group, index, grad):
        master, first, second = (ref[index] for ref in states[group])
        grad = grad * factor
        first = BETA_ONE * first + (1.0 - BETA_ONE) * grad
        second = BETA_TWO * second + (1.0 - BETA_TWO) * grad * grad
        step = first / grown_one / (jnp.sqrt(second / grown_two) + ADAM_EPS) + DECAY * master
        outs[group][0][index] = master - RATES[group] * step
        outs[group][1][index] = first
        outs[group][2][index] = second

    every = slice(None)
    update(0, (every, slice(0, D)), gexpand[...])
    update(0, (every, slice(D, 2 * D)), gproject[...])
    taps = jnp.concatenate([gtaps[...], jnp.zeros((112, 128), f32)], axis=0).T
    update(0, (every, slice(2 * D, 2 * D + 9)), taps[0:24, 0:9])
    for i in range(3):
        update(1, (every, slice(D * i, D * i + D)), gmisc[4 * i : 4 * i + 4, :])
    update(1, (every, slice(3 * D, 2 * D + TABLE)), gmisc[12:16, 0:SMALL_AT])
    update(2, (every, every), gmisc[12:16, SMALL_AT : SMALL_AT + 11])
    for j in range(4):
        update(3, j, gone[:, 128 * j : 128 * j + 128])
    for j in range(2):
        update(4, j, gtwo[:, 512 * j : 512 * j + 512])
    for k in range(DIMS):
        update(5, k, gone[:, 512 + 64 * k : 576 + 64 * k])


def adam(step_count, totals, grads, states):
    smem = pl.BlockSpec(memory_space=pltpu.SMEM)
    one = jax.ShapeDtypeStruct((1,), f32)
    return pl.pallas_call(
        adam_kernel,
        out_shape=[one, one] + [jax.ShapeDtypeStruct(s.shape, f32) for s in states],
        in_specs=[smem] + [INVMEM] * (1 + len(grads) + len(states)),
        out_specs=[smem, smem] + [INVMEM] * len(states),
    )(step_count, totals, *grads, *states)


def per_device(
    frames, camera_ids, instruction_ids, action_bins, final_mask, step_count,
    conv_w, conv_m1, conv_m2, cond_w, cond_m1, cond_m2, small_w, small_m1, small_m2,
    attn_w, attn_m1, attn_m2, mlp_w, mlp_m1, mlp_m2, head_w, head_m1, head_m2,
):
    core, high = lax.axis_index("mp_1"), lax.axis_index("mp_0")
    states = [
        *[v.T for v in (conv_w, conv_m1, conv_m2, cond_w, cond_m1, cond_m2, small_w, small_m1, small_m2)],
        *(attn_w, attn_m1, attn_m2, mlp_w, mlp_m1, mlp_m2),
        *[v.transpose(1, 0, 2) for v in (head_w, head_m1, head_m2)],
    ]
    cam2, cells, project, taps, misc_all, one_all, two_all, pre, deep, part = forward(
        frames, camera_ids, states[0::3], GATHER, 1
    )
    instr = jnp.repeat(lax.dynamic_slice_in_dim(instruction_ids, high * 4, 4), FRAMES)
    bins = jnp.pad(
        lax.dynamic_slice_in_dim(action_bins, high * PAIR, PAIR), ((0, 0), (0, 128 - DIMS)), constant_values=-1
    )
    mask = lax.dynamic_slice_in_dim(final_mask, high * PAIR, PAIR).astype(f32)
    dcells, dmisc, done_one, done_two, stats = middle(
        core[None],
        part,
        cells,
        misc_all.reshape(2048, D),
        one_all.reshape(4, D, 1280),
        two_all.reshape(4, D, 1024),
        jnp.broadcast_to(instr[:, None], (PAIR, 128)),
        cam2,
        bins,
        jnp.broadcast_to(mask[:, None], (PAIR, 128)),
    )
    parts = [
        g.reshape(*lead(dims), *slab)
        for g, slab, (dims, _) in zip((dmisc, done_one, done_two), SLABS[3:], SCATTER[3:])
    ]
    totals, *grads = backward(cells, dcells, project, taps, pre, deep, stats, parts, SLABS, SCATTER, 2)
    loss, norm, *new = adam(step_count, totals, grads, states)
    new = [v.T for v in new[:9]] + new[9:15] + [v.transpose(1, 0, 2) for v in new[15:]]
    return loss.reshape(()), norm.reshape(()), *new


def solution(mesh):
    torus = Mesh(mesh.devices.reshape(2, 4, 4, 2, 2), NAMES)
    weights = (
        *[P(None, DP_MP)] * 9,
        *[P(None, DP, MP)] * 6,
        *[P(DP, None, MP)] * 3,
    )
    data = (P(DP_MP, None, None), P(DP_MP), P(DP), P(DP, None), P(DP), P())
    return jax.shard_map(
        per_device, mesh=torus, in_specs=(*data, *weights), out_specs=(P(), P(), *weights), check_vma=False
    )
```

```python
import functools
import itertools
import math
import typing

import jax
import jax.numpy as jnp
from jax import lax
from jax.experimental import pallas as pl
from jax.experimental.pallas import tpu as pltpu
from jax.sharding import Mesh
from jax.sharding import PartitionSpec as P

f32 = jnp.float32
bf16 = jnp.bfloat16
NAMES = ("dp_0", "dp_1", "dp_2", "mp_0", "mp_1")
SIZES = {"l": 2, "z": 4, "x": 4, "h": 2, "c": 2}
RING = 4
MESH_ID = pl.DeviceIdType.MESH
ANY = pl.BlockSpec(memory_space=pl.ANY)
INVMEM = pl.BlockSpec(memory_space=pltpu.VMEM)


class Along(typing.NamedTuple):
    low: typing.Any
    high: typing.Any


def here():
    low, z, x, high, core = (lax.axis_index(n) for n in NAMES)
    me = {"c": {0: core, 1: 1 - core}}
    for axis, at in (("x", x), ("y", high * 2 + low), ("z", z)):
        me[axis] = {}
        for step in (0, 1, 2, -1):
            pos = lax.rem(at + step + RING, RING) if step else at
            if axis == "y":
                pos = Along(lax.rem(pos, 2), lax.div(pos, 2)) if step else Along(low, high)
            me[axis][step] = pos
    return me


def device_of(axis, at):
    if axis == "y":
        return {"dp_0": at.low, "mp_0": at.high}
    return {{"x": "dp_2", "z": "dp_1", "c": "mp_1"}[axis]: at}


def extents(dims, at):
    found = []
    for d in dims:
        if d in at:
            v = at[d]
        elif d in "lh" and "y" in at:
            v = at["y"].low if d == "l" else at["y"].high
        else:
            v = (0, SIZES[d])
        found.append(v if isinstance(v, tuple) else (v, None))
    return found


def spot(dims, at):
    return tuple(start if size is None else pl.ds(start, size) for start, size in extents(dims, at))


def free_sizes(dims, at):
    return tuple(size for _, size in extents(dims, at) if size is not None)


def half(axis, side):
    return {"h": side} if axis == "y" else {axis: (2 * side, 2)}


def without(dims, axis):
    return tuple(d for d in dims if d not in ("lh" if axis == "y" else axis))


def lead(dims):
    return tuple(SIZES[d] for d in dims)


def announce(me, wide=False):
    barrier = pltpu.get_barrier_semaphore()
    peers = [{a: k} for a in "xyz" for k in range(1, RING)] + [{"c": 1}]
    if wide:
        peers += [{"x": k, "c": 1} for k in range(1, RING)]
        peers += [{"y": j, "z": k} for j in range(1, RING) for k in range(1, RING)]
    for moves in peers:
        pl.semaphore_signal(barrier, inc=1, device_id=moved(me, moves), device_id_type=MESH_ID)
    return len(peers)


def moved(me, moves):
    found = {}
    for axis, k in moves.items():
        found.update(device_of(axis, me[axis][-1 if k == 3 else k]))
    return found


def meet(count):
    pl.semaphore_wait(pltpu.get_barrier_semaphore(), count)


def remote(src, dst, send, recv, axis, at):
    copy = pltpu.make_async_remote_copy(
        src_ref=src, dst_ref=dst, send_sem=send, recv_sem=recv, device_id=device_of(axis, at), device_id_type=MESH_ID
    )
    copy.start()
    return copy


class Gather:
    def __init__(self, me, dims, order, shard, out, send, recv, fsend, frecv, local):
        self.me, self.dims, self.order, self.shard, self.out = me, dims, order, shard, out
        self.send, self.recv, self.fsend, self.frecv, self.local = send, recv, fsend, frecv, local
        self.forwards = []

    def region(self, phase, step=0, part=None):
        at = {a: self.me[a][0] for a in self.order[phase:]}
        at[self.order[phase]] = self.me[self.order[phase]][step]
        if "c" in self.dims:
            at["c"] = self.me["c"][0]
        if part is not None:
            at.update(half(self.order[0], part))
        return self.out.at[spot(self.dims, at)]

    def push(self, phase, slot, where, step):
        axis = self.order[phase]
        src = self.shard if phase == 0 else where
        return remote(src, where, self.send.at[phase, slot], self.recv.at[phase, slot], axis, self.me[axis][step])

    def forward(self, number, where):
        if "c" in self.dims:
            self.forwards.append(
                remote(where, where, self.fsend.at[number], self.frecv.at[number], "c", self.me["c"][1])
            )

    def begin(self):
        self.kept = pltpu.make_async_copy(self.shard, self.region(0), self.local)
        self.kept.start()
        self.launch(0)

    def launch(self, phase):
        where = self.region(phase)
        self.going = [self.push(phase, 0, where, 1), self.push(phase, 1, where, -1)]
        if phase == 0:
            self.going.append(self.push(0, 2, where, 2))

    def relay(self, phase):
        for slot, step in ((0, 1), (1, -1)):
            self.going[slot].wait()
            if phase > 0:
                self.going.append(self.push(phase, 2 + slot, self.region(phase, -step, slot), step))
                self.forward(3 * phase - 2 + slot, self.region(phase, -step))

    def finish(self, phase, launch=True):
        for copy in self.going[2:]:
            copy.wait()
        if phase == 0:
            self.kept.wait()
            if "c" in self.dims:
                at = {a: self.me[a][0] for a in (*self.order[1:], "c")}
                self.forward(0, self.out.at[spot(self.dims, at)])
        else:
            self.forward(3 * phase, self.region(phase, 2))
        if phase < 2 and launch:
            self.launch(phase + 1)

    def end(self):
        for copy in self.forwards:
            copy.wait()


def add_into(full, dims, at, others):
    found = extents(dims, at)
    for place in itertools.product(*(range(size) for _, size in found if size is not None)):
        index, along = [], iter(place)
        for start, size in found:
            index.append(start if size is None else start + next(along))
        index = tuple(index)
        total = full[index].astype(f32)
        for o in others:
            total = total + o[place].astype(f32)
        full[index] = total.astype(full.dtype)


def folded(v):
    total = None
    for r in range(0, v.shape[0], 8):
        for c in range(0, v.shape[1], 128):
            part = v[r : r + 8, c : c + 128]
            total = part if total is None else total + part
    return total


class Scatter:
    def __init__(self, me, dims, order, part, full, boxes, send, recv, local):
        self.me, self.dims, self.order, self.part, self.full, self.boxes = me, dims, order, part, full, boxes
        self.send, self.recv, self.local = send, recv, local

    def at(self, phase, step, side=None):
        at = {a: self.me[a][0] for a in self.order[:phase]}
        axis = self.order[phase]
        at[axis] = self.me[axis][step]
        if side is not None:
            at.update(half(self.order[phase + 1], side))
        return at

    def push(self, phase, slot, src, step):
        axis = self.order[phase]
        return remote(
            src, self.boxes[phase][slot], self.send.at[phase, slot], self.recv.at[phase, slot], axis, self.me[axis][step]
        )

    def begin(self):
        self.kept = pltpu.make_async_copy(self.part, self.full, self.local)
        self.kept.start()
        self.launch(0)

    def launch(self, phase):
        src = self.part if phase == 0 else self.full
        if phase < 2:
            self.going = [
                self.push(phase, side, src.at[spot(self.dims, self.at(phase, 2, side))], 1 - 2 * side) for side in range(2)
            ]
        else:
            self.going = [
                self.push(phase, slot, src.at[spot(self.dims, self.at(phase, step))], step)
                for slot, step in ((0, 2), (2, 1), (3, -1))
            ]

    def relay(self, phase):
        if phase == 0:
            self.kept.wait()
        if phase == 2:
            return
        for side, step in ((0, 1), (1, -1)):
            self.going[side].wait()
            add_into(self.full, self.dims, self.at(phase, step, side), [self.boxes[phase][side]])
            self.going.append(self.push(phase, 2 + side, self.full.at[spot(self.dims, self.at(phase, step))], step))

    def finish(self, phase):
        if phase < 2:
            for copy in self.going[2:]:
                copy.wait()
            add_into(self.full, self.dims, self.at(phase, 0), self.boxes[phase][2:4])
            self.launch(phase + 1)
            return None
        for copy in self.going:
            copy.wait()
        total = self.full[spot(self.dims, self.at(2, 0))].astype(f32)
        for slot in (0, 2, 3):
            total = total + self.boxes[2][slot][...].astype(f32)
        return total

    @staticmethod
    def scratch(dims, order, slab, dtype):
        shapes = [(*lead(dims), *slab)]
        rest = dims
        for phase, axis in enumerate(order):
            rest = without(rest, axis)
            if phase < 2:
                small = free_sizes(rest, half(order[phase + 1], 0))
            else:
                small = ()
            shapes += [(*small, *slab)] * 2 + [(*lead(rest), *slab)] * 2
        return [pltpu.VMEM(s, dtype) for s in shapes]


OWNED = ("x", "l", "z", "h")
GATHER = (
    (OWNED, ("z", "y", "x")),
    (OWNED, ("x", "z", "y")),
    (OWNED, ("z", "y", "x")),
    (("c", "l", "z", "x", "h"), ("x", "z", "y")),
    (("h", "c", "l", "z", "x"), ("y", "x", "z")),
    (("h", "c", "l", "z", "x"), ("z", "y", "x")),
)
SCATTER = (
    (OWNED, ("z", "y", "x")),
    (OWNED, ("y", "z", "x")),
    (OWNED, ("z", "y", "x")),
    (("l", "z", "x", "h"), ("z", "y", "x")),
    (("h", "l", "z", "x"), ("x", "y", "z")),
    (("h", "l", "z", "x"), ("y", "x", "z")),
)
SLABS = ((24, 512), (24, 512), (16, 128), (16, 512), (16, 1280), (16, 1024))


D, EXP, MAP, PIX = 512, 3072, 9, 81
PAIR = 24
WIDTH = 384
OWNERS = WIDTH // 24
CHUNK = 3
SPAN = CHUNK * MAP * PAIR
EXPAND = 8.0 / math.sqrt(D)
PROJECT = 8.0 / math.sqrt(EXP)
VMEM_BYTES = 60 * 2**20


def sigmoid(v):
    return 0.5 + 0.5 * jnp.tanh(0.5 * v)


def nt(left, right):
    return lax.dot_general(left, right, (((1,), (1,)), ((), ())), preferred_element_type=f32)


def nn(left, right):
    return lax.dot_general(left, right, (((1,), (0,)), ((), ())), preferred_element_type=f32)


def tn(left, right):
    return lax.dot_general(left, right, (((0,), (0,)), ((), ())), preferred_element_type=f32)


def clear_borders(padded):
    zero = jnp.zeros((MAP, PAIR, WIDTH), f32)
    padded[0] = zero
    padded[MAP + 1] = zero


def each_block(body):
    def one(row, _):
        for lane in range(WIDTH // 128):
            for group in range(PAIR // 8):
                body(row, slice(8 * group, 8 * group + 8), slice(128 * lane, 128 * lane + 128))
        return 0

    lax.fori_loop(0, MAP, one, 0)


INSTR, DIMS, BINS, NTOK, FRAMES, HEADS, HD = 744, 11, 256, 8, 6, 8, 64
TABLE = INSTR + 2
ROWS = PAIR * NTOK
PADDED = 2048
SMALL_AT = TABLE - D
LN_EPS = 1e-06
OUT_MULT = 2.0
HIGH = lax.Precision.HIGHEST
FILM = 16.0 / math.sqrt(D)
LEARN = 4.0 / math.sqrt(D)


def norm_fwd(x, gain):
    centre = x - jnp.mean(x, -1, keepdims=True)
    inverse = lax.rsqrt(jnp.mean(centre * centre, -1, keepdims=True) + LN_EPS)
    normed = centre * inverse
    return normed * (1.0 + gain), normed, inverse


def norm_back(normed, inverse, gain, grad_out):
    dnormed = grad_out * (1.0 + gain)
    grad_in = inverse * (
        dnormed
        - jnp.mean(dnormed, -1, keepdims=True)
        - normed * jnp.mean(dnormed * normed, -1, keepdims=True)
    )
    return grad_in, jnp.sum(grad_out * normed, 0, keepdims=True)


def gelu_parts(u):
    c = math.sqrt(2.0 / math.pi)
    square = u * u
    t = jnp.tanh(c * u * (1.0 + 0.044715 * square))
    half = 0.5 * (1.0 + t)
    return u * half, half + 0.5 * u * (1.0 - t * t) * c * (1.0 + 3.0 * 0.044715 * square)


def iota(shape, axis):
    return lax.broadcasted_iota(jnp.int32, shape, axis)


def shifted(v, places):
    tiles = [pltpu.roll(v[:, i : i + 128], (128 - places) % 128, 1) for i in range(0, v.shape[1], 128)]
    return jnp.concatenate(tiles, axis=1)


def only(v, first):
    place = iota(v.shape, 1) & 15
    return jnp.where((place >= first) & (place < first + 4), v, 0.0)


def place_of_feature(start, rows):
    d = iota((rows, D), 1)
    owner = d >> 2
    row = (owner & 1) * 1024 + (owner >> 1) * 16 + 12 + (d & 3)
    return (iota((rows, D), 0) + start == row).astype(bf16)


def over_cells(body, carry):
    many = 16 * PAIR
    carry = lax.fori_loop(
        0, PIX // 16, lambda i, c: body(pl.ds(pl.multiple_of(i * many, many), many), many, c), carry
    )
    return body(slice(PIX // 16 * many, PIX * PAIR), PAIR, carry)


def middle_kernel(
    instr_in, mask_in, part, cells, misc, one_in, two_in, cam, bins_in,
    dcells, dmisc, one_out, two_out, stats,
    one, two, done_one, done_two, y_hi, y_lo, logit, att, qkv, prob, ctx, up, hid, acc, dlog, lowgrad, turn, sems,
):
    core, high = lax.axis_index("mp_1"), lax.axis_index("mp_0")
    fetch_one = pltpu.make_async_copy(one_in, one, sems.at[0])
    fetch_two = pltpu.make_async_copy(two_in, two, sems.at[1])
    fetch_one.start()
    fetch_two.start()
    lanes, images = iota((PAIR, 128), 1), iota((PAIR, 128), 0)
    instr = jnp.zeros((PAIR, 128), jnp.int32)
    for i in range(PAIR // FRAMES):
        instr = jnp.where(lax.div(images, FRAMES) == i, instr_in[high * (PAIR // FRAMES) + i], instr)
    mask = jnp.zeros((PAIR, 128), jnp.int32)
    for i in range(PAIR):
        mask = jnp.where(images == i, mask_in[high * PAIR + i], mask)
    turn[...] = jnp.zeros_like(turn)
    turn[0:DIMS, 0 : 2 * PAIR] = bins_in[...].astype(f32)
    turn[...] = turn[...].T
    bins = turn[pl.ds(pl.multiple_of(high * PAIR, PAIR), PAIR), :].astype(jnp.int32)

    def chosen(tile):
        at = lanes + 128 * tile
        return ((at == instr) | (at == INSTR + cam[0] + cam[1])).astype(f32)

    choose_lo = jnp.concatenate([chosen(i) for i in range(4)], axis=1).astype(bf16)
    choose_hi = jnp.concatenate([chosen(i) for i in range(4, 8)], axis=1).astype(bf16)
    flat = misc[...]
    cvec = only(shifted(nt(choose_lo, flat), 8) + shifted(nt(choose_hi, flat), 12), 0).astype(bf16).astype(f32)
    cvec_4 = shifted(cvec, 124)
    cvec_low, cvec_4_low = cvec.astype(bf16), cvec_4.astype(bf16)
    gamma = nn(cvec_low, flat) * FILM
    beta = nn(cvec_4_low, flat) * FILM
    scale = 1.0 + gamma
    pick = (iota((16, D), 1) == SMALL_AT + iota((16, D), 0)).astype(bf16)
    small = nn(nt(pick, flat).astype(bf16), place_of_feature(0, 2048))
    gains = [small[i : i + 1] for i in range(3)]
    learner = jnp.concatenate([small[3:11], jnp.zeros((120, D), f32)], axis=0).astype(bf16)

    def feature(rows, size, _):
        v = part[rows, :].reshape(size // PAIR, PAIR, D) * scale + beta
        v = v.reshape(size, D) + cells[rows, :].astype(f32)
        hi = v.astype(bf16)
        y_hi[rows, :] = hi
        y_lo[rows, :] = (v - hi.astype(f32)).astype(bf16)
        return 0

    over_cells(feature, 0)
    tail = slice(PIX * PAIR, PADDED)
    for ref in (y_hi, y_lo, att, logit):
        ref[tail, :] = jnp.zeros((PADDED - PIX * PAIR, ref.shape[1]), ref.dtype)
    used = slice(0, PIX * PAIR)
    logit[used, :] = (nt(y_hi[used, :], learner) + nt(y_lo[used, :], learner)) * LEARN

    def softmax_over_cells(v):
        v = v.reshape(PIX, PAIR, 128)
        e = jnp.exp(v - jnp.max(v, 0, keepdims=True))
        return e / jnp.sum(e, 0, keepdims=True)

    att[used, :] = softmax_over_cells(logit[used, :]).reshape(PIX * PAIR, 128)
    acc[...] = jnp.zeros_like(acc)

    def gather(i, _):
        rows = pl.ds(pl.multiple_of(i * 512, 512), 512)
        turned = jnp.concatenate(
            [att[pl.ds(pl.multiple_of(i * 512 + 128 * k, 128), 128), :].T[0:NTOK] for k in range(4)], axis=1
        )
        hi = turned.astype(bf16).astype(f32)
        lo = turned - hi
        image = lax.rem(i * 512 + iota((8, 512), 1), PAIR)
        own = [image == 8 * g + iota((8, 512), 0) for g in range(3)]

        def wide(v):
            pieces = [jnp.where(m, v[t : t + 1], 0.0) for t in range(NTOK) for m in own]
            return jnp.concatenate(pieces, axis=0).astype(bf16)

        wide_hi = wide(hi)
        upper = y_hi[rows, :]
        acc[...] += nn(wide_hi, upper) + nn(wide(lo), upper) + nn(wide_hi, y_lo[rows, :])
        return 0

    lax.fori_loop(0, PADDED // 512, gather, 0)
    tok = acc[...].astype(bf16).astype(f32)
    fetch_one.wait()
    fetch_two.wait()

    h1, normed1, inverse1 = norm_fwd(tok, gains[0])
    h1_low = h1.astype(bf16)
    row_q, row_k = iota((ROWS, ROWS), 0), iota((ROWS, ROWS), 1)
    image_q, image_k = lax.rem(row_q, PAIR), lax.rem(row_k, PAIR)
    order_q = image_q * NTOK + lax.div(row_q, PAIR)
    order_k = image_k * NTOK + lax.div(row_k, PAIR)
    seen = (lax.div(image_q, FRAMES) == lax.div(image_k, FRAMES)) & (order_k <= order_q)
    root = HD**-0.5
    acc[...] = jnp.zeros_like(acc)

    def attend(m, _):
        p = nn(h1_low, one[m, :, 0:384]).astype(bf16)
        qkv[m] = p
        outs = []
        for head in range(2):
            q, k, v = (p[:, 128 * j + 64 * head : 128 * j + 64 * head + 64] for j in range(3))
            s = jnp.where(seen, nt(q, k) * root, -1e30)
            e = jnp.exp(s - jnp.max(s, -1, keepdims=True))
            w = e / jnp.sum(e, -1, keepdims=True)
            prob[m, head] = w
            outs.append(nn(w.astype(bf16), v))
        o = jnp.concatenate(outs, axis=1).astype(bf16)
        ctx[m] = o
        acc[...] += nt(o, one[m, :, 384:512])
        return 0

    lax.fori_loop(0, 4, attend, 0)
    x1 = tok + OUT_MULT * acc[...]
    h2, normed2, inverse2 = norm_fwd(x1, gains[1])
    h2_low = h2.astype(bf16)
    acc[...] = x1

    def feed(m, _):
        u = nn(h2_low, two[m, :, 0:512])
        up[m] = u
        low = gelu_parts(u)[0].astype(bf16)
        hid[m] = low
        acc[...] += nt(low, two[m, :, 512:1024])
        return 0

    lax.fori_loop(0, 4, feed, 0)
    x2 = acc[...]
    normed_out, normed3, inverse3 = norm_fwd(x2, gains[2])
    pooled = (jnp.sum(normed_out.reshape(NTOK, PAIR, D), axis=0) * (1.0 / NTOK)).astype(bf16)

    low_half = lanes < 64
    scores = [nn(pooled, one[m, :, 512:1280]) for m in range(4)]
    weight = mask.astype(f32)
    loss = jnp.zeros((PAIR, 128), f32)
    for u in range(6):
        tiles = [s[:, 128 * u : 128 * u + 128] for s in scores]
        top = jnp.maximum(jnp.maximum(tiles[0], tiles[1]), jnp.maximum(tiles[2], tiles[3]))
        left = jnp.max(jnp.where(low_half, top, -jnp.inf), -1, keepdims=True)
        right = jnp.max(jnp.where(low_half, -jnp.inf, top), -1, keepdims=True)
        top = jnp.where(low_half, left, right)
        total = sum(jnp.exp(t - top) for t in tiles)
        left = jnp.sum(jnp.where(low_half, total, 0.0), -1, keepdims=True)
        right = jnp.sum(jnp.where(low_half, 0.0, total), -1, keepdims=True)
        lse = top + jnp.log(jnp.where(low_half, left, right))
        label = jnp.where(low_half, bins[:, 2 * u : 2 * u + 1], bins[:, 2 * u + 1 : 2 * u + 2])
        real = low_half | (2 * u + 1 < DIMS)
        target = jnp.zeros((PAIR, 128), f32)
        for m, t in enumerate(tiles):
            hit = label == (lanes & 63) + 64 * m
            target = target + jnp.where(hit, t, 0.0)
            slope = weight * (jnp.exp(t - lse) - hit.astype(f32))
            dlog[m, :, 128 * u : 128 * u + 128] = jnp.where(real, slope, 0.0).astype(bf16)
        counted = real & ((lanes & 63) == 0)
        loss = loss + weight * (jnp.where(counted, lse, 0.0) - target)
    stats[...] = jnp.zeros_like(stats)
    stats[0:8] = loss[0:8] + loss[8:16] + loss[16:24]
    counts = jnp.where(lanes == 0, weight, 0.0)
    stats[8:16] = counts[0:8] + counts[8:16] + counts[16:24]
    dpooled = jnp.zeros((PAIR, D), f32)
    for m in range(4):
        dpooled = dpooled + nt(dlog[m], one[m, :, 512:1280])
    dnormed = jnp.broadcast_to(dpooled * (1.0 / NTOK), (NTOK, PAIR, D)).reshape(ROWS, D)
    dx2, dgain2 = norm_back(normed3, inverse3, gains[2], dnormed)
    dbranch = dx2.astype(bf16)
    acc[...] = jnp.zeros_like(acc)

    def feed_back(m, _):
        slope = gelu_parts(up[m])[1]
        dup = (nn(dbranch, two[m, :, 512:1024]) * slope).astype(bf16)
        lowgrad[m] = dup
        acc[...] += nt(dup, two[m, :, 0:512])
        return 0

    lax.fori_loop(0, 4, feed_back, 0)
    dx1_norm, dgain1 = norm_back(normed2, inverse2, gains[1], acc[...])
    dx1 = dx2 + dx1_norm
    dattn = dx1.astype(bf16)

    def feed_weights(h, _):
        m = 2 * h + core
        done_one[h, :, 512:1280] = tn(pooled, dlog[m]).astype(bf16)
        done_two[h, :, 0:512] = tn(h2_low, lowgrad[m]).astype(bf16)
        done_two[h, :, 512:1024] = tn(dbranch, hid[m]).astype(bf16)
        done_one[h, :, 384:512] = (tn(dattn, ctx[m]) * OUT_MULT).astype(bf16)
        return 0

    lax.fori_loop(0, 2, feed_weights, 0)
    acc[...] = jnp.zeros_like(acc)

    def attend_back(m, _):
        do = (nn(dattn, one[m, :, 384:512]) * OUT_MULT).astype(bf16)
        p = qkv[m]
        dq, dk, dv = [], [], []
        for head in range(2):
            q, k, v = (p[:, 128 * j + 64 * head : 128 * j + 64 * head + 64] for j in range(3))
            w = prob[m, head]
            d = do[:, 64 * head : 64 * head + 64]
            dp = nt(d, v)
            dv.append(tn(w.astype(bf16), d))
            ds = (w * (dp - jnp.sum(w * dp, -1, keepdims=True))).astype(bf16)
            dq.append(nn(ds, k) * root)
            dk.append(tn(ds, q) * root)
        g = jnp.concatenate([*dq, *dk, *dv], axis=1).astype(bf16)
        lowgrad[m, :, 0:384] = g
        acc[...] += nt(g, one[m, :, 0:384])
        return 0

    lax.fori_loop(0, 4, attend_back, 0)

    def attend_weights(h, _):
        done_one[h, :, 0:384] = tn(h1_low, lowgrad[2 * h + core, :, 0:384]).astype(bf16)
        return 0

    lax.fori_loop(0, 2, attend_weights, 0)
    dtok_norm, dgain0 = norm_back(normed1, inverse1, gains[0], acc[...])
    acc[...] = dx1 + dtok_norm

    send_one = pltpu.make_async_copy(done_one, one_out, sems.at[0])
    send_two = pltpu.make_async_copy(done_two, two_out, sems.at[1])
    send_one.start()
    send_two.start()
    dtok_hi = acc[...].astype(bf16)
    dtok_lo = (acc[...] - dtok_hi.astype(f32)).astype(bf16)
    same = lax.rem(iota((PAIR, ROWS), 1), PAIR) == iota((PAIR, ROWS), 0)
    token_of = (lax.div(iota((128, ROWS), 1), PAIR) == iota((128, ROWS), 0)).astype(bf16)

    def own_image(v):
        return jnp.where(same, v.reshape(-1, PAIR, ROWS), 0.0).reshape(-1, ROWS)

    def halves(v):
        hi = v.astype(bf16)
        return hi, (v - hi.astype(f32)).astype(bf16)

    def slope_of(rows, size, _):
        upper = y_hi[rows, :]
        g = own_image(nt(upper, dtok_hi) + nt(upper, dtok_lo) + nt(y_lo[rows, :], dtok_hi))
        hi, lo = halves(g)
        logit[rows, :] = nt(hi, token_of) + nt(lo, token_of)
        return 0

    over_cells(slope_of, 0)
    a = att[used, :].reshape(PIX, PAIR, 128)
    da = logit[used, :].reshape(PIX, PAIR, 128)
    logit[used, :] = (a * (da - jnp.sum(a * da, 0, keepdims=True)) * LEARN).reshape(PIX * PAIR, 128)
    turned = jnp.concatenate([logit[128 * k : 128 * k + 128, :].T[0:NTOK] for k in range(PADDED // 128)], axis=1)
    upper = turned.astype(bf16).astype(f32)
    both = jnp.concatenate([upper, turned - upper], axis=0).astype(bf16)
    sums = nn(both, y_hi[...])
    dlearner = sums[0:8] + sums[8:16] + nn(both, y_lo[...])[0:8]

    def spread(rows, size, sums):
        hi, lo = halves(att[rows, :])
        hi, lo = own_image(nn(hi, token_of)).astype(bf16), own_image(nn(lo, token_of)).astype(bf16)
        slope_hi, slope_lo = halves(logit[rows, :])
        dy = nn(hi, dtok_hi) + nn(lo, dtok_hi) + nn(hi, dtok_lo) + nn(slope_hi, learner) + nn(slope_lo, learner)
        dy = dy.reshape(size // PAIR, PAIR, D)
        dcells[rows, :] = (dy * scale).astype(bf16).reshape(size, D)
        p = part[rows, :].reshape(size // PAIR, PAIR, D)
        return sums[0] + jnp.sum(dy * p, 0), sums[1] + jnp.sum(dy, 0)

    zero = jnp.zeros((PAIR, D), f32)
    dgamma, dbeta = over_cells(spread, (zero, zero))
    dgamma, dbeta = dgamma.astype(bf16), dbeta.astype(bf16)
    dcvec = only(nt(dgamma, flat) + shifted(nt(dbeta, flat), 4), 0) * FILM
    high = dcvec.astype(bf16).astype(f32)
    rest = dcvec - high
    dsmall = jnp.concatenate([dgain0, dgain1, dgain2, dlearner, jnp.zeros((5, D), f32)], axis=0).astype(bf16)
    mine = pl.ds(pl.multiple_of(core * 1024, 1024), 1024)
    lhs = jnp.concatenate(
        [cvec, cvec_4, shifted(high, 120), shifted(rest, 120), shifted(high, 116), shifted(rest, 116)], axis=0
    )
    lhs = jnp.where(core == 0, lhs[:, 0:1024], lhs[:, 1024:2048])
    lhs = jnp.concatenate([lhs, nt(dsmall, place_of_feature(core * 1024, 1024))], axis=0).astype(bf16)
    rhs = jnp.concatenate([dgamma, dbeta, choose_lo, choose_lo, choose_hi, choose_hi, pick], axis=0)
    result = tn(lhs, rhs)
    film_rows = (iota((1024, D), 0) & 15) < 8
    dmisc[...] = jnp.where(film_rows, result * FILM, result).astype(bf16)
    send_one.wait()
    send_two.wait()


def middle(instr, mask, part, cells, misc, one, two, cam, bins):
    vmem = pl.BlockSpec(memory_space=pltpu.VMEM)
    return pl.pallas_call(
        middle_kernel,
        out_shape=[
            jax.ShapeDtypeStruct((PIX * PAIR, D), bf16),
            jax.ShapeDtypeStruct((1024, D), bf16),
            jax.ShapeDtypeStruct((2, D, 1280), bf16),
            jax.ShapeDtypeStruct((2, D, 1024), bf16),
            jax.ShapeDtypeStruct((16, 128), f32),
        ],
        in_specs=[pl.BlockSpec(memory_space=pltpu.SMEM)] * 2 + [vmem] * 3 + [ANY] * 2 + [vmem] * 2,
        out_specs=[vmem, vmem, ANY, ANY, vmem],
        scratch_shapes=[
            pltpu.VMEM((4, D, 1280), bf16),
            pltpu.VMEM((4, D, 1024), bf16),
            pltpu.VMEM((2, D, 1280), bf16),
            pltpu.VMEM((2, D, 1024), bf16),
            pltpu.VMEM((PADDED, D), bf16),
            pltpu.VMEM((PADDED, D), bf16),
            pltpu.VMEM((PADDED, 128), f32),
            pltpu.VMEM((PADDED, 128), f32),
            pltpu.VMEM((4, ROWS, 384), bf16),
            pltpu.VMEM((4, 2, ROWS, ROWS), f32),
            pltpu.VMEM((4, ROWS, 128), bf16),
            pltpu.VMEM((4, ROWS, 512), f32),
            pltpu.VMEM((4, ROWS, 512), bf16),
            pltpu.VMEM((ROWS, D), f32),
            pltpu.VMEM((4, PAIR, 768), bf16),
            pltpu.VMEM((4, ROWS, 512), bf16),
            pltpu.VMEM((128, 128), f32),
            pltpu.SemaphoreType.DMA((2,)),
        ],
        compiler_params=pltpu.CompilerParams(vmem_limit_bytes=VMEM_BYTES),
    )(instr, mask, part, cells, misc, one, two, cam, bins)


STEPS = 4
BLOCK = (PIX, PAIR, WIDTH)


def tap_places():
    row, col = iota((OWNERS * 128, WIDTH), 0), iota((OWNERS * 128, WIDTH), 1)
    return (((row >> 7) * 24 + (row & 127) == col) & ((row & 127) < 24)).astype(bf16)


def to_cells(frames, cells):
    rows = 8 * PAIR
    at, of = iota((rows, rows), 0), iota((rows, rows), 1)
    turn = (lax.rem(at, PAIR) * 8 + lax.div(at, PAIR) == of).astype(bf16)
    for first in (*range(0, PIX - 8, 8), PIX - 8):
        block = frames[:, :, first : first + 8, :].reshape(rows, D)
        cells[first * PAIR : first * PAIR + rows, :] = nn(turn, block).astype(bf16)


def fill_shards(conv, cond, small, attn, mlp, head, camera, core, shards, staged, tap_tile, cam):
    shards[0][...] = conv[:, 0:D].astype(bf16)
    shards[1][...] = conv[:, D : 2 * D].astype(bf16)
    tap_tile[...] = jnp.zeros_like(tap_tile)
    tap_tile[0:24, 0:9] = conv[:, 2 * D :]
    shards[2][...] = tap_tile[...].T[0:16].astype(bf16)
    staged[...] = jnp.zeros_like(staged)
    for i in range(3):
        staged[4 * i : 4 * i + 4, :] = cond[:, D * i : D * i + D]
    staged[12:16, 0:SMALL_AT] = cond[:, 3 * D :]
    staged[12:16, SMALL_AT : SMALL_AT + 11] = small[...]
    shards[3][...] = staged[...].astype(bf16)
    for j in range(4):
        shards[4][:, 128 * j : 128 * j + 128] = attn[j].astype(bf16)
    for k in range(0, DIMS - 1, 2):
        both = jnp.concatenate([head[k], head[k + 1]], axis=1)
        shards[4][:, 512 + 64 * k : 640 + 64 * k] = both.astype(bf16)
    last = jnp.concatenate([head[DIMS - 1], jnp.zeros((16, 64), f32)], axis=1)
    shards[4][:, 1152:1280] = last.astype(bf16)
    for j in range(2):
        shards[5][:, 512 * j : 512 * j + 512] = mlp[j].astype(bf16)
    row = iota((PAIR, 128), 0)
    found = jnp.zeros((PAIR, 128), jnp.int32)
    for i in range(PAIR // 2):
        found = jnp.where(row == core * (PAIR // 2) + i, camera[i], found)
    cam[...] = found


def forward_kernel(plan, *refs):
    n = len(plan)
    frames, camera = refs[0:2]
    masters = refs[2 : 2 + n]
    refs = refs[2 + n :]
    cam2, cells_out, project_out, taps_out, misc_out, one_out, two_out, pre_out, deep_out, total_out = refs[:10]
    frames2, cells, expand, project, slabs, taps, places, act, pre, deep, part, other = refs[10:22]
    shards, staged, tap_tile, cam = refs[22 : 22 + n], refs[22 + n], refs[23 + n], refs[24 + n]
    send, recv, fsend, frecv, local, kept, swap_send, swap_recv = refs[25 + n :]
    me = here()
    count = announce(me)
    fill_shards(*masters, camera, me["c"][0], shards, staged, tap_tile, cam)
    meet(count)
    swaps = []
    for i, (src, out) in enumerate(((frames, frames2), (cam, cam2))):
        where = out.at[me["c"][0]]
        mine = pltpu.make_async_copy(src, where, local.at[n + i])
        mine.start()
        swaps += [mine, remote(src, where, swap_send.at[i], swap_recv.at[i], "c", me["c"][1])]
    outs = (expand, project, slabs, misc_out, one_out, two_out)
    jobs = [
        Gather(me, dims, order, shards[b], outs[b], send.at[b], recv.at[b], fsend.at[b], frecv.at[b], local.at[b])
        for b, (dims, order) in enumerate(plan)
    ]
    early, late, middle_one, outer = (jobs[0], jobs[2]), (jobs[1],), (jobs[4],), (jobs[3], jobs[5])
    first, rest = jobs[:3], jobs[3:]

    def relay(some, phase):
        for job in some:
            job.relay(phase)

    def finish(some, phase, launch=True):
        for job in some:
            job.finish(phase, launch)

    for job in jobs:
        job.begin()
    relay(first, 0)
    finish(first, 0)
    clear_borders(act)
    places[...] = tap_places()
    relay(rest, 0)
    finish(rest, 0)
    relay(first, 1)
    relay(rest, 1)
    finish(first, 1)
    finish(middle_one, 1)
    finish(outer, 1, False)
    part[...] = jnp.zeros_like(part)
    swaps[0].wait()
    swaps[1].wait()
    to_cells(frames2, cells)
    saves = []

    def save(src, dst, number):
        copy = pltpu.make_async_copy(src, dst, kept.at[number])
        copy.start()
        saves.append(copy)

    save(cells, cells_out, 0)
    spans, leaves = [None] * STEPS, []
    for step in range(STEPS):
        slot = step % 2
        at = me["x"][(0, -1, 1, 2)[step]]
        if step == 1:
            relay(early, 2)
            relay(late, 2)
            for job in outer:
                job.launch(2)
        if step == 2:
            relay(middle_one, 2)
        if step == 3:
            finish(early, 2)
            relay(outer, 2)
        if step >= 2:
            for copy in spans[step - 2]:
                copy.wait()
        weight = expand[at].reshape(WIDTH, D)
        tap = slabs[at].reshape(OWNERS, 16, 128)
        side = jnp.concatenate([tap[i] for i in range(OWNERS)], axis=1)
        taps[at] = nn(side, places[...]) * (8.0 / 3.0)

        def enter(i, _, weight=weight, slot=slot):
            rows = pl.ds(pl.multiple_of(i * SPAN, SPAN), SPAN)
            e = (nt(cells[rows, :], weight) * EXPAND).reshape(CHUNK * MAP, PAIR, WIDTH)
            pre[slot, pl.ds(i * CHUNK * MAP, CHUNK * MAP)] = e
            act[pl.ds(1 + i * CHUNK, CHUNK)] = (e * sigmoid(e)).reshape(CHUNK, MAP, PAIR, WIDTH)
            return 0

        lax.fori_loop(0, MAP // CHUNK, enter, 0)
        out = [pltpu.make_async_copy(pre.at[slot], pre_out.at[at], kept.at[3 + 2 * step])]
        out[0].start()

        def mix(row, subs, cols, slot=slot, at=at):
            near = act[pl.ds(row, 3), :, subs, cols]
            tap = [jnp.broadcast_to(taps[at, t : t + 1, cols], (8, 128)) for t in range(9)]
            for col in range(MAP):
                total = None
                for t in range(9):
                    p = col + t % 3 - 1
                    if 0 <= p < MAP:
                        term = near[t // 3, p] * tap[t]
                        total = term if total is None else total + term
                deep[slot, row * MAP + col, subs, cols] = total

        each_block(mix)
        out.append(pltpu.make_async_copy(deep.at[slot], deep_out.at[at], kept.at[4 + 2 * step]))
        out[1].start()
        spans[step] = out
        if step == 3:
            finish(middle_one, 2)

        def leave(i, _, at=at, slot=slot):
            back = project[at].reshape(WIDTH, D)
            rows = pl.ds(pl.multiple_of(i * SPAN, SPAN), SPAN)
            v = deep[slot, pl.ds(i * CHUNK * MAP, CHUNK * MAP)].reshape(SPAN, WIDTH)
            part[rows, :] += nn((v * sigmoid(v)).astype(bf16), back) * PROJECT
            return 0

        leaves.append(leave)
        if step == 1:
            finish(late, 2)
            save(project, project_out, 1)
            lax.fori_loop(0, MAP // CHUNK, leaves[0], 0)
        if 0 < step < STEPS - 1:
            lax.fori_loop(0, MAP // CHUNK, leave, 0)
    save(taps, taps_out, 2)
    trades = []
    for i in range(MAP // CHUNK):
        leave(i, 0)
        rows = pl.ds(i * SPAN, SPAN)
        trades.append(
            remote(part.at[rows], other.at[rows], swap_send.at[2 + i], swap_recv.at[2 + i], "c", me["c"][1])
        )
    finish(outer, 2)
    for i, copy in enumerate(trades):
        copy.wait()
        rows = slice(i * SPAN, (i + 1) * SPAN)
        other[rows, :] += part[rows, :]
        save(other.at[rows], total_out.at[rows], 3 + 2 * STEPS + i)
    for step in (STEPS - 2, STEPS - 1):
        saves += spans[step]
    for job in jobs:
        job.end()
    for copy in saves + swaps[2:]:
        copy.wait()


def forward(frames, camera, masters, plan, collective_id):
    n = len(plan)
    maps = jax.ShapeDtypeStruct((STEPS, *BLOCK), f32)
    shape = jax.ShapeDtypeStruct
    full = [shape((*lead(dims), *slab), bf16) for slab, (dims, _) in zip(SLABS, plan)]
    rows = PIX * PAIR
    return pl.pallas_call(
        functools.partial(forward_kernel, plan),
        out_shape=[
            shape((2, PAIR, 128), jnp.int32),
            shape((rows, D), bf16),
            full[1],
            shape((STEPS, 16, WIDTH), f32),
            *full[3:],
            maps,
            maps,
            shape((rows, D), f32),
        ],
        in_specs=[ANY, pl.BlockSpec(memory_space=pltpu.SMEM)] + [INVMEM] * n,
        out_specs=[ANY] * 10,
        scratch_shapes=[
            pltpu.VMEM((2, *frames.shape), bf16),
            pltpu.VMEM((rows, D), bf16),
            pltpu.VMEM(full[0].shape, bf16),
            pltpu.VMEM(full[1].shape, bf16),
            pltpu.VMEM(full[2].shape, bf16),
            pltpu.VMEM((STEPS, 16, WIDTH), f32),
            pltpu.VMEM((OWNERS * 128, WIDTH), bf16),
            pltpu.VMEM((MAP + 2, MAP, PAIR, WIDTH), f32),
            pltpu.VMEM((2, *BLOCK), f32),
            pltpu.VMEM((2, *BLOCK), f32),
            pltpu.VMEM((rows, D), f32),
            pltpu.VMEM((rows, D), f32),
            *[pltpu.VMEM(slab, bf16) for slab in SLABS],
            pltpu.VMEM((16, D), f32),
            pltpu.VMEM((128, 128), f32),
            pltpu.VMEM((PAIR, 128), jnp.int32),
            pltpu.SemaphoreType.DMA((n, 3, 4)),
            pltpu.SemaphoreType.DMA((n, 3, 4)),
            pltpu.SemaphoreType.DMA((n, 7)),
            pltpu.SemaphoreType.DMA((n, 7)),
            pltpu.SemaphoreType.DMA((n + 2,)),
            pltpu.SemaphoreType.DMA((3 + 2 * STEPS + MAP // CHUNK,)),
            pltpu.SemaphoreType.DMA((2 + MAP // CHUNK,)),
            pltpu.SemaphoreType.DMA((2 + MAP // CHUNK,)),
        ],
        compiler_params=pltpu.CompilerParams(
            collective_id=collective_id, has_side_effects=True, vmem_limit_bytes=VMEM_BYTES
        ),
    )(frames, camera, *masters)


class Blocks:
    def __init__(self, me, dims, order, full, room, send, recv):
        self.me, self.dims, self.order, self.full = me, dims, order, full
        self.halves, self.wholes, self.slabs, self.last = room
        self.send, self.recv = send, recv
        self.going = [None] * STEPS
        self.sent = []

    def at(self, step, **more):
        return {"x": self.me["x"][BACK[step]], **more}

    def push(self, step, slot, src, box, axis, move):
        return remote(src, box, self.send.at[step, slot], self.recv.at[step, slot], axis, self.me[axis][move])

    def launch(self, step):
        a, b, _ = self.order
        self.going[step] = [
            self.push(
                step, side, self.full.at[spot(self.dims, self.at(step, **{a: self.me[a][2]}, **half(b, side)))],
                self.halves.at[step, side], a, 1 - 2 * side,
            )
            for side in range(2)
        ]

    def relay(self, step):
        a, b, _ = self.order
        for side, move in ((0, 1), (1, -1)):
            self.going[step][side].wait()
            pos = {a: self.me[a][move]}
            add_into(self.full, self.dims, self.at(step, **pos, **half(b, side)), [self.halves.at[step, side]])
            where = self.full.at[spot(self.dims, self.at(step, **pos))]
            self.going[step].append(self.push(step, 2 + side, where, self.wholes.at[step, side], a, move))

    def middle(self, step):
        a, b, _ = self.order
        for copy in self.going[step][2:]:
            copy.wait()
        own = {a: self.me[a][0]}
        add_into(self.full, self.dims, self.at(step, **own), [self.wholes.at[step, side] for side in range(2)])
        self.going[step] = [
            self.push(
                step, 4 + i, self.full.at[spot(self.dims, self.at(step, **own, **{b: self.me[b][move]}))],
                self.slabs.at[step, i], b, move,
            )
            for i, move in enumerate((2, 1, -1))
        ]

    def finish(self, step):
        a, b, _ = self.order
        for copy in self.going[step]:
            copy.wait()
        index = spot(self.dims, self.at(step, **{a: self.me[a][0], b: self.me[b][0]}))
        total = self.full[index].astype(f32)
        for i in range(3):
            total = total + self.slabs[step, i].astype(f32)
        if BACK[step] != 0:
            self.full[index] = total.astype(bf16)
            self.sent.append(self.push(step, 7, self.full.at[index], self.last.at[step], "x", BACK[step]))
        return total

    def close(self, total):
        for copy in self.sent:
            copy.wait()
        for i in range(STEPS - 1):
            total = total + self.last[i].astype(f32)
        return total

    @staticmethod
    def scratch(dims, order, slab):
        rest = without(without(dims, "x"), order[0])
        small = free_sizes(rest, half(order[1], 0))
        shapes = [
            (*lead(dims), *slab), (STEPS, 2, *small, *slab), (STEPS, 2, *lead(rest), *slab), (STEPS, 3, *slab),
            (STEPS - 1, *slab),
        ]
        return [pltpu.VMEM(s, bf16) for s in shapes]


BACK = (2, 1, -1, 0)


def backward_kernel(plan, *refs):
    n = len(plan)
    cells_in, dcells_in, project_in, taps_in, pre_in, deep_in, stats = refs[:7]
    parts = refs[7 : 7 + n - 3]
    refs = refs[4 + n :]
    stats_out, outs = refs[0], refs[1 : 1 + n]
    refs = refs[1 + n :]
    cells, dcells, project, taps, places, pre, deep, spread, mid, dpre, acc = refs[:11]
    refs = refs[11:]
    blocks_room, rest_room = refs[:15], refs[15 : 15 + 13 * (n - 3)]
    tile, tile_box, bsend, brecv, send, recv, local, kept, tsend, trecv = refs[15 + 13 * (n - 3) :]
    me = here()
    loads = []
    for i, (src, dst) in enumerate(((cells_in, cells), (dcells_in, dcells), (project_in, project), (taps_in, taps))):
        copy = pltpu.make_async_copy(src, dst, kept.at[i])
        copy.start()
        loads.append(copy)

    def fetch(step):
        at = me["x"][BACK[step]]
        pair = []
        for i, (src, dst) in enumerate(((pre_in, pre), (deep_in, deep))):
            copy = pltpu.make_async_copy(src.at[at], dst.at[step % 2], kept.at[4 + 2 * step + i])
            copy.start()
            pair.append(copy)
        return pair

    maps = [fetch(0), fetch(1), None, None]
    meet(announce(me, wide=True))
    rest = []
    for b, (dims, order) in enumerate(plan[3:]):
        own = rest_room[13 * b : 13 * b + 13]
        boxes = [own[1:5], own[5:9], own[9:13]]
        rest.append(Scatter(me, dims, order, parts[b], own[0], boxes, send.at[b], recv.at[b], local.at[b]))
    first = [
        Blocks(me, dims, order, blocks_room[5 * b], blocks_room[5 * b + 1 : 5 * b + 5], bsend.at[b], brecv.at[b])
        for b, (dims, order) in enumerate(plan[:3])
    ]
    for job in rest:
        job.begin()
    clear_borders(spread)
    places[...] = tap_places()
    for copy in loads:
        copy.wait()
    square = jnp.zeros((8, 128), f32)

    def close_rest(square):
        for b, job in enumerate(rest):
            total = job.finish(2)
            outs[3 + b][...] = total
            square = square + folded(total * total)
        return square

    for step in range(STEPS):
        slot = step % 2
        at = me["x"][BACK[step]]
        for copy in maps[step]:
            copy.wait()
        back = project[at].reshape(WIDTH, D)

        def enter(i, _, back=back, slot=slot):
            rows = pl.ds(pl.multiple_of(i * SPAN, SPAN), SPAN)
            dmid = nt(dcells[rows, :], back) * PROJECT
            v = deep[slot, pl.ds(i * CHUNK * MAP, CHUNK * MAP)].reshape(SPAN, WIDTH)
            s = sigmoid(v)
            m = v * s
            mid[rows, :] = m.astype(bf16)
            spread[pl.ds(1 + i * CHUNK, CHUNK)] = (dmid * (s + m * (1.0 - s))).reshape(CHUNK, MAP, PAIR, WIDTH)
            return 0

        lax.fori_loop(0, MAP // CHUNK, enter, 0)
        if step > 0:
            for job in first:
                job.relay(step - 1)
        if step > 1:
            for job in first:
                job.finish(step - 2)
        if step == 1:
            for job in rest:
                job.relay(0)
        if step == 2:
            for job in rest:
                job.finish(0)
        if step == 3:
            for job in rest:
                job.finish(1)
        acc[...] = jnp.zeros_like(acc)

        def mix(row, subs, cols, slot=slot, at=at):
            near = spread[pl.ds(row, 3), :, subs, cols]
            tap = [jnp.broadcast_to(taps[at, t : t + 1, cols], (8, 128)) for t in range(9)]
            sums = [None] * 9
            for col in range(MAP):
                e = pre[slot, row * MAP + col, subs, cols]
                s = sigmoid(e)
                a = e * s
                total = None
                for t in range(9):
                    p = col + 1 - t % 3
                    if 0 <= p < MAP:
                        g = near[2 - t // 3, p]
                        term = g * tap[t]
                        total = term if total is None else total + term
                        term = g * a
                        sums[t] = term if sums[t] is None else sums[t] + term
                dpre[row * MAP + col, subs, cols] = total * (s + a * (1.0 - s))
            for t in range(9):
                acc[t, :, cols] += sums[t]

        each_block(mix)
        if step + 2 < STEPS:
            maps[step + 2] = fetch(step + 2)
        if step == 2:
            for job in rest:
                job.relay(1)
        if step > 0:
            for job in first:
                job.middle(step - 1)
        owned = (2, 4, 2, 24, D)
        low = dpre[...].reshape(PIX * PAIR, WIDTH).astype(bf16)
        first[0].full[at] = (tn(low, cells[...]) * EXPAND).astype(bf16).reshape(owned)
        first[1].full[at] = (tn(mid[...], dcells[...]) * PROJECT).astype(bf16).reshape(owned)
        dtaps = jnp.concatenate([jnp.sum(acc[...], axis=1) * (8.0 / 3.0), jnp.zeros((7, WIDTH), f32)], axis=0)
        side = nt(dtaps.astype(bf16), places[...]).astype(bf16)
        for i in range(OWNERS):
            first[2].full[at, i // 8, (i // 2) % 4, i % 2] = side[:, 128 * i : 128 * i + 128]
        for job in first:
            job.launch(step)
    for job in first:
        job.finish(STEPS - 2)
    square = close_rest(square)
    for job in first:
        job.relay(STEPS - 1)
    for job in first:
        job.middle(STEPS - 1)
    for b, job in enumerate(first):
        total = job.close(job.finish(STEPS - 1))
        outs[b][...] = total
        square = square + folded(total * total)
    lines = [jnp.sum(v, 0, keepdims=True) for v in (stats[0:8], stats[8:16], square)]
    tile[0] = jnp.concatenate([*lines, jnp.zeros((5, 128), f32)], axis=0)
    number = 0
    for phase, (one, two) in enumerate((("c", "x"), ("y", "z"))):
        spans = [range(2 if a == "c" else RING) for a in (one, two)]
        moves = [{a: k for a, k in ((one, j), (two, k)) if k} for j in spans[0] for k in spans[1] if j or k]
        copies = []
        for move in moves:
            copy = pltpu.make_async_remote_copy(
                src_ref=tile.at[phase], dst_ref=tile_box.at[number], send_sem=tsend.at[number],
                recv_sem=trecv.at[number], device_id=moved(me, move), device_id_type=MESH_ID,
            )
            copy.start()
            copies.append(copy)
            number += 1
        for copy in copies:
            copy.wait()
        total = tile[phase]
        for i in range(number - len(copies), number):
            total = total + tile_box[i]
        tile[phase + 1] = total
    stats_out[...] = tile[2]


def backward(cells, dcells, project, taps, pre, deep, stats, parts, slabs, plan, collective_id):
    n = len(plan)
    shape = jax.ShapeDtypeStruct
    rows = PIX * PAIR
    room = []
    for (dims, order), slab in zip(plan[:3], slabs[:3]):
        room += Blocks.scratch(dims, order, slab)
    for (dims, order), slab in zip(plan[3:], slabs[3:]):
        room += Scatter.scratch(dims, order, slab, bf16)
    return pl.pallas_call(
        functools.partial(backward_kernel, plan),
        out_shape=[shape((8, 128), f32)] + [shape(s, f32) for s in slabs],
        in_specs=[ANY] * 6 + [INVMEM] + [ANY] * (n - 3),
        out_specs=[INVMEM] * (1 + n),
        scratch_shapes=[
            pltpu.VMEM((rows, D), bf16),
            pltpu.VMEM((rows, D), bf16),
            pltpu.VMEM(project.shape, bf16),
            pltpu.VMEM(taps.shape, f32),
            pltpu.VMEM((OWNERS * 128, WIDTH), bf16),
            pltpu.VMEM((2, *BLOCK), f32),
            pltpu.VMEM((2, *BLOCK), f32),
            pltpu.VMEM((MAP + 2, MAP, PAIR, WIDTH), f32),
            pltpu.VMEM((rows, WIDTH), bf16),
            pltpu.VMEM(BLOCK, f32),
            pltpu.VMEM((9, 8, WIDTH), f32),
            *room,
            pltpu.VMEM((3, 8, 128), f32),
            pltpu.VMEM((22, 8, 128), f32),
            pltpu.SemaphoreType.DMA((3, STEPS, 8)),
            pltpu.SemaphoreType.DMA((3, STEPS, 8)),
            pltpu.SemaphoreType.DMA((n - 3, 3, 4)),
            pltpu.SemaphoreType.DMA((n - 3, 3, 4)),
            pltpu.SemaphoreType.DMA((n - 3,)),
            pltpu.SemaphoreType.DMA((4 + 2 * STEPS,)),
            pltpu.SemaphoreType.DMA((22,)),
            pltpu.SemaphoreType.DMA((22,)),
        ],
        compiler_params=pltpu.CompilerParams(
            collective_id=collective_id, has_side_effects=True, vmem_limit_bytes=VMEM_BYTES
        ),
    )(cells, dcells, project, taps, pre, deep, stats, *parts)


IMAGES = 12
DP_MP = NAMES
DP = ("dp_0", "dp_1", "dp_2")
MP = ("mp_0", "mp_1")
CLIP_NORM = 0.02
BETA_ONE = 0.9
BETA_TWO = 0.999
ADAM_EPS = 1e-08
DECAY = 0.01
RATES = (0.1, 0.1, 0.2, 0.05, 0.05, 0.2)


def adam_kernel(count_ref, totals, gexpand, gproject, gtaps, gmisc, gone, gtwo, *refs):
    states = [refs[3 * i : 3 * i + 3] for i in range(6)]
    loss_ref, norm_ref = refs[18:20]
    outs = [refs[20 + 3 * i : 23 + 3 * i] for i in range(6)]

    def total(line):
        return jnp.sum(totals[line : line + 1, :], axis=(0, 1), keepdims=True)

    scored = 0.5 * total(1)
    norm = jnp.sqrt(total(2)) / scored
    factor = jnp.minimum(1.0, CLIP_NORM / norm) / scored
    loss_ref[0] = (0.5 * total(0) / scored)[0, 0]
    norm_ref[0] = norm[0, 0]
    steps = jnp.full((1, 1), count_ref[0], jnp.int32).astype(f32)
    z = steps * math.log(BETA_TWO)
    grown_two = -z * (1.0 + z / 2.0 * (1.0 + z / 3.0 * (1.0 + z / 4.0 * (1.0 + z / 5.0))))
    grown_one = 1.0 - jnp.exp(steps * math.log(BETA_ONE))

    def update(group, index, grad):
        master, first, second = (ref[index] for ref in states[group])
        grad = grad * factor
        first = BETA_ONE * first + (1.0 - BETA_ONE) * grad
        second = BETA_TWO * second + (1.0 - BETA_TWO) * grad * grad
        step = first / grown_one / (jnp.sqrt(second / grown_two) + ADAM_EPS) + DECAY * master
        outs[group][0][index] = master - RATES[group] * step
        outs[group][1][index] = first
        outs[group][2][index] = second

    every = slice(None)
    update(0, (every, slice(0, D)), gexpand[...])
    update(0, (every, slice(D, 2 * D)), gproject[...])
    taps = jnp.concatenate([gtaps[...], jnp.zeros((112, 128), f32)], axis=0).T
    update(0, (every, slice(2 * D, 2 * D + 9)), taps[0:24, 0:9])
    for i in range(3):
        update(1, (every, slice(D * i, D * i + D)), gmisc[4 * i : 4 * i + 4, :])
    update(1, (every, slice(3 * D, 2 * D + TABLE)), gmisc[12:16, 0:SMALL_AT])
    update(2, (every, every), gmisc[12:16, SMALL_AT : SMALL_AT + 11])
    for j in range(4):
        update(3, j, gone[:, 128 * j : 128 * j + 128])
    for j in range(2):
        update(4, j, gtwo[:, 512 * j : 512 * j + 512])
    for k in range(DIMS):
        update(5, k, gone[:, 512 + 64 * k : 576 + 64 * k])


def adam(step_count, totals, grads, states):
    smem = pl.BlockSpec(memory_space=pltpu.SMEM)
    one = jax.ShapeDtypeStruct((1,), f32)
    return pl.pallas_call(
        adam_kernel,
        out_shape=[one, one] + [jax.ShapeDtypeStruct(s.shape, f32) for s in states],
        in_specs=[smem] + [INVMEM] * (1 + len(grads) + len(states)),
        out_specs=[smem, smem] + [INVMEM] * len(states),
    )(step_count, totals, *grads, *states)


def per_device(
    frames, camera_ids, instruction_ids, action_bins, final_mask, step_count,
    conv_w, conv_m1, conv_m2, cond_w, cond_m1, cond_m2, small_w, small_m1, small_m2,
    attn_w, attn_m1, attn_m2, mlp_w, mlp_m1, mlp_m2, head_w, head_m1, head_m2,
):
    states = [
        *[v.T for v in (conv_w, conv_m1, conv_m2, cond_w, cond_m1, cond_m2, small_w, small_m1, small_m2)],
        *(attn_w, attn_m1, attn_m2, mlp_w, mlp_m1, mlp_m2),
        *[v.transpose(1, 0, 2) for v in (head_w, head_m1, head_m2)],
    ]
    cam2, cells, project, taps, misc_all, one_all, two_all, pre, deep, part = forward(
        frames, camera_ids, states[0::3], GATHER, 1
    )
    dcells, dmisc, done_one, done_two, stats = middle(
        instruction_ids,
        final_mask,
        part,
        cells,
        misc_all.reshape(2048, D),
        one_all.reshape(4, D, 1280),
        two_all.reshape(4, D, 1024),
        cam2,
        action_bins.T,
    )
    parts = [
        g.reshape(*lead(dims), *slab)
        for g, slab, (dims, _) in zip((dmisc, done_one, done_two), SLABS[3:], SCATTER[3:])
    ]
    totals, *grads = backward(cells, dcells, project, taps, pre, deep, stats, parts, SLABS, SCATTER, 2)
    loss, norm, *new = adam(step_count, totals, grads, states)
    new = [v.T for v in new[:9]] + new[9:15] + [v.transpose(1, 0, 2) for v in new[15:]]
    return loss.reshape(()), norm.reshape(()), *new


def solution(mesh):
    torus = Mesh(mesh.devices.reshape(2, 4, 4, 2, 2), NAMES)
    weights = (
        *[P(None, DP_MP)] * 9,
        *[P(None, DP, MP)] * 6,
        *[P(DP, None, MP)] * 3,
    )
    data = (P(DP_MP, None, None), P(DP_MP), P(DP), P(DP, None), P(DP), P())
    return jax.shard_map(
        per_device, mesh=torus, in_specs=(*data, *weights), out_specs=(P(), P(), *weights), check_vma=False
    )
```

```python
import functools
import itertools
import math
import typing

import jax
import jax.numpy as jnp
from jax import lax
from jax.experimental import pallas as pl
from jax.experimental.pallas import tpu as pltpu
from jax.sharding import Mesh
from jax.sharding import PartitionSpec as P

f32 = jnp.float32
bf16 = jnp.bfloat16
NAMES = ("dp_0", "dp_1", "dp_2", "mp_0", "mp_1")
SIZES = {"l": 2, "z": 4, "x": 4, "h": 2, "c": 2}
RING = 4
MESH_ID = pl.DeviceIdType.MESH
ANY = pl.BlockSpec(memory_space=pl.ANY)
INVMEM = pl.BlockSpec(memory_space=pltpu.VMEM)


class Along(typing.NamedTuple):
    low: typing.Any
    high: typing.Any


def here():
    low, z, x, high, core = (lax.axis_index(n) for n in NAMES)
    me = {"c": {0: core, 1: 1 - core}}
    for axis, at in (("x", x), ("y", high * 2 + low), ("z", z)):
        me[axis] = {}
        for step in (0, 1, 2, -1):
            pos = lax.rem(at + step + RING, RING) if step else at
            if axis == "y":
                pos = Along(lax.rem(pos, 2), lax.div(pos, 2)) if step else Along(low, high)
            me[axis][step] = pos
    return me


def device_of(axis, at):
    if axis == "y":
        return {"dp_0": at.low, "mp_0": at.high}
    return {{"x": "dp_2", "z": "dp_1", "c": "mp_1"}[axis]: at}


def extents(dims, at):
    found = []
    for d in dims:
        if d in at:
            v = at[d]
        elif d in "lh" and "y" in at:
            v = at["y"].low if d == "l" else at["y"].high
        else:
            v = (0, SIZES[d])
        found.append(v if isinstance(v, tuple) else (v, None))
    return found


def spot(dims, at):
    return tuple(start if size is None else pl.ds(start, size) for start, size in extents(dims, at))


def free_sizes(dims, at):
    return tuple(size for _, size in extents(dims, at) if size is not None)


def half(axis, side):
    return {"h": side} if axis == "y" else {axis: (2 * side, 2)}


def without(dims, axis):
    return tuple(d for d in dims if d not in ("lh" if axis == "y" else axis))


def lead(dims):
    return tuple(SIZES[d] for d in dims)


def announce(me, wide=False):
    barrier = pltpu.get_barrier_semaphore()
    peers = [{a: k} for a in "xyz" for k in range(1, RING)] + [{"c": 1}]
    if wide:
        peers += [{"x": k, "c": 1} for k in range(1, RING)]
        peers += [{"y": j, "z": k} for j in range(1, RING) for k in range(1, RING)]
    for moves in peers:
        pl.semaphore_signal(barrier, inc=1, device_id=moved(me, moves), device_id_type=MESH_ID)
    return len(peers)


def moved(me, moves):
    found = {}
    for axis, k in moves.items():
        found.update(device_of(axis, me[axis][-1 if k == 3 else k]))
    return found


def meet(count):
    pl.semaphore_wait(pltpu.get_barrier_semaphore(), count)


def remote(src, dst, send, recv, axis, at):
    copy = pltpu.make_async_remote_copy(
        src_ref=src, dst_ref=dst, send_sem=send, recv_sem=recv, device_id=device_of(axis, at), device_id_type=MESH_ID
    )
    copy.start()
    return copy


class Gather:
    def __init__(self, me, dims, order, shard, out, send, recv, fsend, frecv, local):
        self.me, self.dims, self.order, self.shard, self.out = me, dims, order, shard, out
        self.send, self.recv, self.fsend, self.frecv, self.local = send, recv, fsend, frecv, local
        self.forwards = []

    def region(self, phase, step=0, part=None):
        at = {a: self.me[a][0] for a in self.order[phase:]}
        at[self.order[phase]] = self.me[self.order[phase]][step]
        if "c" in self.dims:
            at["c"] = self.me["c"][0]
        if part is not None:
            at.update(half(self.order[0], part))
        return self.out.at[spot(self.dims, at)]

    def push(self, phase, slot, where, step):
        axis = self.order[phase]
        src = self.shard if phase == 0 else where
        return remote(src, where, self.send.at[phase, slot], self.recv.at[phase, slot], axis, self.me[axis][step])

    def forward(self, number, where):
        if "c" in self.dims:
            self.forwards.append(
                remote(where, where, self.fsend.at[number], self.frecv.at[number], "c", self.me["c"][1])
            )

    def begin(self):
        self.kept = pltpu.make_async_copy(self.shard, self.region(0), self.local)
        self.kept.start()
        self.launch(0)

    def launch(self, phase):
        where = self.region(phase)
        self.going = [self.push(phase, 0, where, 1), self.push(phase, 1, where, -1)]
        if phase == 0:
            self.going.append(self.push(0, 2, where, 2))

    def relay(self, phase):
        for slot, step in ((0, 1), (1, -1)):
            self.going[slot].wait()
            if phase > 0:
                self.going.append(self.push(phase, 2 + slot, self.region(phase, -step, slot), step))
                self.forward(3 * phase - 2 + slot, self.region(phase, -step))

    def finish(self, phase, launch=True):
        for copy in self.going[2:]:
            copy.wait()
        if phase == 0:
            self.kept.wait()
            if "c" in self.dims:
                at = {a: self.me[a][0] for a in (*self.order[1:], "c")}
                self.forward(0, self.out.at[spot(self.dims, at)])
        else:
            self.forward(3 * phase, self.region(phase, 2))
        if phase < 2 and launch:
            self.launch(phase + 1)

    def end(self):
        for copy in self.forwards:
            copy.wait()


def add_into(full, dims, at, others):
    found = extents(dims, at)
    for place in itertools.product(*(range(size) for _, size in found if size is not None)):
        index, along = [], iter(place)
        for start, size in found:
            index.append(start if size is None else start + next(along))
        index = tuple(index)
        total = full[index].astype(f32)
        for o in others:
            total = total + o[place].astype(f32)
        full[index] = total.astype(full.dtype)


def folded(v):
    total = None
    for r in range(0, v.shape[0], 8):
        for c in range(0, v.shape[1], 128):
            part = v[r : r + 8, c : c + 128]
            total = part if total is None else total + part
    return total


class Scatter:
    def __init__(self, me, dims, order, part, full, boxes, send, recv, local):
        self.me, self.dims, self.order, self.part, self.full, self.boxes = me, dims, order, part, full, boxes
        self.send, self.recv, self.local = send, recv, local

    def at(self, phase, step, side=None):
        at = {a: self.me[a][0] for a in self.order[:phase]}
        axis = self.order[phase]
        at[axis] = self.me[axis][step]
        if side is not None:
            at.update(half(self.order[phase + 1], side))
        return at

    def push(self, phase, slot, src, step):
        axis = self.order[phase]
        return remote(
            src, self.boxes[phase][slot], self.send.at[phase, slot], self.recv.at[phase, slot], axis, self.me[axis][step]
        )

    def begin(self):
        self.kept = pltpu.make_async_copy(self.part, self.full, self.local)
        self.kept.start()
        self.launch(0)

    def launch(self, phase):
        src = self.part if phase == 0 else self.full
        if phase < 2:
            self.going = [
                self.push(phase, side, src.at[spot(self.dims, self.at(phase, 2, side))], 1 - 2 * side) for side in range(2)
            ]
        else:
            self.going = [
                self.push(phase, slot, src.at[spot(self.dims, self.at(phase, step))], step)
                for slot, step in ((0, 2), (2, 1), (3, -1))
            ]

    def relay(self, phase):
        if phase == 0:
            self.kept.wait()
        if phase == 2:
            return
        for side, step in ((0, 1), (1, -1)):
            self.going[side].wait()
            add_into(self.full, self.dims, self.at(phase, step, side), [self.boxes[phase][side]])
            self.going.append(self.push(phase, 2 + side, self.full.at[spot(self.dims, self.at(phase, step))], step))

    def finish(self, phase):
        if phase < 2:
            for copy in self.going[2:]:
                copy.wait()
            add_into(self.full, self.dims, self.at(phase, 0), self.boxes[phase][2:4])
            self.launch(phase + 1)
            return None
        for copy in self.going:
            copy.wait()
        total = self.full[spot(self.dims, self.at(2, 0))].astype(f32)
        for slot in (0, 2, 3):
            total = total + self.boxes[2][slot][...].astype(f32)
        return total

    @staticmethod
    def scratch(dims, order, slab, dtype):
        shapes = [(*lead(dims), *slab)]
        rest = dims
        for phase, axis in enumerate(order):
            rest = without(rest, axis)
            if phase < 2:
                small = free_sizes(rest, half(order[phase + 1], 0))
            else:
                small = ()
            shapes += [(*small, *slab)] * 2 + [(*lead(rest), *slab)] * 2
        return [pltpu.VMEM(s, dtype) for s in shapes]


OWNED = ("x", "l", "z", "h")
GATHER = (
    (OWNED, ("z", "y", "x")),
    (OWNED, ("x", "z", "y")),
    (OWNED, ("z", "y", "x")),
    (("c", "l", "z", "x", "h"), ("x", "z", "y")),
    (("h", "c", "l", "z", "x"), ("y", "x", "z")),
    (("h", "c", "l", "z", "x"), ("z", "y", "x")),
)
SCATTER = (
    (OWNED, ("z", "y", "x")),
    (OWNED, ("y", "z", "x")),
    (OWNED, ("z", "y", "x")),
    (("l", "z", "x", "h"), ("y", "x", "z")),
    (("h", "l", "z", "x"), ("x", "z", "y")),
    (("h", "l", "z", "x"), ("z", "x", "y")),
)
SLABS = ((24, 512), (24, 512), (16, 128), (16, 512), (16, 1280), (16, 1024))


D, EXP, MAP, PIX = 512, 3072, 9, 81
PAIR = 24
WIDTH = 384
OWNERS = WIDTH // 24
CHUNK = 3
SPAN = CHUNK * MAP * PAIR
EXPAND = 8.0 / math.sqrt(D)
PROJECT = 8.0 / math.sqrt(EXP)
VMEM_BYTES = 60 * 2**20


def sigmoid(v):
    return 0.5 + 0.5 * jnp.tanh(0.5 * v)


def nt(left, right):
    return lax.dot_general(left, right, (((1,), (1,)), ((), ())), preferred_element_type=f32)


def nn(left, right):
    return lax.dot_general(left, right, (((1,), (0,)), ((), ())), preferred_element_type=f32)


def tn(left, right):
    return lax.dot_general(left, right, (((0,), (0,)), ((), ())), preferred_element_type=f32)


def clear_borders(padded):
    zero = jnp.zeros((MAP, PAIR, WIDTH), f32)
    padded[0] = zero
    padded[MAP + 1] = zero


def each_block(body):
    def one(row, _):
        for lane in range(WIDTH // 128):
            for group in range(PAIR // 8):
                body(row, slice(8 * group, 8 * group + 8), slice(128 * lane, 128 * lane + 128))
        return 0

    lax.fori_loop(0, MAP, one, 0)


INSTR, DIMS, BINS, NTOK, FRAMES, HEADS, HD = 744, 11, 256, 8, 6, 8, 64
TABLE = INSTR + 2
ROWS = PAIR * NTOK
PADDED = 2048
SMALL_AT = TABLE - D
LN_EPS = 1e-06
OUT_MULT = 2.0
HIGH = lax.Precision.HIGHEST
FILM = 16.0 / math.sqrt(D)
LEARN = 4.0 / math.sqrt(D)


def norm_fwd(x, gain):
    centre = x - jnp.mean(x, -1, keepdims=True)
    inverse = lax.rsqrt(jnp.mean(centre * centre, -1, keepdims=True) + LN_EPS)
    normed = centre * inverse
    return normed * (1.0 + gain), normed, inverse


def norm_back(normed, inverse, gain, grad_out):
    dnormed = grad_out * (1.0 + gain)
    grad_in = inverse * (
        dnormed
        - jnp.mean(dnormed, -1, keepdims=True)
        - normed * jnp.mean(dnormed * normed, -1, keepdims=True)
    )
    return grad_in, jnp.sum(grad_out * normed, 0, keepdims=True)


def gelu_parts(u):
    c = math.sqrt(2.0 / math.pi)
    square = u * u
    t = jnp.tanh(c * u * (1.0 + 0.044715 * square))
    half = 0.5 * (1.0 + t)
    return u * half, half + 0.5 * u * (1.0 - t * t) * c * (1.0 + 3.0 * 0.044715 * square)


def iota(shape, axis):
    return lax.broadcasted_iota(jnp.int32, shape, axis)


def shifted(v, places):
    tiles = [pltpu.roll(v[:, i : i + 128], (128 - places) % 128, 1) for i in range(0, v.shape[1], 128)]
    return jnp.concatenate(tiles, axis=1)


def only(v, first):
    place = iota(v.shape, 1) & 15
    return jnp.where((place >= first) & (place < first + 4), v, 0.0)


def place_of_feature(start, rows):
    d = iota((rows, D), 1)
    owner = d >> 2
    row = (owner & 1) * 1024 + (owner >> 1) * 16 + 12 + (d & 3)
    return (iota((rows, D), 0) + start == row).astype(bf16)


def over_cells(body, carry):
    many = 16 * PAIR
    carry = lax.fori_loop(
        0, PIX // 16, lambda i, c: body(pl.ds(pl.multiple_of(i * many, many), many), many, c), carry
    )
    return body(slice(PIX // 16 * many, PIX * PAIR), PAIR, carry)


def middle_kernel(
    instr_in, mask_in, part_in, cells_in, misc, one_in, two_in, cam, bins_in,
    dcells, dmisc, one_out, two_out, stats,
    one, two, done_one, done_two, y_hi, y_lo, logit, att, qkv, prob, ctx, up, hid, acc, dlog, lowgrad, turn, part, cells, sems,
):
    core, high = lax.axis_index("mp_1"), lax.axis_index("mp_0")
    fetch_part = pltpu.make_async_copy(part_in, part, sems.at[2])
    fetch_cells = pltpu.make_async_copy(cells_in, cells, sems.at[3])
    fetch_part.start()
    fetch_cells.start()
    fetch_one = pltpu.make_async_copy(one_in, one, sems.at[0])
    fetch_two = pltpu.make_async_copy(two_in, two, sems.at[1])
    fetch_one.start()
    fetch_two.start()
    lanes, images = iota((PAIR, 128), 1), iota((PAIR, 128), 0)
    instr = jnp.zeros((PAIR, 128), jnp.int32)
    for i in range(PAIR // FRAMES):
        instr = jnp.where(lax.div(images, FRAMES) == i, instr_in[high * (PAIR // FRAMES) + i], instr)
    mask = jnp.zeros((PAIR, 128), jnp.int32)
    for i in range(PAIR):
        mask = jnp.where(images == i, mask_in[high * PAIR + i], mask)
    turn[...] = jnp.zeros_like(turn)
    turn[0:DIMS, 0 : 2 * PAIR] = bins_in[...].astype(f32)
    turn[...] = turn[...].T
    bins = turn[pl.ds(pl.multiple_of(high * PAIR, PAIR), PAIR), :].astype(jnp.int32)

    def chosen(tile):
        at = lanes + 128 * tile
        return ((at == instr) | (at == INSTR + cam[0] + cam[1])).astype(f32)

    choose_lo = jnp.concatenate([chosen(i) for i in range(4)], axis=1).astype(bf16)
    choose_hi = jnp.concatenate([chosen(i) for i in range(4, 8)], axis=1).astype(bf16)
    flat = misc[...]
    cvec = only(shifted(nt(choose_lo, flat), 8) + shifted(nt(choose_hi, flat), 12), 0).astype(bf16).astype(f32)
    cvec_4 = shifted(cvec, 124)
    cvec_low, cvec_4_low = cvec.astype(bf16), cvec_4.astype(bf16)
    gamma = nn(cvec_low, flat) * FILM
    beta = nn(cvec_4_low, flat) * FILM
    scale = 1.0 + gamma
    pick = (iota((16, D), 1) == SMALL_AT + iota((16, D), 0)).astype(bf16)
    small = nn(nt(pick, flat).astype(bf16), place_of_feature(0, 2048))
    gains = [small[i : i + 1] for i in range(3)]
    learner = jnp.concatenate([small[3:11], jnp.zeros((120, D), f32)], axis=0).astype(bf16)

    fetch_part.wait()
    fetch_cells.wait()

    def feature(rows, size, _):
        v = part[rows, :].reshape(size // PAIR, PAIR, D) * scale + beta
        v = v.reshape(size, D) + cells[rows, :].astype(f32)
        hi = v.astype(bf16)
        y_hi[rows, :] = hi
        y_lo[rows, :] = (v - hi.astype(f32)).astype(bf16)
        return 0

    over_cells(feature, 0)
    tail = slice(PIX * PAIR, PADDED)
    for ref in (y_hi, y_lo, att, logit):
        ref[tail, :] = jnp.zeros((PADDED - PIX * PAIR, ref.shape[1]), ref.dtype)
    used = slice(0, PIX * PAIR)
    logit[used, :] = (nt(y_hi[used, :], learner) + nt(y_lo[used, :], learner)) * LEARN

    def softmax_over_cells(v):
        v = v.reshape(PIX, PAIR, 128)
        e = jnp.exp(v - jnp.max(v, 0, keepdims=True))
        return e / jnp.sum(e, 0, keepdims=True)

    att[used, :] = softmax_over_cells(logit[used, :]).reshape(PIX * PAIR, 128)
    acc[...] = jnp.zeros_like(acc)

    def gather(i, _):
        rows = pl.ds(pl.multiple_of(i * 512, 512), 512)
        turned = jnp.concatenate(
            [att[pl.ds(pl.multiple_of(i * 512 + 128 * k, 128), 128), :].T[0:NTOK] for k in range(4)], axis=1
        )
        hi = turned.astype(bf16).astype(f32)
        lo = turned - hi
        image = lax.rem(i * 512 + iota((8, 512), 1), PAIR)
        own = [image == 8 * g + iota((8, 512), 0) for g in range(3)]

        def wide(v):
            pieces = [jnp.where(m, v[t : t + 1], 0.0) for t in range(NTOK) for m in own]
            return jnp.concatenate(pieces, axis=0).astype(bf16)

        wide_hi = wide(hi)
        upper = y_hi[rows, :]
        acc[...] += nn(wide_hi, upper) + nn(wide(lo), upper) + nn(wide_hi, y_lo[rows, :])
        return 0

    lax.fori_loop(0, PADDED // 512, gather, 0)
    tok = acc[...].astype(bf16).astype(f32)
    fetch_one.wait()
    fetch_two.wait()

    h1, normed1, inverse1 = norm_fwd(tok, gains[0])
    h1_low = h1.astype(bf16)
    row_q, row_k = iota((ROWS, ROWS), 0), iota((ROWS, ROWS), 1)
    image_q, image_k = lax.rem(row_q, PAIR), lax.rem(row_k, PAIR)
    order_q = image_q * NTOK + lax.div(row_q, PAIR)
    order_k = image_k * NTOK + lax.div(row_k, PAIR)
    seen = (lax.div(image_q, FRAMES) == lax.div(image_k, FRAMES)) & (order_k <= order_q)
    root = HD**-0.5
    acc[...] = jnp.zeros_like(acc)

    def attend(m, _):
        p = nn(h1_low, one[m, :, 0:384]).astype(bf16)
        qkv[m] = p
        outs = []
        for head in range(2):
            q, k, v = (p[:, 128 * j + 64 * head : 128 * j + 64 * head + 64] for j in range(3))
            s = jnp.where(seen, nt(q, k) * root, -1e30)
            e = jnp.exp(s - jnp.max(s, -1, keepdims=True))
            w = e / jnp.sum(e, -1, keepdims=True)
            prob[m, head] = w
            outs.append(nn(w.astype(bf16), v))
        o = jnp.concatenate(outs, axis=1).astype(bf16)
        ctx[m] = o
        acc[...] += nt(o, one[m, :, 384:512])
        return 0

    lax.fori_loop(0, 4, attend, 0)
    x1 = tok + OUT_MULT * acc[...]
    h2, normed2, inverse2 = norm_fwd(x1, gains[1])
    h2_low = h2.astype(bf16)
    acc[...] = x1

    def feed(m, _):
        u = nn(h2_low, two[m, :, 0:512])
        up[m] = u
        low = gelu_parts(u)[0].astype(bf16)
        hid[m] = low
        acc[...] += nt(low, two[m, :, 512:1024])
        return 0

    lax.fori_loop(0, 4, feed, 0)
    x2 = acc[...]
    normed_out, normed3, inverse3 = norm_fwd(x2, gains[2])
    pooled = (jnp.sum(normed_out.reshape(NTOK, PAIR, D), axis=0) * (1.0 / NTOK)).astype(bf16)

    low_half = lanes < 64
    scores = [nn(pooled, one[m, :, 512:1280]) for m in range(4)]
    weight = mask.astype(f32)
    loss = jnp.zeros((PAIR, 128), f32)
    for u in range(6):
        tiles = [s[:, 128 * u : 128 * u + 128] for s in scores]
        top = jnp.maximum(jnp.maximum(tiles[0], tiles[1]), jnp.maximum(tiles[2], tiles[3]))
        left = jnp.max(jnp.where(low_half, top, -jnp.inf), -1, keepdims=True)
        right = jnp.max(jnp.where(low_half, -jnp.inf, top), -1, keepdims=True)
        top = jnp.where(low_half, left, right)
        total = sum(jnp.exp(t - top) for t in tiles)
        left = jnp.sum(jnp.where(low_half, total, 0.0), -1, keepdims=True)
        right = jnp.sum(jnp.where(low_half, 0.0, total), -1, keepdims=True)
        lse = top + jnp.log(jnp.where(low_half, left, right))
        label = jnp.where(low_half, bins[:, 2 * u : 2 * u + 1], bins[:, 2 * u + 1 : 2 * u + 2])
        real = low_half | (2 * u + 1 < DIMS)
        target = jnp.zeros((PAIR, 128), f32)
        for m, t in enumerate(tiles):
            hit = label == (lanes & 63) + 64 * m
            target = target + jnp.where(hit, t, 0.0)
            slope = weight * (jnp.exp(t - lse) - hit.astype(f32))
            dlog[m, :, 128 * u : 128 * u + 128] = jnp.where(real, slope, 0.0).astype(bf16)
        counted = real & ((lanes & 63) == 0)
        loss = loss + weight * (jnp.where(counted, lse, 0.0) - target)
    stats[...] = jnp.zeros_like(stats)
    stats[0:8] = loss[0:8] + loss[8:16] + loss[16:24]
    counts = jnp.where(lanes == 0, weight, 0.0)
    stats[8:16] = counts[0:8] + counts[8:16] + counts[16:24]
    dpooled = jnp.zeros((PAIR, D), f32)
    for m in range(4):
        dpooled = dpooled + nt(dlog[m], one[m, :, 512:1280])
    dnormed = jnp.broadcast_to(dpooled * (1.0 / NTOK), (NTOK, PAIR, D)).reshape(ROWS, D)
    dx2, dgain2 = norm_back(normed3, inverse3, gains[2], dnormed)
    dbranch = dx2.astype(bf16)
    acc[...] = jnp.zeros_like(acc)

    def feed_back(m, _):
        slope = gelu_parts(up[m])[1]
        dup = (nn(dbranch, two[m, :, 512:1024]) * slope).astype(bf16)
        lowgrad[m] = dup
        acc[...] += nt(dup, two[m, :, 0:512])
        return 0

    lax.fori_loop(0, 4, feed_back, 0)
    dx1_norm, dgain1 = norm_back(normed2, inverse2, gains[1], acc[...])
    dx1 = dx2 + dx1_norm
    dattn = dx1.astype(bf16)

    def feed_weights(h, _):
        m = 2 * h + core
        done_one[h, :, 512:1280] = tn(pooled, dlog[m]).astype(bf16)
        done_two[h, :, 0:512] = tn(h2_low, lowgrad[m]).astype(bf16)
        done_two[h, :, 512:1024] = tn(dbranch, hid[m]).astype(bf16)
        done_one[h, :, 384:512] = (tn(dattn, ctx[m]) * OUT_MULT).astype(bf16)
        return 0

    lax.fori_loop(0, 2, feed_weights, 0)
    acc[...] = jnp.zeros_like(acc)

    def attend_back(m, _):
        do = (nn(dattn, one[m, :, 384:512]) * OUT_MULT).astype(bf16)
        p = qkv[m]
        dq, dk, dv = [], [], []
        for head in range(2):
            q, k, v = (p[:, 128 * j + 64 * head : 128 * j + 64 * head + 64] for j in range(3))
            w = prob[m, head]
            d = do[:, 64 * head : 64 * head + 64]
            dp = nt(d, v)
            dv.append(tn(w.astype(bf16), d))
            ds = (w * (dp - jnp.sum(w * dp, -1, keepdims=True))).astype(bf16)
            dq.append(nn(ds, k) * root)
            dk.append(tn(ds, q) * root)
        g = jnp.concatenate([*dq, *dk, *dv], axis=1).astype(bf16)
        lowgrad[m, :, 0:384] = g
        acc[...] += nt(g, one[m, :, 0:384])
        return 0

    lax.fori_loop(0, 4, attend_back, 0)

    def attend_weights(h, _):
        done_one[h, :, 0:384] = tn(h1_low, lowgrad[2 * h + core, :, 0:384]).astype(bf16)
        return 0

    lax.fori_loop(0, 2, attend_weights, 0)
    dtok_norm, dgain0 = norm_back(normed1, inverse1, gains[0], acc[...])
    acc[...] = dx1 + dtok_norm

    send_one = pltpu.make_async_copy(done_one, one_out, sems.at[0])
    send_two = pltpu.make_async_copy(done_two, two_out, sems.at[1])
    send_one.start()
    send_two.start()
    dtok_hi = acc[...].astype(bf16)
    dtok_lo = (acc[...] - dtok_hi.astype(f32)).astype(bf16)
    same = lax.rem(iota((PAIR, ROWS), 1), PAIR) == iota((PAIR, ROWS), 0)
    token_of = (lax.div(iota((128, ROWS), 1), PAIR) == iota((128, ROWS), 0)).astype(bf16)

    def own_image(v):
        return jnp.where(same, v.reshape(-1, PAIR, ROWS), 0.0).reshape(-1, ROWS)

    def halves(v):
        hi = v.astype(bf16)
        return hi, (v - hi.astype(f32)).astype(bf16)

    def slope_of(rows, size, _):
        upper = y_hi[rows, :]
        g = own_image(nt(upper, dtok_hi) + nt(upper, dtok_lo) + nt(y_lo[rows, :], dtok_hi))
        hi, lo = halves(g)
        logit[rows, :] = nt(hi, token_of) + nt(lo, token_of)
        return 0

    over_cells(slope_of, 0)
    a = att[used, :].reshape(PIX, PAIR, 128)
    da = logit[used, :].reshape(PIX, PAIR, 128)
    logit[used, :] = (a * (da - jnp.sum(a * da, 0, keepdims=True)) * LEARN).reshape(PIX * PAIR, 128)
    turned = jnp.concatenate([logit[128 * k : 128 * k + 128, :].T[0:NTOK] for k in range(PADDED // 128)], axis=1)
    upper = turned.astype(bf16).astype(f32)
    both = jnp.concatenate([upper, turned - upper], axis=0).astype(bf16)
    sums = nn(both, y_hi[...])
    dlearner = sums[0:8] + sums[8:16] + nn(both, y_lo[...])[0:8]

    def spread(rows, size, sums):
        hi, lo = halves(att[rows, :])
        hi, lo = own_image(nn(hi, token_of)).astype(bf16), own_image(nn(lo, token_of)).astype(bf16)
        slope_hi, slope_lo = halves(logit[rows, :])
        dy = nn(hi, dtok_hi) + nn(lo, dtok_hi) + nn(hi, dtok_lo) + nn(slope_hi, learner) + nn(slope_lo, learner)
        dy = dy.reshape(size // PAIR, PAIR, D)
        dcells[rows, :] = (dy * scale).astype(bf16).reshape(size, D)
        p = part[rows, :].reshape(size // PAIR, PAIR, D)
        return sums[0] + jnp.sum(dy * p, 0), sums[1] + jnp.sum(dy, 0)

    zero = jnp.zeros((PAIR, D), f32)
    dgamma, dbeta = over_cells(spread, (zero, zero))
    dgamma, dbeta = dgamma.astype(bf16), dbeta.astype(bf16)
    dcvec = only(nt(dgamma, flat) + shifted(nt(dbeta, flat), 4), 0) * FILM
    high = dcvec.astype(bf16).astype(f32)
    rest = dcvec - high
    dsmall = jnp.concatenate([dgain0, dgain1, dgain2, dlearner, jnp.zeros((5, D), f32)], axis=0).astype(bf16)
    mine = pl.ds(pl.multiple_of(core * 1024, 1024), 1024)
    lhs = jnp.concatenate(
        [cvec, cvec_4, shifted(high, 120), shifted(rest, 120), shifted(high, 116), shifted(rest, 116)], axis=0
    )
    lhs = jnp.where(core == 0, lhs[:, 0:1024], lhs[:, 1024:2048])
    lhs = jnp.concatenate([lhs, nt(dsmall, place_of_feature(core * 1024, 1024))], axis=0).astype(bf16)
    rhs = jnp.concatenate([dgamma, dbeta, choose_lo, choose_lo, choose_hi, choose_hi, pick], axis=0)
    result = tn(lhs, rhs)
    film_rows = (iota((1024, D), 0) & 15) < 8
    dmisc[...] = jnp.where(film_rows, result * FILM, result).astype(bf16)
    send_one.wait()
    send_two.wait()


def middle(instr, mask, part, cells, misc, one, two, cam, bins):
    vmem = pl.BlockSpec(memory_space=pltpu.VMEM)
    return pl.pallas_call(
        middle_kernel,
        out_shape=[
            jax.ShapeDtypeStruct((PIX * PAIR, D), bf16),
            jax.ShapeDtypeStruct((1024, D), bf16),
            jax.ShapeDtypeStruct((2, D, 1280), bf16),
            jax.ShapeDtypeStruct((2, D, 1024), bf16),
            jax.ShapeDtypeStruct((16, 128), f32),
        ],
        in_specs=[pl.BlockSpec(memory_space=pltpu.SMEM)] * 2 + [ANY] * 2 + [vmem] + [ANY] * 2 + [vmem] * 2,
        out_specs=[vmem, vmem, ANY, ANY, vmem],
        scratch_shapes=[
            pltpu.VMEM((4, D, 1280), bf16),
            pltpu.VMEM((4, D, 1024), bf16),
            pltpu.VMEM((2, D, 1280), bf16),
            pltpu.VMEM((2, D, 1024), bf16),
            pltpu.VMEM((PADDED, D), bf16),
            pltpu.VMEM((PADDED, D), bf16),
            pltpu.VMEM((PADDED, 128), f32),
            pltpu.VMEM((PADDED, 128), f32),
            pltpu.VMEM((4, ROWS, 384), bf16),
            pltpu.VMEM((4, 2, ROWS, ROWS), f32),
            pltpu.VMEM((4, ROWS, 128), bf16),
            pltpu.VMEM((4, ROWS, 512), f32),
            pltpu.VMEM((4, ROWS, 512), bf16),
            pltpu.VMEM((ROWS, D), f32),
            pltpu.VMEM((4, PAIR, 768), bf16),
            pltpu.VMEM((4, ROWS, 512), bf16),
            pltpu.VMEM((128, 128), f32),
            pltpu.VMEM((PIX * PAIR, D), f32),
            pltpu.VMEM((PIX * PAIR, D), bf16),
            pltpu.SemaphoreType.DMA((4,)),
        ],
        compiler_params=pltpu.CompilerParams(vmem_limit_bytes=VMEM_BYTES),
    )(instr, mask, part, cells, misc, one, two, cam, bins)


STEPS = 4
BLOCK = (PIX, PAIR, WIDTH)


def tap_places():
    row, col = iota((OWNERS * 128, WIDTH), 0), iota((OWNERS * 128, WIDTH), 1)
    return (((row >> 7) * 24 + (row & 127) == col) & ((row & 127) < 24)).astype(bf16)


def to_cells(frames, cells):
    rows = 8 * PAIR
    at, of = iota((rows, rows), 0), iota((rows, rows), 1)
    turn = (lax.rem(at, PAIR) * 8 + lax.div(at, PAIR) == of).astype(bf16)
    for first in (*range(0, PIX - 8, 8), PIX - 8):
        block = frames[:, :, first : first + 8, :].reshape(rows, D)
        cells[first * PAIR : first * PAIR + rows, :] = nn(turn, block).astype(bf16)


def fill_shards(conv, cond, small, attn, mlp, head, camera, core, shards, staged, tap_tile, cam):
    shards[0][...] = conv[:, 0:D].astype(bf16)
    shards[1][...] = conv[:, D : 2 * D].astype(bf16)
    tap_tile[...] = jnp.zeros_like(tap_tile)
    tap_tile[0:24, 0:9] = conv[:, 2 * D :]
    shards[2][...] = tap_tile[...].T[0:16].astype(bf16)
    staged[...] = jnp.zeros_like(staged)
    for i in range(3):
        staged[4 * i : 4 * i + 4, :] = cond[:, D * i : D * i + D]
    staged[12:16, 0:SMALL_AT] = cond[:, 3 * D :]
    staged[12:16, SMALL_AT : SMALL_AT + 11] = small[...]
    shards[3][...] = staged[...].astype(bf16)
    for j in range(4):
        shards[4][:, 128 * j : 128 * j + 128] = attn[j].astype(bf16)
    for k in range(0, DIMS - 1, 2):
        both = jnp.concatenate([head[k], head[k + 1]], axis=1)
        shards[4][:, 512 + 64 * k : 640 + 64 * k] = both.astype(bf16)
    last = jnp.concatenate([head[DIMS - 1], jnp.zeros((16, 64), f32)], axis=1)
    shards[4][:, 1152:1280] = last.astype(bf16)
    for j in range(2):
        shards[5][:, 512 * j : 512 * j + 512] = mlp[j].astype(bf16)
    row = iota((PAIR, 128), 0)
    found = jnp.zeros((PAIR, 128), jnp.int32)
    for i in range(PAIR // 2):
        found = jnp.where(row == core * (PAIR // 2) + i, camera[i], found)
    cam[...] = found


def forward_kernel(plan, *refs):
    n = len(plan)
    frames, camera = refs[0:2]
    masters = refs[2 : 2 + n]
    refs = refs[2 + n :]
    cam2, cells_out, project_out, taps_out, misc_out, one_out, two_out, pre_out, deep_out, total_out = refs[:10]
    frames2, cells, expand, project, slabs, taps, places, act, pre, deep, part, part_low, other_low = refs[10:23]
    shards, staged, tap_tile, cam = refs[23 : 23 + n], refs[23 + n], refs[24 + n], refs[25 + n]
    send, recv, fsend, frecv, local, kept, swap_send, swap_recv = refs[26 + n :]
    me = here()
    count = announce(me)
    fill_shards(*masters, camera, me["c"][0], shards, staged, tap_tile, cam)
    meet(count)
    swaps = []
    for i, (src, out) in enumerate(((frames, frames2), (cam, cam2))):
        where = out.at[me["c"][0]]
        mine = pltpu.make_async_copy(src, where, local.at[n + i])
        mine.start()
        swaps += [mine, remote(src, where, swap_send.at[i], swap_recv.at[i], "c", me["c"][1])]
    outs = (expand, project, slabs, misc_out, one_out, two_out)
    jobs = [
        Gather(me, dims, order, shards[b], outs[b], send.at[b], recv.at[b], fsend.at[b], frecv.at[b], local.at[b])
        for b, (dims, order) in enumerate(plan)
    ]
    early, late, middle_one, outer = (jobs[0], jobs[2]), (jobs[1],), (jobs[4],), (jobs[3], jobs[5])
    first, rest = jobs[:3], jobs[3:]

    def relay(some, phase):
        for job in some:
            job.relay(phase)

    def finish(some, phase, launch=True):
        for job in some:
            job.finish(phase, launch)

    for job in jobs:
        job.begin()
    relay(first, 0)
    finish(first, 0)
    clear_borders(act)
    places[...] = tap_places()
    relay(rest, 0)
    finish(rest, 0)
    relay(first, 1)
    relay(rest, 1)
    finish(first, 1)
    finish(middle_one, 1)
    finish(outer, 1, False)
    part[...] = jnp.zeros_like(part)
    swaps[0].wait()
    swaps[1].wait()
    to_cells(frames2, cells)
    saves = []

    def save(src, dst, number):
        copy = pltpu.make_async_copy(src, dst, kept.at[number])
        copy.start()
        saves.append(copy)

    save(cells, cells_out, 0)
    spans, leaves = [None] * STEPS, []
    for step in range(STEPS):
        slot = step % 2
        at = me["x"][(0, -1, 1, 2)[step]]
        if step == 1:
            relay(early, 2)
            relay(late, 2)
            for job in outer:
                job.launch(2)
        if step == 2:
            relay(middle_one, 2)
        if step == 3:
            finish(early, 2)
            relay(outer, 2)
        if step >= 2:
            for copy in spans[step - 2]:
                copy.wait()
        weight = expand[at].reshape(WIDTH, D)
        tap = slabs[at].reshape(OWNERS, 16, 128)
        side = jnp.concatenate([tap[i] for i in range(OWNERS)], axis=1)
        taps[at] = nn(side, places[...]) * (8.0 / 3.0)

        def enter(i, _, weight=weight, slot=slot):
            rows = pl.ds(pl.multiple_of(i * SPAN, SPAN), SPAN)
            e = (nt(cells[rows, :], weight) * EXPAND).reshape(CHUNK * MAP, PAIR, WIDTH)
            pre[slot, pl.ds(i * CHUNK * MAP, CHUNK * MAP)] = e
            act[pl.ds(1 + i * CHUNK, CHUNK)] = (e * sigmoid(e)).reshape(CHUNK, MAP, PAIR, WIDTH)
            return 0

        lax.fori_loop(0, MAP // CHUNK, enter, 0)
        out = [pltpu.make_async_copy(pre.at[slot], pre_out.at[at], kept.at[3 + 2 * step])]
        out[0].start()

        def mix(row, subs, cols, slot=slot, at=at):
            near = act[pl.ds(row, 3), :, subs, cols]
            tap = [jnp.broadcast_to(taps[at, t : t + 1, cols], (8, 128)) for t in range(9)]
            for col in range(MAP):
                total = None
                for t in range(9):
                    p = col + t % 3 - 1
                    if 0 <= p < MAP:
                        term = near[t // 3, p] * tap[t]
                        total = term if total is None else total + term
                deep[slot, row * MAP + col, subs, cols] = total

        each_block(mix)
        out.append(pltpu.make_async_copy(deep.at[slot], deep_out.at[at], kept.at[4 + 2 * step]))
        out[1].start()
        spans[step] = out
        if step == 3:
            finish(middle_one, 2)

        def leave(i, _, at=at, slot=slot):
            back = project[at].reshape(WIDTH, D)
            rows = pl.ds(pl.multiple_of(i * SPAN, SPAN), SPAN)
            v = deep[slot, pl.ds(i * CHUNK * MAP, CHUNK * MAP)].reshape(SPAN, WIDTH)
            part[rows, :] += nn((v * sigmoid(v)).astype(bf16), back) * PROJECT
            return 0

        leaves.append(leave)
        if step == 1:
            finish(late, 2)
            save(project, project_out, 1)
            lax.fori_loop(0, MAP // CHUNK, leaves[0], 0)
        if 0 < step < STEPS - 1:
            lax.fori_loop(0, MAP // CHUNK, leave, 0)
    save(taps, taps_out, 2)
    trades = []
    for i in range(MAP // CHUNK):
        leave(i, 0)
        part_low[i] = part[i * SPAN : (i + 1) * SPAN, :].astype(bf16)
        trades.append(
            remote(part_low.at[i], other_low.at[i], swap_send.at[2 + i], swap_recv.at[2 + i], "c", me["c"][1])
        )
    finish(outer, 2)
    for i, copy in enumerate(trades):
        copy.wait()
        rows = slice(i * SPAN, (i + 1) * SPAN)
        part[rows, :] += other_low[i].astype(f32)
        save(part.at[rows], total_out.at[rows], 3 + 2 * STEPS + i)
    for step in (STEPS - 2, STEPS - 1):
        saves += spans[step]
    for job in jobs:
        job.end()
    for copy in saves + swaps[2:]:
        copy.wait()


def forward(frames, camera, masters, plan, collective_id):
    n = len(plan)
    maps = jax.ShapeDtypeStruct((STEPS, *BLOCK), f32)
    shape = jax.ShapeDtypeStruct
    full = [shape((*lead(dims), *slab), bf16) for slab, (dims, _) in zip(SLABS, plan)]
    rows = PIX * PAIR
    return pl.pallas_call(
        functools.partial(forward_kernel, plan),
        out_shape=[
            shape((2, PAIR, 128), jnp.int32),
            shape((rows, D), bf16),
            full[1],
            shape((STEPS, 16, WIDTH), f32),
            *full[3:],
            maps,
            maps,
            shape((rows, D), f32),
        ],
        in_specs=[ANY, pl.BlockSpec(memory_space=pltpu.SMEM)] + [INVMEM] * n,
        out_specs=[ANY] * 10,
        scratch_shapes=[
            pltpu.VMEM((2, *frames.shape), bf16),
            pltpu.VMEM((rows, D), bf16),
            pltpu.VMEM(full[0].shape, bf16),
            pltpu.VMEM(full[1].shape, bf16),
            pltpu.VMEM(full[2].shape, bf16),
            pltpu.VMEM((STEPS, 16, WIDTH), f32),
            pltpu.VMEM((OWNERS * 128, WIDTH), bf16),
            pltpu.VMEM((MAP + 2, MAP, PAIR, WIDTH), f32),
            pltpu.VMEM((2, *BLOCK), f32),
            pltpu.VMEM((2, *BLOCK), f32),
            pltpu.VMEM((rows, D), f32),
            pltpu.VMEM((MAP // CHUNK, SPAN, D), bf16),
            pltpu.VMEM((MAP // CHUNK, SPAN, D), bf16),
            *[pltpu.VMEM(slab, bf16) for slab in SLABS],
            pltpu.VMEM((16, D), f32),
            pltpu.VMEM((128, 128), f32),
            pltpu.VMEM((PAIR, 128), jnp.int32),
            pltpu.SemaphoreType.DMA((n, 3, 4)),
            pltpu.SemaphoreType.DMA((n, 3, 4)),
            pltpu.SemaphoreType.DMA((n, 7)),
            pltpu.SemaphoreType.DMA((n, 7)),
            pltpu.SemaphoreType.DMA((n + 2,)),
            pltpu.SemaphoreType.DMA((3 + 2 * STEPS + MAP // CHUNK,)),
            pltpu.SemaphoreType.DMA((2 + MAP // CHUNK,)),
            pltpu.SemaphoreType.DMA((2 + MAP // CHUNK,)),
        ],
        compiler_params=pltpu.CompilerParams(
            collective_id=collective_id, has_side_effects=True, vmem_limit_bytes=VMEM_BYTES
        ),
    )(frames, camera, *masters)


class Blocks:
    def __init__(self, me, dims, order, full, room, send, recv):
        self.me, self.dims, self.order, self.full = me, dims, order, full
        self.halves, self.wholes, self.slabs, self.last = room
        self.send, self.recv = send, recv
        self.going = [None] * STEPS
        self.sent = []

    def at(self, step, **more):
        return {"x": self.me["x"][BACK[step]], **more}

    def push(self, step, slot, src, box, axis, move):
        return remote(src, box, self.send.at[step, slot], self.recv.at[step, slot], axis, self.me[axis][move])

    def launch(self, step):
        a, b, _ = self.order
        self.going[step] = [
            self.push(
                step, side, self.full.at[spot(self.dims, self.at(step, **{a: self.me[a][2]}, **half(b, side)))],
                self.halves.at[step, side], a, 1 - 2 * side,
            )
            for side in range(2)
        ]

    def relay(self, step):
        a, b, _ = self.order
        for side, move in ((0, 1), (1, -1)):
            self.going[step][side].wait()
            pos = {a: self.me[a][move]}
            add_into(self.full, self.dims, self.at(step, **pos, **half(b, side)), [self.halves.at[step, side]])
            where = self.full.at[spot(self.dims, self.at(step, **pos))]
            self.going[step].append(self.push(step, 2 + side, where, self.wholes.at[step, side], a, move))

    def middle(self, step):
        a, b, _ = self.order
        for copy in self.going[step][2:]:
            copy.wait()
        own = {a: self.me[a][0]}
        add_into(self.full, self.dims, self.at(step, **own), [self.wholes.at[step, side] for side in range(2)])
        self.going[step] = [
            self.push(
                step, 4 + i, self.full.at[spot(self.dims, self.at(step, **own, **{b: self.me[b][move]}))],
                self.slabs.at[step, i], b, move,
            )
            for i, move in enumerate((2, 1, -1))
        ]

    def finish(self, step):
        a, b, _ = self.order
        for copy in self.going[step]:
            copy.wait()
        index = spot(self.dims, self.at(step, **{a: self.me[a][0], b: self.me[b][0]}))
        total = self.full[index].astype(f32)
        for i in range(3):
            total = total + self.slabs[step, i].astype(f32)
        if BACK[step] != 0:
            self.full[index] = total.astype(bf16)
            self.sent.append(self.push(step, 7, self.full.at[index], self.last.at[step], "x", BACK[step]))
        return total

    def close(self, total):
        for copy in self.sent:
            copy.wait()
        for i in range(STEPS - 1):
            total = total + self.last[i].astype(f32)
        return total

    @staticmethod
    def scratch(dims, order, slab):
        rest = without(without(dims, "x"), order[0])
        small = free_sizes(rest, half(order[1], 0))
        shapes = [
            (*lead(dims), *slab), (STEPS, 2, *small, *slab), (STEPS, 2, *lead(rest), *slab), (STEPS, 3, *slab),
            (STEPS - 1, *slab),
        ]
        return [pltpu.VMEM(s, bf16) for s in shapes]


BACK = (2, 1, -1, 0)


def backward_kernel(plan, *refs):
    n = len(plan)
    cells_in, dcells_in, project_in, taps_in, pre_in, deep_in, stats = refs[:7]
    parts = refs[7 : 7 + n - 3]
    refs = refs[4 + n :]
    stats_out, outs = refs[0], refs[1 : 1 + n]
    refs = refs[1 + n :]
    cells, dcells, project, taps, places, pre, deep, spread, mid, dpre, acc = refs[:11]
    refs = refs[11:]
    blocks_room, rest_room = refs[:15], refs[15 : 15 + 13 * (n - 3)]
    tile, tile_box, bsend, brecv, send, recv, local, kept, tsend, trecv = refs[15 + 13 * (n - 3) :]
    me = here()
    loads = []
    for i, (src, dst) in enumerate(((cells_in, cells), (dcells_in, dcells), (project_in, project), (taps_in, taps))):
        copy = pltpu.make_async_copy(src, dst, kept.at[i])
        copy.start()
        loads.append(copy)

    def fetch(step):
        at = me["x"][BACK[step]]
        pair = []
        for i, (src, dst) in enumerate(((pre_in, pre), (deep_in, deep))):
            copy = pltpu.make_async_copy(src.at[at], dst.at[step % 2], kept.at[4 + 2 * step + i])
            copy.start()
            pair.append(copy)
        return pair

    maps = [fetch(0), fetch(1), None, None]
    meet(announce(me, wide=True))
    rest = []
    for b, (dims, order) in enumerate(plan[3:]):
        own = rest_room[13 * b : 13 * b + 13]
        boxes = [own[1:5], own[5:9], own[9:13]]
        rest.append(Scatter(me, dims, order, parts[b], own[0], boxes, send.at[b], recv.at[b], local.at[b]))
    first = [
        Blocks(me, dims, order, blocks_room[5 * b], blocks_room[5 * b + 1 : 5 * b + 5], bsend.at[b], brecv.at[b])
        for b, (dims, order) in enumerate(plan[:3])
    ]
    for job in rest:
        job.begin()
    clear_borders(spread)
    places[...] = tap_places()
    loads[1].wait()
    loads[2].wait()
    square = jnp.zeros((8, 128), f32)

    def close_rest(square):
        for b, job in enumerate(rest):
            total = job.finish(2)
            outs[3 + b][...] = total
            square = square + folded(total * total)
        return square

    for step in range(STEPS):
        slot = step % 2
        at = me["x"][BACK[step]]
        for copy in maps[step]:
            copy.wait()
        back = project[at].reshape(WIDTH, D)

        def enter(i, _, back=back, slot=slot):
            rows = pl.ds(pl.multiple_of(i * SPAN, SPAN), SPAN)
            dmid = nt(dcells[rows, :], back) * PROJECT
            v = deep[slot, pl.ds(i * CHUNK * MAP, CHUNK * MAP)].reshape(SPAN, WIDTH)
            s = sigmoid(v)
            m = v * s
            mid[rows, :] = m.astype(bf16)
            spread[pl.ds(1 + i * CHUNK, CHUNK)] = (dmid * (s + m * (1.0 - s))).reshape(CHUNK, MAP, PAIR, WIDTH)
            return 0

        lax.fori_loop(0, MAP // CHUNK, enter, 0)
        if step > 0:
            for job in first:
                job.relay(step - 1)
        if step > 1:
            for job in first:
                job.finish(step - 2)
        if step == 1:
            for job in rest:
                job.relay(0)
        if step == 2:
            for job in rest:
                job.finish(0)
        if step == 3:
            for job in rest:
                job.finish(1)
        acc[...] = jnp.zeros_like(acc)
        if step == 0:
            loads[0].wait()
            loads[3].wait()

        def mix(row, subs, cols, slot=slot, at=at):
            near = spread[pl.ds(row, 3), :, subs, cols]
            tap = [jnp.broadcast_to(taps[at, t : t + 1, cols], (8, 128)) for t in range(9)]
            sums = [None] * 9
            for col in range(MAP):
                e = pre[slot, row * MAP + col, subs, cols]
                s = sigmoid(e)
                a = e * s
                total = None
                for t in range(9):
                    p = col + 1 - t % 3
                    if 0 <= p < MAP:
                        g = near[2 - t // 3, p]
                        term = g * tap[t]
                        total = term if total is None else total + term
                        term = g * a
                        sums[t] = term if sums[t] is None else sums[t] + term
                dpre[row * MAP + col, subs, cols] = total * (s + a * (1.0 - s))
            for t in range(9):
                acc[t, :, cols] += sums[t]

        each_block(mix)
        if step + 2 < STEPS:
            maps[step + 2] = fetch(step + 2)
        if step == 2:
            for job in rest:
                job.relay(1)
        if step > 0:
            for job in first:
                job.middle(step - 1)
        owned = (2, 4, 2, 24, D)
        low = dpre[...].reshape(PIX * PAIR, WIDTH).astype(bf16)
        first[0].full[at] = (tn(low, cells[...]) * EXPAND).astype(bf16).reshape(owned)
        first[1].full[at] = (tn(mid[...], dcells[...]) * PROJECT).astype(bf16).reshape(owned)
        dtaps = jnp.concatenate([jnp.sum(acc[...], axis=1) * (8.0 / 3.0), jnp.zeros((7, WIDTH), f32)], axis=0)
        side = nt(dtaps.astype(bf16), places[...]).astype(bf16)
        for i in range(OWNERS):
            first[2].full[at, i // 8, (i // 2) % 4, i % 2] = side[:, 128 * i : 128 * i + 128]
        for job in first:
            job.launch(step)
    for job in first:
        job.finish(STEPS - 2)
    square = close_rest(square)
    for job in first:
        job.relay(STEPS - 1)
    for job in first:
        job.middle(STEPS - 1)
    for b, job in enumerate(first):
        total = job.close(job.finish(STEPS - 1))
        outs[b][...] = total
        square = square + folded(total * total)
    lines = [jnp.sum(v, 0, keepdims=True) for v in (stats[0:8], stats[8:16], square)]
    tile[0] = jnp.concatenate([*lines, jnp.zeros((5, 128), f32)], axis=0)
    number = 0
    for phase, (one, two) in enumerate((("c", "x"), ("y", "z"))):
        spans = [range(2 if a == "c" else RING) for a in (one, two)]
        moves = [{a: k for a, k in ((one, j), (two, k)) if k} for j in spans[0] for k in spans[1] if j or k]
        copies = []
        for move in moves:
            copy = pltpu.make_async_remote_copy(
                src_ref=tile.at[phase], dst_ref=tile_box.at[number], send_sem=tsend.at[number],
                recv_sem=trecv.at[number], device_id=moved(me, move), device_id_type=MESH_ID,
            )
            copy.start()
            copies.append(copy)
            number += 1
        for copy in copies:
            copy.wait()
        total = tile[phase]
        for i in range(number - len(copies), number):
            total = total + tile_box[i]
        tile[phase + 1] = total
    stats_out[...] = tile[2]


def backward(cells, dcells, project, taps, pre, deep, stats, parts, slabs, plan, collective_id):
    n = len(plan)
    shape = jax.ShapeDtypeStruct
    rows = PIX * PAIR
    room = []
    for (dims, order), slab in zip(plan[:3], slabs[:3]):
        room += Blocks.scratch(dims, order, slab)
    for (dims, order), slab in zip(plan[3:], slabs[3:]):
        room += Scatter.scratch(dims, order, slab, bf16)
    return pl.pallas_call(
        functools.partial(backward_kernel, plan),
        out_shape=[shape((8, 128), f32)] + [shape(s, f32) for s in slabs],
        in_specs=[ANY] * 6 + [INVMEM] + [ANY] * (n - 3),
        out_specs=[INVMEM] * (1 + n),
        scratch_shapes=[
            pltpu.VMEM((rows, D), bf16),
            pltpu.VMEM((rows, D), bf16),
            pltpu.VMEM(project.shape, bf16),
            pltpu.VMEM(taps.shape, f32),
            pltpu.VMEM((OWNERS * 128, WIDTH), bf16),
            pltpu.VMEM((2, *BLOCK), f32),
            pltpu.VMEM((2, *BLOCK), f32),
            pltpu.VMEM((MAP + 2, MAP, PAIR, WIDTH), f32),
            pltpu.VMEM((rows, WIDTH), bf16),
            pltpu.VMEM(BLOCK, f32),
            pltpu.VMEM((9, 8, WIDTH), f32),
            *room,
            pltpu.VMEM((3, 8, 128), f32),
            pltpu.VMEM((22, 8, 128), f32),
            pltpu.SemaphoreType.DMA((3, STEPS, 8)),
            pltpu.SemaphoreType.DMA((3, STEPS, 8)),
            pltpu.SemaphoreType.DMA((n - 3, 3, 4)),
            pltpu.SemaphoreType.DMA((n - 3, 3, 4)),
            pltpu.SemaphoreType.DMA((n - 3,)),
            pltpu.SemaphoreType.DMA((4 + 2 * STEPS,)),
            pltpu.SemaphoreType.DMA((22,)),
            pltpu.SemaphoreType.DMA((22,)),
        ],
        compiler_params=pltpu.CompilerParams(
            collective_id=collective_id, has_side_effects=True, vmem_limit_bytes=VMEM_BYTES
        ),
    )(cells, dcells, project, taps, pre, deep, stats, *parts)


IMAGES = 12
DP_MP = NAMES
DP = ("dp_0", "dp_1", "dp_2")
MP = ("mp_0", "mp_1")
CLIP_NORM = 0.02
BETA_ONE = 0.9
BETA_TWO = 0.999
ADAM_EPS = 1e-08
DECAY = 0.01
RATES = (0.1, 0.1, 0.2, 0.05, 0.05, 0.2)


def adam_kernel(count_ref, totals, gexpand, gproject, gtaps, gmisc, gone, gtwo, *refs):
    states = [refs[3 * i : 3 * i + 3] for i in range(6)]
    loss_ref, norm_ref = refs[18:20]
    outs = [refs[20 + 3 * i : 23 + 3 * i] for i in range(6)]

    def total(line):
        return jnp.sum(totals[line : line + 1, :], axis=(0, 1), keepdims=True)

    scored = 0.5 * total(1)
    norm = jnp.sqrt(total(2)) / scored
    factor = jnp.minimum(1.0, CLIP_NORM / norm) / scored
    loss_ref[0] = (0.5 * total(0) / scored)[0, 0]
    norm_ref[0] = norm[0, 0]
    steps = jnp.full((1, 1), count_ref[0], jnp.int32).astype(f32)
    z = steps * math.log(BETA_TWO)
    grown_two = -z * (1.0 + z / 2.0 * (1.0 + z / 3.0 * (1.0 + z / 4.0 * (1.0 + z / 5.0))))
    grown_one = 1.0 - jnp.exp(steps * math.log(BETA_ONE))

    def update(group, index, grad):
        master, first, second = (ref[index] for ref in states[group])
        grad = grad * factor
        first = BETA_ONE * first + (1.0 - BETA_ONE) * grad
        second = BETA_TWO * second + (1.0 - BETA_TWO) * grad * grad
        step = first / grown_one / (jnp.sqrt(second / grown_two) + ADAM_EPS) + DECAY * master
        outs[group][0][index] = master - RATES[group] * step
        outs[group][1][index] = first
        outs[group][2][index] = second

    every = slice(None)
    update(0, (every, slice(0, D)), gexpand[...])
    update(0, (every, slice(D, 2 * D)), gproject[...])
    taps = jnp.concatenate([gtaps[...], jnp.zeros((112, 128), f32)], axis=0).T
    update(0, (every, slice(2 * D, 2 * D + 9)), taps[0:24, 0:9])
    for i in range(3):
        update(1, (every, slice(D * i, D * i + D)), gmisc[4 * i : 4 * i + 4, :])
    update(1, (every, slice(3 * D, 2 * D + TABLE)), gmisc[12:16, 0:SMALL_AT])
    update(2, (every, every), gmisc[12:16, SMALL_AT : SMALL_AT + 11])
    for j in range(4):
        update(3, j, gone[:, 128 * j : 128 * j + 128])
    for j in range(2):
        update(4, j, gtwo[:, 512 * j : 512 * j + 512])
    for k in range(DIMS):
        update(5, k, gone[:, 512 + 64 * k : 576 + 64 * k])


def adam(step_count, totals, grads, states):
    smem = pl.BlockSpec(memory_space=pltpu.SMEM)
    one = jax.ShapeDtypeStruct((1,), f32)
    return pl.pallas_call(
        adam_kernel,
        out_shape=[one, one] + [jax.ShapeDtypeStruct(s.shape, f32) for s in states],
        in_specs=[smem] + [INVMEM] * (1 + len(grads) + len(states)),
        out_specs=[smem, smem] + [INVMEM] * len(states),
    )(step_count, totals, *grads, *states)


def per_device(
    frames, camera_ids, instruction_ids, action_bins, final_mask, step_count,
    conv_w, conv_m1, conv_m2, cond_w, cond_m1, cond_m2, small_w, small_m1, small_m2,
    attn_w, attn_m1, attn_m2, mlp_w, mlp_m1, mlp_m2, head_w, head_m1, head_m2,
):
    states = [
        *[v.T for v in (conv_w, conv_m1, conv_m2, cond_w, cond_m1, cond_m2, small_w, small_m1, small_m2)],
        *(attn_w, attn_m1, attn_m2, mlp_w, mlp_m1, mlp_m2),
        *[v.transpose(1, 0, 2) for v in (head_w, head_m1, head_m2)],
    ]
    cam2, cells, project, taps, misc_all, one_all, two_all, pre, deep, part = forward(
        frames, camera_ids, states[0::3], GATHER, 1
    )
    dcells, dmisc, done_one, done_two, stats = middle(
        instruction_ids,
        final_mask,
        part,
        cells,
        misc_all.reshape(2048, D),
        one_all.reshape(4, D, 1280),
        two_all.reshape(4, D, 1024),
        cam2,
        action_bins.T,
    )
    parts = [
        g.reshape(*lead(dims), *slab)
        for g, slab, (dims, _) in zip((dmisc, done_one, done_two), SLABS[3:], SCATTER[3:])
    ]
    totals, *grads = backward(cells, dcells, project, taps, pre, deep, stats, parts, SLABS, SCATTER, 2)
    loss, norm, *new = adam(step_count, totals, grads, states)
    new = [v.T for v in new[:9]] + new[9:15] + [v.transpose(1, 0, 2) for v in new[15:]]
    return loss.reshape(()), norm.reshape(()), *new


def solution(mesh):
    torus = Mesh(mesh.devices.reshape(2, 4, 4, 2, 2), NAMES)
    weights = (
        *[P(None, DP_MP)] * 9,
        *[P(None, DP, MP)] * 6,
        *[P(DP, None, MP)] * 3,
    )
    data = (P(DP_MP, None, None), P(DP_MP), P(DP), P(DP, None), P(DP), P())
    return jax.shard_map(
        per_device, mesh=torus, in_specs=(*data, *weights), out_specs=(P(), P(), *weights), check_vma=False
    )
```

```python
import functools
import itertools
import math
import typing

import jax
import jax.numpy as jnp
from jax import lax
from jax.experimental import pallas as pl
from jax.experimental.pallas import tpu as pltpu
from jax.sharding import Mesh
from jax.sharding import PartitionSpec as P

f32 = jnp.float32
bf16 = jnp.bfloat16
NAMES = ("dp_0", "dp_1", "dp_2", "mp_0", "mp_1")
SIZES = {"l": 2, "z": 4, "x": 4, "h": 2, "c": 2}
RING = 4
MESH_ID = pl.DeviceIdType.MESH
ANY = pl.BlockSpec(memory_space=pl.ANY)
INVMEM = pl.BlockSpec(memory_space=pltpu.VMEM)


class Along(typing.NamedTuple):
    low: typing.Any
    high: typing.Any


def here():
    low, z, x, high, core = (lax.axis_index(n) for n in NAMES)
    me = {"c": {0: core, 1: 1 - core}}
    for axis, at in (("x", x), ("y", high * 2 + low), ("z", z)):
        me[axis] = {}
        for step in (0, 1, 2, -1):
            pos = lax.rem(at + step + RING, RING) if step else at
            if axis == "y":
                pos = Along(lax.rem(pos, 2), lax.div(pos, 2)) if step else Along(low, high)
            me[axis][step] = pos
    return me


def device_of(axis, at):
    if axis == "y":
        return {"dp_0": at.low, "mp_0": at.high}
    return {{"x": "dp_2", "z": "dp_1", "c": "mp_1"}[axis]: at}


def extents(dims, at):
    found = []
    for d in dims:
        if d in at:
            v = at[d]
        elif d in "lh" and "y" in at:
            v = at["y"].low if d == "l" else at["y"].high
        else:
            v = (0, SIZES[d])
        found.append(v if isinstance(v, tuple) else (v, None))
    return found


def spot(dims, at):
    return tuple(start if size is None else pl.ds(start, size) for start, size in extents(dims, at))


def free_sizes(dims, at):
    return tuple(size for _, size in extents(dims, at) if size is not None)


def half(axis, side):
    return {"h": side} if axis == "y" else {axis: (2 * side, 2)}


def without(dims, axis):
    return tuple(d for d in dims if d not in ("lh" if axis == "y" else axis))


def lead(dims):
    return tuple(SIZES[d] for d in dims)


def announce(me, wide=False):
    barrier = pltpu.get_barrier_semaphore()
    peers = [{a: k} for a in "xyz" for k in range(1, RING)] + [{"c": 1}]
    if wide:
        peers += [{"x": k, "c": 1} for k in range(1, RING)]
        peers += [{"y": j, "z": k} for j in range(1, RING) for k in range(1, RING)]
    for moves in peers:
        pl.semaphore_signal(barrier, inc=1, device_id=moved(me, moves), device_id_type=MESH_ID)
    return len(peers)


def moved(me, moves):
    found = {}
    for axis, k in moves.items():
        found.update(device_of(axis, me[axis][-1 if k == 3 else k]))
    return found


def meet(count):
    pl.semaphore_wait(pltpu.get_barrier_semaphore(), count)


def remote(src, dst, send, recv, axis, at):
    copy = pltpu.make_async_remote_copy(
        src_ref=src, dst_ref=dst, send_sem=send, recv_sem=recv, device_id=device_of(axis, at), device_id_type=MESH_ID
    )
    copy.start()
    return copy


class Gather:
    def __init__(self, me, dims, order, shard, out, send, recv, fsend, frecv, local):
        self.me, self.dims, self.order, self.shard, self.out = me, dims, order, shard, out
        self.send, self.recv, self.fsend, self.frecv, self.local = send, recv, fsend, frecv, local
        self.forwards = []

    def region(self, phase, step=0, part=None):
        at = {a: self.me[a][0] for a in self.order[phase:]}
        at[self.order[phase]] = self.me[self.order[phase]][step]
        if "c" in self.dims:
            at["c"] = self.me["c"][0]
        if part is not None:
            at.update(half(self.order[0], part))
        return self.out.at[spot(self.dims, at)]

    def push(self, phase, slot, where, step):
        axis = self.order[phase]
        src = self.shard if phase == 0 else where
        return remote(src, where, self.send.at[phase, slot], self.recv.at[phase, slot], axis, self.me[axis][step])

    def forward(self, number, where):
        if "c" in self.dims:
            self.forwards.append(
                remote(where, where, self.fsend.at[number], self.frecv.at[number], "c", self.me["c"][1])
            )

    def begin(self):
        self.kept = pltpu.make_async_copy(self.shard, self.region(0), self.local)
        self.kept.start()
        self.launch(0)

    def launch(self, phase):
        where = self.region(phase)
        self.going = [self.push(phase, 0, where, 1), self.push(phase, 1, where, -1)]
        if phase == 0:
            self.going.append(self.push(0, 2, where, 2))

    def relay(self, phase):
        for slot, step in ((0, 1), (1, -1)):
            self.going[slot].wait()
            if phase > 0:
                self.going.append(self.push(phase, 2 + slot, self.region(phase, -step, slot), step))
                self.forward(3 * phase - 2 + slot, self.region(phase, -step))

    def finish(self, phase, launch=True):
        for copy in self.going[2:]:
            copy.wait()
        if phase == 0:
            self.kept.wait()
            if "c" in self.dims:
                at = {a: self.me[a][0] for a in (*self.order[1:], "c")}
                self.forward(0, self.out.at[spot(self.dims, at)])
        else:
            self.forward(3 * phase, self.region(phase, 2))
        if phase < 2 and launch:
            self.launch(phase + 1)

    def end(self):
        for copy in self.forwards:
            copy.wait()


def add_into(full, dims, at, others):
    found = extents(dims, at)
    for place in itertools.product(*(range(size) for _, size in found if size is not None)):
        index, along = [], iter(place)
        for start, size in found:
            index.append(start if size is None else start + next(along))
        index = tuple(index)
        total = full[index].astype(f32)
        for o in others:
            total = total + o[place].astype(f32)
        full[index] = total.astype(full.dtype)


def folded(v):
    total = None
    for r in range(0, v.shape[0], 8):
        for c in range(0, v.shape[1], 128):
            part = v[r : r + 8, c : c + 128]
            total = part if total is None else total + part
    return total


class Scatter:
    def __init__(self, me, dims, order, part, full, boxes, send, recv, local):
        self.me, self.dims, self.order, self.part, self.full, self.boxes = me, dims, order, part, full, boxes
        self.send, self.recv, self.local = send, recv, local

    def at(self, phase, step, side=None):
        at = {a: self.me[a][0] for a in self.order[:phase]}
        axis = self.order[phase]
        at[axis] = self.me[axis][step]
        if side is not None:
            at.update(half(self.order[phase + 1], side))
        return at

    def push(self, phase, slot, src, step):
        axis = self.order[phase]
        return remote(
            src, self.boxes[phase][slot], self.send.at[phase, slot], self.recv.at[phase, slot], axis, self.me[axis][step]
        )

    def begin(self):
        self.kept = pltpu.make_async_copy(self.part, self.full, self.local)
        self.kept.start()
        self.launch(0)

    def launch(self, phase):
        src = self.part if phase == 0 else self.full
        if phase < 2:
            self.going = [
                self.push(phase, side, src.at[spot(self.dims, self.at(phase, 2, side))], 1 - 2 * side) for side in range(2)
            ]
        else:
            self.going = [
                self.push(phase, slot, src.at[spot(self.dims, self.at(phase, step))], step)
                for slot, step in ((0, 2), (2, 1), (3, -1))
            ]

    def relay(self, phase):
        if phase == 0:
            self.kept.wait()
        if phase == 2:
            return
        for side, step in ((0, 1), (1, -1)):
            self.going[side].wait()
            add_into(self.full, self.dims, self.at(phase, step, side), [self.boxes[phase][side]])
            self.going.append(self.push(phase, 2 + side, self.full.at[spot(self.dims, self.at(phase, step))], step))

    def finish(self, phase):
        if phase < 2:
            for copy in self.going[2:]:
                copy.wait()
            add_into(self.full, self.dims, self.at(phase, 0), self.boxes[phase][2:4])
            self.launch(phase + 1)
            return None
        for copy in self.going:
            copy.wait()
        total = self.full[spot(self.dims, self.at(2, 0))].astype(f32)
        for slot in (0, 2, 3):
            total = total + self.boxes[2][slot][...].astype(f32)
        return total

    @staticmethod
    def scratch(dims, order, slab, dtype):
        shapes = [(*lead(dims), *slab)]
        rest = dims
        for phase, axis in enumerate(order):
            rest = without(rest, axis)
            if phase < 2:
                small = free_sizes(rest, half(order[phase + 1], 0))
            else:
                small = ()
            shapes += [(*small, *slab)] * 2 + [(*lead(rest), *slab)] * 2
        return [pltpu.VMEM(s, dtype) for s in shapes]


OWNED = ("x", "l", "z", "h")
GATHER = (
    (OWNED, ("z", "y", "x")),
    (OWNED, ("x", "z", "y")),
    (OWNED, ("z", "y", "x")),
    (("c", "l", "z", "x", "h"), ("x", "z", "y")),
    (("h", "c", "l", "z", "x"), ("y", "x", "z")),
    (("h", "c", "l", "z", "x"), ("z", "y", "x")),
)
SCATTER = (
    (OWNED, ("z", "y", "x")),
    (OWNED, ("y", "z", "x")),
    (OWNED, ("z", "y", "x")),
    (("l", "z", "x", "h"), ("y", "x", "z")),
    (("h", "l", "z", "x"), ("x", "z", "y")),
    (("h", "l", "z", "x"), ("z", "x", "y")),
)
SLABS = ((24, 512), (24, 512), (16, 128), (16, 512), (16, 1280), (16, 1024))


D, EXP, MAP, PIX = 512, 3072, 9, 81
PAIR = 24
WIDTH = 384
OWNERS = WIDTH // 24
CHUNK = 3
SPAN = CHUNK * MAP * PAIR
EXPAND = 8.0 / math.sqrt(D)
PROJECT = 8.0 / math.sqrt(EXP)
VMEM_BYTES = 60 * 2**20


def sigmoid(v):
    return 0.5 + 0.5 * jnp.tanh(0.5 * v)


def nt(left, right):
    return lax.dot_general(left, right, (((1,), (1,)), ((), ())), preferred_element_type=f32)


def nn(left, right):
    return lax.dot_general(left, right, (((1,), (0,)), ((), ())), preferred_element_type=f32)


def tn(left, right):
    return lax.dot_general(left, right, (((0,), (0,)), ((), ())), preferred_element_type=f32)


def clear_borders(padded):
    zero = jnp.zeros((MAP, PAIR, WIDTH), f32)
    padded[0] = zero
    padded[MAP + 1] = zero


def each_block(body):
    def one(row, _):
        for lane in range(WIDTH // 128):
            for group in range(PAIR // 8):
                body(row, slice(8 * group, 8 * group + 8), slice(128 * lane, 128 * lane + 128))
        return 0

    lax.fori_loop(0, MAP, one, 0)


INSTR, DIMS, BINS, NTOK, FRAMES, HEADS, HD = 744, 11, 256, 8, 6, 8, 64
TABLE = INSTR + 2
ROWS = PAIR * NTOK
PADDED = 2048
SMALL_AT = TABLE - D
LN_EPS = 1e-06
OUT_MULT = 2.0
HIGH = lax.Precision.HIGHEST
FILM = 16.0 / math.sqrt(D)
LEARN = 4.0 / math.sqrt(D)


def norm_fwd(x, gain):
    centre = x - jnp.mean(x, -1, keepdims=True)
    inverse = lax.rsqrt(jnp.mean(centre * centre, -1, keepdims=True) + LN_EPS)
    normed = centre * inverse
    return normed * (1.0 + gain), normed, inverse


def norm_back(normed, inverse, gain, grad_out):
    dnormed = grad_out * (1.0 + gain)
    grad_in = inverse * (
        dnormed
        - jnp.mean(dnormed, -1, keepdims=True)
        - normed * jnp.mean(dnormed * normed, -1, keepdims=True)
    )
    return grad_in, jnp.sum(grad_out * normed, 0, keepdims=True)


def gelu_parts(u):
    c = math.sqrt(2.0 / math.pi)
    square = u * u
    t = jnp.tanh(c * u * (1.0 + 0.044715 * square))
    half = 0.5 * (1.0 + t)
    return u * half, half + 0.5 * u * (1.0 - t * t) * c * (1.0 + 3.0 * 0.044715 * square)


def iota(shape, axis):
    return lax.broadcasted_iota(jnp.int32, shape, axis)


def shifted(v, places):
    tiles = [pltpu.roll(v[:, i : i + 128], (128 - places) % 128, 1) for i in range(0, v.shape[1], 128)]
    return jnp.concatenate(tiles, axis=1)


def only(v, first):
    place = iota(v.shape, 1) & 15
    return jnp.where((place >= first) & (place < first + 4), v, 0.0)


def place_of_feature(start, rows):
    d = iota((rows, D), 1)
    owner = d >> 2
    row = (owner & 1) * 1024 + (owner >> 1) * 16 + 12 + (d & 3)
    return (iota((rows, D), 0) + start == row).astype(bf16)


def over_cells(body, carry):
    many = 16 * PAIR
    carry = lax.fori_loop(
        0, PIX // 16, lambda i, c: body(pl.ds(pl.multiple_of(i * many, many), many), many, c), carry
    )
    return body(slice(PIX // 16 * many, PIX * PAIR), PAIR, carry)


def middle_kernel(
    instr_in, mask_in, part_in, cells_in, misc, one_in, two_in, cam, bins_in,
    dcells, dmisc, one_out, two_out, stats,
    one, two, done_one, done_two, y_hi, y_lo, logit, att, qkv, prob, ctx, up, hid, acc, dlog, lowgrad, turn, part, cells, sems,
):
    core, high = lax.axis_index("mp_1"), lax.axis_index("mp_0")
    fetch_part = pltpu.make_async_copy(part_in, part, sems.at[2])
    fetch_cells = pltpu.make_async_copy(cells_in, cells, sems.at[3])
    fetch_part.start()
    fetch_cells.start()
    fetch_one = pltpu.make_async_copy(one_in, one, sems.at[0])
    fetch_two = pltpu.make_async_copy(two_in, two, sems.at[1])
    fetch_one.start()
    fetch_two.start()
    lanes, images = iota((PAIR, 128), 1), iota((PAIR, 128), 0)
    instr = jnp.zeros((PAIR, 128), jnp.int32)
    for i in range(PAIR // FRAMES):
        instr = jnp.where(lax.div(images, FRAMES) == i, instr_in[high * (PAIR // FRAMES) + i], instr)
    mask = jnp.zeros((PAIR, 128), jnp.int32)
    for i in range(PAIR):
        mask = jnp.where(images == i, mask_in[high * PAIR + i], mask)
    turn[...] = jnp.zeros_like(turn)
    turn[0:DIMS, 0 : 2 * PAIR] = bins_in[...].astype(f32)
    turn[...] = turn[...].T
    bins = turn[pl.ds(pl.multiple_of(high * PAIR, PAIR), PAIR), :].astype(jnp.int32)

    def chosen(tile):
        at = lanes + 128 * tile
        return ((at == instr) | (at == INSTR + cam[0] + cam[1])).astype(f32)

    choose_lo = jnp.concatenate([chosen(i) for i in range(4)], axis=1).astype(bf16)
    choose_hi = jnp.concatenate([chosen(i) for i in range(4, 8)], axis=1).astype(bf16)
    flat = misc[...]
    cvec = only(shifted(nt(choose_lo, flat), 8) + shifted(nt(choose_hi, flat), 12), 0).astype(bf16).astype(f32)
    cvec_4 = shifted(cvec, 124)
    cvec_low, cvec_4_low = cvec.astype(bf16), cvec_4.astype(bf16)
    gamma = nn(cvec_low, flat) * FILM
    beta = nn(cvec_4_low, flat) * FILM
    scale = 1.0 + gamma
    pick = (iota((16, D), 1) == SMALL_AT + iota((16, D), 0)).astype(bf16)
    small = nn(nt(pick, flat).astype(bf16), place_of_feature(0, 2048))
    gains = [small[i : i + 1] for i in range(3)]
    learner = jnp.concatenate([small[3:11], jnp.zeros((120, D), f32)], axis=0).astype(bf16)

    fetch_part.wait()
    fetch_cells.wait()

    def feature(rows, size, _):
        v = part[rows, :].reshape(size // PAIR, PAIR, D) * scale + beta
        v = v.reshape(size, D) + cells[rows, :].astype(f32)
        hi = v.astype(bf16)
        y_hi[rows, :] = hi
        y_lo[rows, :] = (v - hi.astype(f32)).astype(bf16)
        return 0

    over_cells(feature, 0)
    tail = slice(PIX * PAIR, PADDED)
    for ref in (y_hi, y_lo, att, logit):
        ref[tail, :] = jnp.zeros((PADDED - PIX * PAIR, ref.shape[1]), ref.dtype)
    used = slice(0, PIX * PAIR)
    logit[used, :] = (nt(y_hi[used, :], learner) + nt(y_lo[used, :], learner)) * LEARN

    def softmax_over_cells(v):
        v = v.reshape(PIX, PAIR, 128)
        e = jnp.exp(v - jnp.max(v, 0, keepdims=True))
        return e / jnp.sum(e, 0, keepdims=True)

    att[used, :] = softmax_over_cells(logit[used, :]).reshape(PIX * PAIR, 128)
    acc[...] = jnp.zeros_like(acc)

    def gather(i, _):
        rows = pl.ds(pl.multiple_of(i * 512, 512), 512)
        turned = jnp.concatenate(
            [att[pl.ds(pl.multiple_of(i * 512 + 128 * k, 128), 128), :].T[0:NTOK] for k in range(4)], axis=1
        )
        hi = turned.astype(bf16).astype(f32)
        lo = turned - hi
        image = lax.rem(i * 512 + iota((8, 512), 1), PAIR)
        own = [image == 8 * g + iota((8, 512), 0) for g in range(3)]

        def wide(v):
            pieces = [jnp.where(m, v[t : t + 1], 0.0) for t in range(NTOK) for m in own]
            return jnp.concatenate(pieces, axis=0).astype(bf16)

        wide_hi = wide(hi)
        upper = y_hi[rows, :]
        acc[...] += nn(wide_hi, upper) + nn(wide(lo), upper) + nn(wide_hi, y_lo[rows, :])
        return 0

    lax.fori_loop(0, PADDED // 512, gather, 0)
    tok = acc[...].astype(bf16).astype(f32)
    fetch_one.wait()
    fetch_two.wait()

    h1, normed1, inverse1 = norm_fwd(tok, gains[0])
    h1_low = h1.astype(bf16)
    row_q, row_k = iota((ROWS, ROWS), 0), iota((ROWS, ROWS), 1)
    image_q, image_k = lax.rem(row_q, PAIR), lax.rem(row_k, PAIR)
    order_q = image_q * NTOK + lax.div(row_q, PAIR)
    order_k = image_k * NTOK + lax.div(row_k, PAIR)
    seen = (lax.div(image_q, FRAMES) == lax.div(image_k, FRAMES)) & (order_k <= order_q)
    root = HD**-0.5
    acc[...] = jnp.zeros_like(acc)

    def attend(m, _):
        p = nn(h1_low, one[m, :, 0:384]).astype(bf16)
        qkv[m] = p
        outs = []
        for head in range(2):
            q, k, v = (p[:, 128 * j + 64 * head : 128 * j + 64 * head + 64] for j in range(3))
            s = jnp.where(seen, nt(q, k) * root, -1e30)
            e = jnp.exp(s - jnp.max(s, -1, keepdims=True))
            w = e / jnp.sum(e, -1, keepdims=True)
            prob[m, head] = w
            outs.append(nn(w.astype(bf16), v))
        o = jnp.concatenate(outs, axis=1).astype(bf16)
        ctx[m] = o
        acc[...] += nt(o, one[m, :, 384:512])
        return 0

    lax.fori_loop(0, 4, attend, 0)
    x1 = tok + OUT_MULT * acc[...]
    h2, normed2, inverse2 = norm_fwd(x1, gains[1])
    h2_low = h2.astype(bf16)
    acc[...] = x1

    def feed(m, _):
        u = nn(h2_low, two[m, :, 0:512])
        up[m] = u
        low = gelu_parts(u)[0].astype(bf16)
        hid[m] = low
        acc[...] += nt(low, two[m, :, 512:1024])
        return 0

    lax.fori_loop(0, 4, feed, 0)
    x2 = acc[...]
    normed_out, normed3, inverse3 = norm_fwd(x2, gains[2])
    pooled = (jnp.sum(normed_out.reshape(NTOK, PAIR, D), axis=0) * (1.0 / NTOK)).astype(bf16)

    low_half = lanes < 64
    scores = [nn(pooled, one[m, :, 512:1280]) for m in range(4)]
    weight = mask.astype(f32)
    loss = jnp.zeros((PAIR, 128), f32)
    for u in range(6):
        tiles = [s[:, 128 * u : 128 * u + 128] for s in scores]
        top = jnp.maximum(jnp.maximum(tiles[0], tiles[1]), jnp.maximum(tiles[2], tiles[3]))
        left = jnp.max(jnp.where(low_half, top, -jnp.inf), -1, keepdims=True)
        right = jnp.max(jnp.where(low_half, -jnp.inf, top), -1, keepdims=True)
        top = jnp.where(low_half, left, right)
        total = sum(jnp.exp(t - top) for t in tiles)
        left = jnp.sum(jnp.where(low_half, total, 0.0), -1, keepdims=True)
        right = jnp.sum(jnp.where(low_half, 0.0, total), -1, keepdims=True)
        lse = top + jnp.log(jnp.where(low_half, left, right))
        label = jnp.where(low_half, bins[:, 2 * u : 2 * u + 1], bins[:, 2 * u + 1 : 2 * u + 2])
        real = low_half | (2 * u + 1 < DIMS)
        target = jnp.zeros((PAIR, 128), f32)
        for m, t in enumerate(tiles):
            hit = label == (lanes & 63) + 64 * m
            target = target + jnp.where(hit, t, 0.0)
            slope = weight * (jnp.exp(t - lse) - hit.astype(f32))
            dlog[m, :, 128 * u : 128 * u + 128] = jnp.where(real, slope, 0.0).astype(bf16)
        counted = real & ((lanes & 63) == 0)
        loss = loss + weight * (jnp.where(counted, lse, 0.0) - target)
    stats[...] = jnp.zeros_like(stats)
    stats[0:8] = loss[0:8] + loss[8:16] + loss[16:24]
    counts = jnp.where(lanes == 0, weight, 0.0)
    stats[8:16] = counts[0:8] + counts[8:16] + counts[16:24]
    dpooled = jnp.zeros((PAIR, D), f32)
    for m in range(4):
        dpooled = dpooled + nt(dlog[m], one[m, :, 512:1280])
    dnormed = jnp.broadcast_to(dpooled * (1.0 / NTOK), (NTOK, PAIR, D)).reshape(ROWS, D)
    dx2, dgain2 = norm_back(normed3, inverse3, gains[2], dnormed)
    dbranch = dx2.astype(bf16)
    acc[...] = jnp.zeros_like(acc)

    def feed_back(m, _):
        slope = gelu_parts(up[m])[1]
        dup = (nn(dbranch, two[m, :, 512:1024]) * slope).astype(bf16)
        lowgrad[m] = dup
        acc[...] += nt(dup, two[m, :, 0:512])
        return 0

    lax.fori_loop(0, 4, feed_back, 0)
    dx1_norm, dgain1 = norm_back(normed2, inverse2, gains[1], acc[...])
    dx1 = dx2 + dx1_norm
    dattn = dx1.astype(bf16)

    def feed_weights(h, _):
        m = 2 * h + core
        done_one[h, :, 512:1280] = tn(pooled, dlog[m]).astype(bf16)
        done_two[h, :, 0:512] = tn(h2_low, lowgrad[m]).astype(bf16)
        done_two[h, :, 512:1024] = tn(dbranch, hid[m]).astype(bf16)
        done_one[h, :, 384:512] = (tn(dattn, ctx[m]) * OUT_MULT).astype(bf16)
        return 0

    lax.fori_loop(0, 2, feed_weights, 0)
    acc[...] = jnp.zeros_like(acc)

    def attend_back(m, _):
        do = (nn(dattn, one[m, :, 384:512]) * OUT_MULT).astype(bf16)
        p = qkv[m]
        dq, dk, dv = [], [], []
        for head in range(2):
            q, k, v = (p[:, 128 * j + 64 * head : 128 * j + 64 * head + 64] for j in range(3))
            w = prob[m, head]
            d = do[:, 64 * head : 64 * head + 64]
            dp = nt(d, v)
            dv.append(tn(w.astype(bf16), d))
            ds = (w * (dp - jnp.sum(w * dp, -1, keepdims=True))).astype(bf16)
            dq.append(nn(ds, k) * root)
            dk.append(tn(ds, q) * root)
        g = jnp.concatenate([*dq, *dk, *dv], axis=1).astype(bf16)
        lowgrad[m, :, 0:384] = g
        acc[...] += nt(g, one[m, :, 0:384])
        return 0

    lax.fori_loop(0, 4, attend_back, 0)

    def attend_weights(h, _):
        done_one[h, :, 0:384] = tn(h1_low, lowgrad[2 * h + core, :, 0:384]).astype(bf16)
        return 0

    lax.fori_loop(0, 2, attend_weights, 0)
    dtok_norm, dgain0 = norm_back(normed1, inverse1, gains[0], acc[...])
    acc[...] = dx1 + dtok_norm

    send_one = pltpu.make_async_copy(done_one, one_out, sems.at[0])
    send_two = pltpu.make_async_copy(done_two, two_out, sems.at[1])
    send_one.start()
    send_two.start()
    dtok_hi = acc[...].astype(bf16)
    dtok_lo = (acc[...] - dtok_hi.astype(f32)).astype(bf16)
    same = lax.rem(iota((PAIR, ROWS), 1), PAIR) == iota((PAIR, ROWS), 0)
    token_of = (lax.div(iota((128, ROWS), 1), PAIR) == iota((128, ROWS), 0)).astype(bf16)

    def own_image(v):
        return jnp.where(same, v.reshape(-1, PAIR, ROWS), 0.0).reshape(-1, ROWS)

    def halves(v):
        hi = v.astype(bf16)
        return hi, (v - hi.astype(f32)).astype(bf16)

    def slope_of(rows, size, _):
        upper = y_hi[rows, :]
        g = own_image(nt(upper, dtok_hi) + nt(upper, dtok_lo) + nt(y_lo[rows, :], dtok_hi))
        hi, lo = halves(g)
        logit[rows, :] = nt(hi, token_of) + nt(lo, token_of)
        return 0

    over_cells(slope_of, 0)
    a = att[used, :].reshape(PIX, PAIR, 128)
    da = logit[used, :].reshape(PIX, PAIR, 128)
    logit[used, :] = (a * (da - jnp.sum(a * da, 0, keepdims=True)) * LEARN).reshape(PIX * PAIR, 128)
    turned = jnp.concatenate([logit[128 * k : 128 * k + 128, :].T[0:NTOK] for k in range(PADDED // 128)], axis=1)
    upper = turned.astype(bf16).astype(f32)
    both = jnp.concatenate([upper, turned - upper], axis=0).astype(bf16)
    sums = nn(both, y_hi[...])
    dlearner = sums[0:8] + sums[8:16] + nn(both, y_lo[...])[0:8]

    def spread(rows, size, sums):
        hi, lo = halves(att[rows, :])
        hi, lo = own_image(nn(hi, token_of)).astype(bf16), own_image(nn(lo, token_of)).astype(bf16)
        slope_hi, slope_lo = halves(logit[rows, :])
        dy = nn(hi, dtok_hi) + nn(lo, dtok_hi) + nn(hi, dtok_lo) + nn(slope_hi, learner) + nn(slope_lo, learner)
        dy = dy.reshape(size // PAIR, PAIR, D)
        dcells[rows, :] = (dy * scale).astype(bf16).reshape(size, D)
        p = part[rows, :].reshape(size // PAIR, PAIR, D)
        return sums[0] + jnp.sum(dy * p, 0), sums[1] + jnp.sum(dy, 0)

    zero = jnp.zeros((PAIR, D), f32)
    dgamma, dbeta = over_cells(spread, (zero, zero))
    dgamma, dbeta = dgamma.astype(bf16), dbeta.astype(bf16)
    dcvec = only(nt(dgamma, flat) + shifted(nt(dbeta, flat), 4), 0) * FILM
    high = dcvec.astype(bf16).astype(f32)
    rest = dcvec - high
    dsmall = jnp.concatenate([dgain0, dgain1, dgain2, dlearner, jnp.zeros((5, D), f32)], axis=0).astype(bf16)
    mine = pl.ds(pl.multiple_of(core * 1024, 1024), 1024)
    lhs = jnp.concatenate(
        [cvec, cvec_4, shifted(high, 120), shifted(rest, 120), shifted(high, 116), shifted(rest, 116)], axis=0
    )
    lhs = jnp.where(core == 0, lhs[:, 0:1024], lhs[:, 1024:2048])
    lhs = jnp.concatenate([lhs, nt(dsmall, place_of_feature(core * 1024, 1024))], axis=0).astype(bf16)
    rhs = jnp.concatenate([dgamma, dbeta, choose_lo, choose_lo, choose_hi, choose_hi, pick], axis=0)
    result = tn(lhs, rhs)
    film_rows = (iota((1024, D), 0) & 15) < 8
    dmisc[...] = jnp.where(film_rows, result * FILM, result).astype(bf16)
    send_one.wait()
    send_two.wait()


def middle(instr, mask, part, cells, misc, one, two, cam, bins):
    vmem = pl.BlockSpec(memory_space=pltpu.VMEM)
    return pl.pallas_call(
        middle_kernel,
        out_shape=[
            jax.ShapeDtypeStruct((PIX * PAIR, D), bf16),
            jax.ShapeDtypeStruct((1024, D), bf16),
            jax.ShapeDtypeStruct((2, D, 1280), bf16),
            jax.ShapeDtypeStruct((2, D, 1024), bf16),
            jax.ShapeDtypeStruct((16, 128), f32),
        ],
        in_specs=[pl.BlockSpec(memory_space=pltpu.SMEM)] * 2 + [ANY] * 2 + [vmem] + [ANY] * 2 + [vmem] * 2,
        out_specs=[vmem, vmem, ANY, ANY, vmem],
        scratch_shapes=[
            pltpu.VMEM((4, D, 1280), bf16),
            pltpu.VMEM((4, D, 1024), bf16),
            pltpu.VMEM((2, D, 1280), bf16),
            pltpu.VMEM((2, D, 1024), bf16),
            pltpu.VMEM((PADDED, D), bf16),
            pltpu.VMEM((PADDED, D), bf16),
            pltpu.VMEM((PADDED, 128), f32),
            pltpu.VMEM((PADDED, 128), f32),
            pltpu.VMEM((4, ROWS, 384), bf16),
            pltpu.VMEM((4, 2, ROWS, ROWS), f32),
            pltpu.VMEM((4, ROWS, 128), bf16),
            pltpu.VMEM((4, ROWS, 512), f32),
            pltpu.VMEM((4, ROWS, 512), bf16),
            pltpu.VMEM((ROWS, D), f32),
            pltpu.VMEM((4, PAIR, 768), bf16),
            pltpu.VMEM((4, ROWS, 512), bf16),
            pltpu.VMEM((128, 128), f32),
            pltpu.VMEM((PIX * PAIR, D), f32),
            pltpu.VMEM((PIX * PAIR, D), bf16),
            pltpu.SemaphoreType.DMA((4,)),
        ],
        compiler_params=pltpu.CompilerParams(vmem_limit_bytes=VMEM_BYTES),
    )(instr, mask, part, cells, misc, one, two, cam, bins)


STEPS = 4
BLOCK = (PIX, PAIR, WIDTH)


def tap_places():
    row, col = iota((OWNERS * 128, WIDTH), 0), iota((OWNERS * 128, WIDTH), 1)
    return (((row >> 7) * 24 + (row & 127) == col) & ((row & 127) < 24)).astype(bf16)


def to_cells(frames, cells):
    rows = 8 * PAIR
    at, of = iota((rows, rows), 0), iota((rows, rows), 1)
    turn = (lax.rem(at, PAIR) * 8 + lax.div(at, PAIR) == of).astype(bf16)
    for first in (*range(0, PIX - 8, 8), PIX - 8):
        block = frames[:, :, first : first + 8, :].reshape(rows, D)
        cells[first * PAIR : first * PAIR + rows, :] = nn(turn, block).astype(bf16)


def fill_shards(conv, cond, small, attn, mlp, head, camera, core, shards, staged, tap_tile, cam):
    shards[0][...] = conv[:, 0:D].astype(bf16)
    shards[1][...] = conv[:, D : 2 * D].astype(bf16)
    tap_tile[...] = jnp.zeros_like(tap_tile)
    tap_tile[0:24, 0:9] = conv[:, 2 * D :]
    shards[2][...] = tap_tile[...].T[0:16].astype(bf16)
    staged[...] = jnp.zeros_like(staged)
    for i in range(3):
        staged[4 * i : 4 * i + 4, :] = cond[:, D * i : D * i + D]
    staged[12:16, 0:SMALL_AT] = cond[:, 3 * D :]
    staged[12:16, SMALL_AT : SMALL_AT + 11] = small[...]
    shards[3][...] = staged[...].astype(bf16)
    for j in range(4):
        shards[4][:, 128 * j : 128 * j + 128] = attn[j].astype(bf16)
    for k in range(0, DIMS - 1, 2):
        both = jnp.concatenate([head[k], head[k + 1]], axis=1)
        shards[4][:, 512 + 64 * k : 640 + 64 * k] = both.astype(bf16)
    last = jnp.concatenate([head[DIMS - 1], jnp.zeros((16, 64), f32)], axis=1)
    shards[4][:, 1152:1280] = last.astype(bf16)
    for j in range(2):
        shards[5][:, 512 * j : 512 * j + 512] = mlp[j].astype(bf16)
    row = iota((PAIR, 128), 0)
    found = jnp.zeros((PAIR, 128), jnp.int32)
    for i in range(PAIR // 2):
        found = jnp.where(row == core * (PAIR // 2) + i, camera[i], found)
    cam[...] = found


def forward_kernel(plan, *refs):
    n = len(plan)
    frames, camera = refs[0:2]
    masters = refs[2 : 2 + n]
    refs = refs[2 + n :]
    cam2, cells_out, project_out, taps_out, misc_out, one_out, two_out, pre_out, deep_out, total_out = refs[:10]
    frames2, cells, expand, project, slabs, taps, places, act, pre, deep, part, part_low, other_low = refs[10:23]
    shards, staged, tap_tile, cam = refs[23 : 23 + n], refs[23 + n], refs[24 + n], refs[25 + n]
    send, recv, fsend, frecv, local, kept, swap_send, swap_recv = refs[26 + n :]
    me = here()
    count = announce(me)
    fill_shards(*masters, camera, me["c"][0], shards, staged, tap_tile, cam)
    meet(count)
    swaps = []
    for i, (src, out) in enumerate(((frames, frames2), (cam, cam2))):
        where = out.at[me["c"][0]]
        mine = pltpu.make_async_copy(src, where, local.at[n + i])
        mine.start()
        swaps += [mine, remote(src, where, swap_send.at[i], swap_recv.at[i], "c", me["c"][1])]
    outs = (expand, project, slabs, misc_out, one_out, two_out)
    jobs = [
        Gather(me, dims, order, shards[b], outs[b], send.at[b], recv.at[b], fsend.at[b], frecv.at[b], local.at[b])
        for b, (dims, order) in enumerate(plan)
    ]
    early, late, middle_one, outer = (jobs[0], jobs[2]), (jobs[1],), (jobs[4],), (jobs[3], jobs[5])
    first, rest = jobs[:3], jobs[3:]

    def relay(some, phase):
        for job in some:
            job.relay(phase)

    def finish(some, phase, launch=True):
        for job in some:
            job.finish(phase, launch)

    for job in jobs:
        job.begin()
    relay(first, 0)
    finish(first, 0)
    clear_borders(act)
    places[...] = tap_places()
    relay(rest, 0)
    finish(rest, 0)
    relay(first, 1)
    relay(rest, 1)
    finish(first, 1)
    finish(middle_one, 1)
    finish(outer, 1, False)
    part[...] = jnp.zeros_like(part)
    swaps[0].wait()
    swaps[1].wait()
    to_cells(frames2, cells)
    saves = []

    def save(src, dst, number):
        copy = pltpu.make_async_copy(src, dst, kept.at[number])
        copy.start()
        saves.append(copy)

    save(cells, cells_out, 0)
    spans, leaves = [None] * STEPS, []
    for step in range(STEPS):
        slot = step % 2
        at = me["x"][(0, -1, 1, 2)[step]]
        if step == 1:
            relay(early, 2)
            relay(late, 2)
            for job in outer:
                job.launch(2)
        if step == 2:
            relay(middle_one, 2)
        if step == 3:
            finish(early, 2)
            relay(outer, 2)
        if step >= 2:
            for copy in spans[step - 2]:
                copy.wait()
        weight = expand[at].reshape(WIDTH, D)
        tap = slabs[at].reshape(OWNERS, 16, 128)
        side = jnp.concatenate([tap[i] for i in range(OWNERS)], axis=1)
        taps[at] = nn(side, places[...]) * (8.0 / 3.0)

        def enter(i, _, weight=weight, slot=slot):
            rows = pl.ds(pl.multiple_of(i * SPAN, SPAN), SPAN)
            e = (nt(cells[rows, :], weight) * EXPAND).reshape(CHUNK * MAP, PAIR, WIDTH)
            pre[slot, pl.ds(i * CHUNK * MAP, CHUNK * MAP)] = e
            act[pl.ds(1 + i * CHUNK, CHUNK)] = (e * sigmoid(e)).reshape(CHUNK, MAP, PAIR, WIDTH)
            return 0

        lax.fori_loop(0, MAP // CHUNK, enter, 0)
        out = [pltpu.make_async_copy(pre.at[slot], pre_out.at[at], kept.at[3 + 2 * step])]
        out[0].start()

        def mix(row, subs, cols, slot=slot, at=at):
            near = act[pl.ds(row, 3), :, subs, cols]
            tap = [jnp.broadcast_to(taps[at, t : t + 1, cols], (8, 128)) for t in range(9)]
            for col in range(MAP):
                total = None
                for t in range(9):
                    p = col + t % 3 - 1
                    if 0 <= p < MAP:
                        term = near[t // 3, p] * tap[t]
                        total = term if total is None else total + term
                deep[slot, row * MAP + col, subs, cols] = total

        each_block(mix)
        out.append(pltpu.make_async_copy(deep.at[slot], deep_out.at[at], kept.at[4 + 2 * step]))
        out[1].start()
        spans[step] = out
        if step == 3:
            finish(middle_one, 2)

        def leave(i, _, at=at, slot=slot):
            back = project[at].reshape(WIDTH, D)
            rows = pl.ds(pl.multiple_of(i * SPAN, SPAN), SPAN)
            v = deep[slot, pl.ds(i * CHUNK * MAP, CHUNK * MAP)].reshape(SPAN, WIDTH)
            part[rows, :] += nn((v * sigmoid(v)).astype(bf16), back) * PROJECT
            return 0

        leaves.append(leave)
        if step == 1:
            finish(late, 2)
            save(project, project_out, 1)
            lax.fori_loop(0, MAP // CHUNK, leaves[0], 0)
        if 0 < step < STEPS - 1:
            lax.fori_loop(0, MAP // CHUNK, leave, 0)
    save(taps, taps_out, 2)
    trades = []
    for i in range(MAP // CHUNK):
        leave(i, 0)
        part_low[i] = part[i * SPAN : (i + 1) * SPAN, :].astype(bf16)
        trades.append(
            remote(part_low.at[i], other_low.at[i], swap_send.at[2 + i], swap_recv.at[2 + i], "c", me["c"][1])
        )
    finish(outer, 2)
    for i, copy in enumerate(trades):
        copy.wait()
        rows = slice(i * SPAN, (i + 1) * SPAN)
        part[rows, :] += other_low[i].astype(f32)
        save(part.at[rows], total_out.at[rows], 3 + 2 * STEPS + i)
    for step in (STEPS - 2, STEPS - 1):
        saves += spans[step]
    for job in jobs:
        job.end()
    for copy in saves + swaps[2:]:
        copy.wait()


def forward(frames, camera, masters, plan, collective_id):
    n = len(plan)
    maps = jax.ShapeDtypeStruct((STEPS, *BLOCK), f32)
    shape = jax.ShapeDtypeStruct
    full = [shape((*lead(dims), *slab), bf16) for slab, (dims, _) in zip(SLABS, plan)]
    rows = PIX * PAIR
    return pl.pallas_call(
        functools.partial(forward_kernel, plan),
        out_shape=[
            shape((2, PAIR, 128), jnp.int32),
            shape((rows, D), bf16),
            full[1],
            shape((STEPS, 16, WIDTH), f32),
            *full[3:],
            maps,
            maps,
            shape((rows, D), f32),
        ],
        in_specs=[ANY, pl.BlockSpec(memory_space=pltpu.SMEM)] + [INVMEM] * n,
        out_specs=[ANY] * 10,
        scratch_shapes=[
            pltpu.VMEM((2, *frames.shape), bf16),
            pltpu.VMEM((rows, D), bf16),
            pltpu.VMEM(full[0].shape, bf16),
            pltpu.VMEM(full[1].shape, bf16),
            pltpu.VMEM(full[2].shape, bf16),
            pltpu.VMEM((STEPS, 16, WIDTH), f32),
            pltpu.VMEM((OWNERS * 128, WIDTH), bf16),
            pltpu.VMEM((MAP + 2, MAP, PAIR, WIDTH), f32),
            pltpu.VMEM((2, *BLOCK), f32),
            pltpu.VMEM((2, *BLOCK), f32),
            pltpu.VMEM((rows, D), f32),
            pltpu.VMEM((MAP // CHUNK, SPAN, D), bf16),
            pltpu.VMEM((MAP // CHUNK, SPAN, D), bf16),
            *[pltpu.VMEM(slab, bf16) for slab in SLABS],
            pltpu.VMEM((16, D), f32),
            pltpu.VMEM((128, 128), f32),
            pltpu.VMEM((PAIR, 128), jnp.int32),
            pltpu.SemaphoreType.DMA((n, 3, 4)),
            pltpu.SemaphoreType.DMA((n, 3, 4)),
            pltpu.SemaphoreType.DMA((n, 7)),
            pltpu.SemaphoreType.DMA((n, 7)),
            pltpu.SemaphoreType.DMA((n + 2,)),
            pltpu.SemaphoreType.DMA((3 + 2 * STEPS + MAP // CHUNK,)),
            pltpu.SemaphoreType.DMA((2 + MAP // CHUNK,)),
            pltpu.SemaphoreType.DMA((2 + MAP // CHUNK,)),
        ],
        compiler_params=pltpu.CompilerParams(
            collective_id=collective_id, has_side_effects=True, vmem_limit_bytes=VMEM_BYTES
        ),
    )(frames, camera, *masters)


class Blocks:
    def __init__(self, me, dims, order, full, room, send, recv):
        self.me, self.dims, self.order, self.full = me, dims, order, full
        self.halves, self.wholes, self.slabs, self.last = room
        self.send, self.recv = send, recv
        self.going = [None] * STEPS
        self.sent = []

    def at(self, step, **more):
        return {"x": self.me["x"][BACK[step]], **more}

    def push(self, step, slot, src, box, axis, move):
        return remote(src, box, self.send.at[step, slot], self.recv.at[step, slot], axis, self.me[axis][move])

    def launch(self, step):
        a, b, _ = self.order
        self.going[step] = [
            self.push(
                step, side, self.full.at[spot(self.dims, self.at(step, **{a: self.me[a][2]}, **half(b, side)))],
                self.halves.at[step, side], a, 1 - 2 * side,
            )
            for side in range(2)
        ]

    def relay(self, step):
        a, b, _ = self.order
        for side, move in ((0, 1), (1, -1)):
            self.going[step][side].wait()
            pos = {a: self.me[a][move]}
            add_into(self.full, self.dims, self.at(step, **pos, **half(b, side)), [self.halves.at[step, side]])
            where = self.full.at[spot(self.dims, self.at(step, **pos))]
            self.going[step].append(self.push(step, 2 + side, where, self.wholes.at[step, side], a, move))

    def middle(self, step):
        a, b, _ = self.order
        for copy in self.going[step][2:]:
            copy.wait()
        own = {a: self.me[a][0]}
        add_into(self.full, self.dims, self.at(step, **own), [self.wholes.at[step, side] for side in range(2)])
        self.going[step] = [
            self.push(
                step, 4 + i, self.full.at[spot(self.dims, self.at(step, **own, **{b: self.me[b][move]}))],
                self.slabs.at[step, i], b, move,
            )
            for i, move in enumerate((2, 1, -1))
        ]

    def finish(self, step):
        a, b, _ = self.order
        for copy in self.going[step]:
            copy.wait()
        index = spot(self.dims, self.at(step, **{a: self.me[a][0], b: self.me[b][0]}))
        total = self.full[index].astype(f32)
        for i in range(3):
            total = total + self.slabs[step, i].astype(f32)
        if BACK[step] != 0:
            self.full[index] = total.astype(bf16)
            self.sent.append(self.push(step, 7, self.full.at[index], self.last.at[step], "x", BACK[step]))
        return total

    def close(self, total):
        for copy in self.sent:
            copy.wait()
        for i in range(STEPS - 1):
            total = total + self.last[i].astype(f32)
        return total

    @staticmethod
    def scratch(dims, order, slab):
        rest = without(without(dims, "x"), order[0])
        small = free_sizes(rest, half(order[1], 0))
        shapes = [
            (*lead(dims), *slab), (STEPS, 2, *small, *slab), (STEPS, 2, *lead(rest), *slab), (STEPS, 3, *slab),
            (STEPS - 1, *slab),
        ]
        return [pltpu.VMEM(s, bf16) for s in shapes]


BACK = (2, 1, -1, 0)


def backward_kernel(plan, *refs):
    n = len(plan)
    cells_in, dcells_in, project_in, taps_in, pre_in, deep_in, stats = refs[:7]
    parts = refs[7 : 7 + n - 3]
    refs = refs[4 + n :]
    stats_out, outs = refs[0], refs[1 : 1 + n]
    refs = refs[1 + n :]
    cells, dcells, project, taps, places, pre, deep, spread, mid, dpre, acc = refs[:11]
    refs = refs[11:]
    blocks_room, rest_room = refs[:15], refs[15 : 15 + 13 * (n - 3)]
    tile, tile_box, bsend, brecv, send, recv, local, kept, tsend, trecv = refs[15 + 13 * (n - 3) :]
    me = here()
    loads = []
    for i, (src, dst) in enumerate(((cells_in, cells), (dcells_in, dcells), (project_in, project), (taps_in, taps))):
        copy = pltpu.make_async_copy(src, dst, kept.at[i])
        copy.start()
        loads.append(copy)

    def fetch(step):
        at = me["x"][BACK[step]]
        pair = []
        for i, (src, dst) in enumerate(((pre_in, pre), (deep_in, deep))):
            copy = pltpu.make_async_copy(src.at[at], dst.at[step % 2], kept.at[4 + 2 * step + i])
            copy.start()
            pair.append(copy)
        return pair

    maps = [fetch(0), fetch(1), None, None]
    meet(announce(me, wide=True))
    rest = []
    for b, (dims, order) in enumerate(plan[3:]):
        own = rest_room[13 * b : 13 * b + 13]
        boxes = [own[1:5], own[5:9], own[9:13]]
        rest.append(Scatter(me, dims, order, parts[b], own[0], boxes, send.at[b], recv.at[b], local.at[b]))
    first = [
        Blocks(me, dims, order, blocks_room[5 * b], blocks_room[5 * b + 1 : 5 * b + 5], bsend.at[b], brecv.at[b])
        for b, (dims, order) in enumerate(plan[:3])
    ]
    for job in rest:
        job.begin()
    clear_borders(spread)
    places[...] = tap_places()
    loads[1].wait()
    loads[2].wait()
    square = jnp.zeros((8, 128), f32)

    def close_rest(square):
        for b, job in enumerate(rest):
            total = job.finish(2)
            outs[3 + b][...] = total
            square = square + folded(total * total)
        return square

    for step in range(STEPS):
        slot = step % 2
        at = me["x"][BACK[step]]
        for copy in maps[step]:
            copy.wait()
        back = project[at].reshape(WIDTH, D)

        def enter(i, _, back=back, slot=slot):
            rows = pl.ds(pl.multiple_of(i * SPAN, SPAN), SPAN)
            dmid = nt(dcells[rows, :], back) * PROJECT
            v = deep[slot, pl.ds(i * CHUNK * MAP, CHUNK * MAP)].reshape(SPAN, WIDTH)
            s = sigmoid(v)
            m = v * s
            mid[rows, :] = m.astype(bf16)
            spread[pl.ds(1 + i * CHUNK, CHUNK)] = (dmid * (s + m * (1.0 - s))).reshape(CHUNK, MAP, PAIR, WIDTH)
            return 0

        lax.fori_loop(0, MAP // CHUNK, enter, 0)
        if step > 0:
            for job in first:
                job.relay(step - 1)
        if step > 1:
            for job in first:
                job.finish(step - 2)
        if step == 1:
            for job in rest:
                job.relay(0)
        if step == 2:
            for job in rest:
                job.finish(0)
        if step == 3:
            for job in rest:
                job.finish(1)
        acc[...] = jnp.zeros_like(acc)
        if step == 0:
            loads[0].wait()
            loads[3].wait()

        def mix(row, subs, cols, slot=slot, at=at):
            near = spread[pl.ds(row, 3), :, subs, cols]
            tap = [jnp.broadcast_to(taps[at, t : t + 1, cols], (8, 128)) for t in range(9)]
            sums = [None] * 9
            for col in range(MAP):
                e = pre[slot, row * MAP + col, subs, cols]
                s = sigmoid(e)
                a = e * s
                total = None
                for t in range(9):
                    p = col + 1 - t % 3
                    if 0 <= p < MAP:
                        g = near[2 - t // 3, p]
                        term = g * tap[t]
                        total = term if total is None else total + term
                        term = g * a
                        sums[t] = term if sums[t] is None else sums[t] + term
                dpre[row * MAP + col, subs, cols] = total * (s + a * (1.0 - s))
            for t in range(9):
                acc[t, :, cols] += sums[t]

        each_block(mix)
        if step + 2 < STEPS:
            maps[step + 2] = fetch(step + 2)
        if step == 2:
            for job in rest:
                job.relay(1)
        if step > 0:
            for job in first:
                job.middle(step - 1)
        owned = (2, 4, 2, 24, D)
        low = dpre[...].reshape(PIX * PAIR, WIDTH).astype(bf16)
        first[0].full[at] = (tn(low, cells[...]) * EXPAND).astype(bf16).reshape(owned)
        first[1].full[at] = (tn(mid[...], dcells[...]) * PROJECT).astype(bf16).reshape(owned)
        for job in first[:2]:
            job.launch(step)
        dtaps = jnp.concatenate([jnp.sum(acc[...], axis=1) * (8.0 / 3.0), jnp.zeros((7, WIDTH), f32)], axis=0)
        side = nt(dtaps.astype(bf16), places[...]).astype(bf16)
        for i in range(OWNERS):
            first[2].full[at, i // 8, (i // 2) % 4, i % 2] = side[:, 128 * i : 128 * i + 128]
        first[2].launch(step)
    for job in first:
        job.finish(STEPS - 2)
    for job in first:
        job.relay(STEPS - 1)
    square = close_rest(square)
    for job in first:
        job.middle(STEPS - 1)
    for b, job in enumerate(first):
        total = job.close(job.finish(STEPS - 1))
        outs[b][...] = total
        square = square + folded(total * total)
    lines = [jnp.sum(v, 0, keepdims=True) for v in (stats[0:8], stats[8:16], square)]
    tile[0] = jnp.concatenate([*lines, jnp.zeros((5, 128), f32)], axis=0)
    number = 0
    for phase, (one, two) in enumerate((("c", "x"), ("y", "z"))):
        spans = [range(2 if a == "c" else RING) for a in (one, two)]
        moves = [{a: k for a, k in ((one, j), (two, k)) if k} for j in spans[0] for k in spans[1] if j or k]
        copies = []
        for move in moves:
            copy = pltpu.make_async_remote_copy(
                src_ref=tile.at[phase], dst_ref=tile_box.at[number], send_sem=tsend.at[number],
                recv_sem=trecv.at[number], device_id=moved(me, move), device_id_type=MESH_ID,
            )
            copy.start()
            copies.append(copy)
            number += 1
        for copy in copies:
            copy.wait()
        total = tile[phase]
        for i in range(number - len(copies), number):
            total = total + tile_box[i]
        tile[phase + 1] = total
    stats_out[...] = tile[2]


def backward(cells, dcells, project, taps, pre, deep, stats, parts, slabs, plan, collective_id):
    n = len(plan)
    shape = jax.ShapeDtypeStruct
    rows = PIX * PAIR
    room = []
    for (dims, order), slab in zip(plan[:3], slabs[:3]):
        room += Blocks.scratch(dims, order, slab)
    for (dims, order), slab in zip(plan[3:], slabs[3:]):
        room += Scatter.scratch(dims, order, slab, bf16)
    return pl.pallas_call(
        functools.partial(backward_kernel, plan),
        out_shape=[shape((8, 128), f32)] + [shape(s, f32) for s in slabs],
        in_specs=[ANY] * 6 + [INVMEM] + [ANY] * (n - 3),
        out_specs=[INVMEM] * (1 + n),
        scratch_shapes=[
            pltpu.VMEM((rows, D), bf16),
            pltpu.VMEM((rows, D), bf16),
            pltpu.VMEM(project.shape, bf16),
            pltpu.VMEM(taps.shape, f32),
            pltpu.VMEM((OWNERS * 128, WIDTH), bf16),
            pltpu.VMEM((2, *BLOCK), f32),
            pltpu.VMEM((2, *BLOCK), f32),
            pltpu.VMEM((MAP + 2, MAP, PAIR, WIDTH), f32),
            pltpu.VMEM((rows, WIDTH), bf16),
            pltpu.VMEM(BLOCK, f32),
            pltpu.VMEM((9, 8, WIDTH), f32),
            *room,
            pltpu.VMEM((3, 8, 128), f32),
            pltpu.VMEM((22, 8, 128), f32),
            pltpu.SemaphoreType.DMA((3, STEPS, 8)),
            pltpu.SemaphoreType.DMA((3, STEPS, 8)),
            pltpu.SemaphoreType.DMA((n - 3, 3, 4)),
            pltpu.SemaphoreType.DMA((n - 3, 3, 4)),
            pltpu.SemaphoreType.DMA((n - 3,)),
            pltpu.SemaphoreType.DMA((4 + 2 * STEPS,)),
            pltpu.SemaphoreType.DMA((22,)),
            pltpu.SemaphoreType.DMA((22,)),
        ],
        compiler_params=pltpu.CompilerParams(
            collective_id=collective_id, has_side_effects=True, vmem_limit_bytes=VMEM_BYTES
        ),
    )(cells, dcells, project, taps, pre, deep, stats, *parts)


IMAGES = 12
DP_MP = NAMES
DP = ("dp_0", "dp_1", "dp_2")
MP = ("mp_0", "mp_1")
CLIP_NORM = 0.02
BETA_ONE = 0.9
BETA_TWO = 0.999
ADAM_EPS = 1e-08
DECAY = 0.01
RATES = (0.1, 0.1, 0.2, 0.05, 0.05, 0.2)


def adam_kernel(count_ref, totals, gexpand, gproject, gtaps, gmisc, gone, gtwo, *refs):
    states = [refs[3 * i : 3 * i + 3] for i in range(6)]
    loss_ref, norm_ref = refs[18:20]
    outs = [refs[20 + 3 * i : 23 + 3 * i] for i in range(6)]

    def total(line):
        return jnp.sum(totals[line : line + 1, :], axis=(0, 1), keepdims=True)

    scored = 0.5 * total(1)
    norm = jnp.sqrt(total(2)) / scored
    factor = jnp.minimum(1.0, CLIP_NORM / norm) / scored
    loss_ref[0] = (0.5 * total(0) / scored)[0, 0]
    norm_ref[0] = norm[0, 0]
    steps = jnp.full((1, 1), count_ref[0], jnp.int32).astype(f32)
    z = steps * math.log(BETA_TWO)
    grown_two = -z * (1.0 + z / 2.0 * (1.0 + z / 3.0 * (1.0 + z / 4.0 * (1.0 + z / 5.0))))
    grown_one = 1.0 - jnp.exp(steps * math.log(BETA_ONE))

    def update(group, index, grad):
        master, first, second = (ref[index] for ref in states[group])
        grad = grad * factor
        first = BETA_ONE * first + (1.0 - BETA_ONE) * grad
        second = BETA_TWO * second + (1.0 - BETA_TWO) * grad * grad
        step = first / grown_one / (jnp.sqrt(second / grown_two) + ADAM_EPS) + DECAY * master
        outs[group][0][index] = master - RATES[group] * step
        outs[group][1][index] = first
        outs[group][2][index] = second

    every = slice(None)
    update(0, (every, slice(0, D)), gexpand[...])
    update(0, (every, slice(D, 2 * D)), gproject[...])
    taps = jnp.concatenate([gtaps[...], jnp.zeros((112, 128), f32)], axis=0).T
    update(0, (every, slice(2 * D, 2 * D + 9)), taps[0:24, 0:9])
    for i in range(3):
        update(1, (every, slice(D * i, D * i + D)), gmisc[4 * i : 4 * i + 4, :])
    update(1, (every, slice(3 * D, 2 * D + TABLE)), gmisc[12:16, 0:SMALL_AT])
    update(2, (every, every), gmisc[12:16, SMALL_AT : SMALL_AT + 11])
    for j in range(4):
        update(3, j, gone[:, 128 * j : 128 * j + 128])
    for j in range(2):
        update(4, j, gtwo[:, 512 * j : 512 * j + 512])
    for k in range(DIMS):
        update(5, k, gone[:, 512 + 64 * k : 576 + 64 * k])


def adam(step_count, totals, grads, states):
    smem = pl.BlockSpec(memory_space=pltpu.SMEM)
    one = jax.ShapeDtypeStruct((1,), f32)
    return pl.pallas_call(
        adam_kernel,
        out_shape=[one, one] + [jax.ShapeDtypeStruct(s.shape, f32) for s in states],
        in_specs=[smem] + [INVMEM] * (1 + len(grads) + len(states)),
        out_specs=[smem, smem] + [INVMEM] * len(states),
    )(step_count, totals, *grads, *states)


def per_device(
    frames, camera_ids, instruction_ids, action_bins, final_mask, step_count,
    conv_w, conv_m1, conv_m2, cond_w, cond_m1, cond_m2, small_w, small_m1, small_m2,
    attn_w, attn_m1, attn_m2, mlp_w, mlp_m1, mlp_m2, head_w, head_m1, head_m2,
):
    states = [
        *[v.T for v in (conv_w, conv_m1, conv_m2, cond_w, cond_m1, cond_m2, small_w, small_m1, small_m2)],
        *(attn_w, attn_m1, attn_m2, mlp_w, mlp_m1, mlp_m2),
        *[v.transpose(1, 0, 2) for v in (head_w, head_m1, head_m2)],
    ]
    cam2, cells, project, taps, misc_all, one_all, two_all, pre, deep, part = forward(
        frames, camera_ids, states[0::3], GATHER, 1
    )
    dcells, dmisc, done_one, done_two, stats = middle(
        instruction_ids,
        final_mask,
        part,
        cells,
        misc_all.reshape(2048, D),
        one_all.reshape(4, D, 1280),
        two_all.reshape(4, D, 1024),
        cam2,
        action_bins.T,
    )
    parts = [
        g.reshape(*lead(dims), *slab)
        for g, slab, (dims, _) in zip((dmisc, done_one, done_two), SLABS[3:], SCATTER[3:])
    ]
    totals, *grads = backward(cells, dcells, project, taps, pre, deep, stats, parts, SLABS, SCATTER, 2)
    loss, norm, *new = adam(step_count, totals, grads, states)
    new = [v.T for v in new[:9]] + new[9:15] + [v.transpose(1, 0, 2) for v in new[15:]]
    return loss.reshape(()), norm.reshape(()), *new


def solution(mesh):
    torus = Mesh(mesh.devices.reshape(2, 4, 4, 2, 2), NAMES)
    weights = (
        *[P(None, DP_MP)] * 9,
        *[P(None, DP, MP)] * 6,
        *[P(DP, None, MP)] * 3,
    )
    data = (P(DP_MP, None, None), P(DP_MP), P(DP), P(DP, None), P(DP), P())
    return jax.shard_map(
        per_device, mesh=torus, in_specs=(*data, *weights), out_specs=(P(), P(), *weights), check_vma=False
    )
```
